256 devices in a mesh: dp: 4 (over y), ctx: 64 (over x, z, core).
Axes of the slice: x: 4, y: 4, z: 8, core: 2. Of those that a mesh axis runs over, the one named last changes fastest.
Arguments:
- inputs: bfloat16 [4, 8192, 2048], P('dp', 'ctx'), may hold values from -6 to 6
- matrix_b: bfloat16 [4, 8192, 128], P('dp', 'ctx'), may hold values from -6 to 6
- matrix_c: bfloat16 [4, 8192, 128], P('dp', 'ctx'), may hold values from -0.119628906 to 0.119628906
- steps_dt: float32 [4, 8192, 32], P('dp', 'ctx'), may hold values from 0.5 to 2
- decay_rate: float32 [32], replicated, may hold values from 1.2207031e-05 to 0.04
- skip_gain: float32 [32], replicated, may hold values from 0.5 to 1.5
- level_weight: bfloat16 [2048, 576], replicated, may hold values from -0.125 to 0.125
- grad_out: bfloat16 [4, 8192, 2048], P('dp', 'ctx'), may hold values from -6 to 6
Outputs:
- output: bfloat16 [4, 8192, 2048], P('dp', 'ctx')
- grad_inputs: bfloat16 [4, 8192, 2048], P('dp', 'ctx')
- grad_b: bfloat16 [4, 8192, 128], P('dp', 'ctx')
- grad_c: bfloat16 [4, 8192, 128], P('dp', 'ctx')
- grad_dt: float32 [4, 8192, 32], P('dp', 'ctx')
- grad_rate: float32 [32], replicated
- grad_skip: float32 [32], replicated
- grad_level: float32 [2048, 576], P('ctx')
The draws below stay inside these ranges and needn't reach their ends.
All inputs are finite; a program needn't handle non-finite values.
Results may differ from the reference program's by a relative error of at most 0.011.
Values sent between devices are 32-bit elements; how exact they have to be, the bound alone decides.
No kernel may reach another device: no remote copies, remote signals or barrier semaphores. Data moves between devices by JAX's collectives and lax.ppermute only.
A program may use at most 192 MiB of HBM per device.

```python
import math
import jax
import jax.numpy as jnp
from jax import lax

H = 32
P_SIZE = 64
N = 128
LEVELS = 18
TOK_DEV = 128
INNER = 2048
BATCH = 4
SEQ = 8192
N_CTX = 64


def steps_of(stream_key, extent, shards, smallest, high):
    def one(dim, shards_of):
        steps = jax.random.uniform(jax.random.fold_in(jax.random.fold_in(stream_key, 6), dim), (shards_of,), jnp.float32, smallest / len(shards), high / len(shards))
        return jnp.repeat(jnp.exp(steps), extent[dim] // shards_of).reshape((-1,) + (1,) * (len(extent) - dim - 1))

    level = one(*shards[0])
    for cut in shards[1:]:
        level = level * one(*cut)
    return level


def centred(own_key, dims, spread, limit, split=(), held_as=jnp.bfloat16):
    values = spread * jax.random.normal(own_key, dims, jnp.float32)
    if split:
        values = values * steps_of(own_key, dims, split, -0.22, 0.18)
    return jnp.clip(values, -limit, limit).astype(held_as)


def setup_inputs(seed: int = 0) -> dict:
    splits = jax.random.split(jax.random.key(seed), 9)
    return {
        "inputs": centred(splits[0], (BATCH, SEQ, INNER), 1.0, 6.0, ((0, 4), (1, 64))),
        "matrix_b": centred(splits[1], (BATCH, SEQ, N), 1.0, 6.0, ((0, 4), (1, 64))),
        "matrix_c": centred(splits[2], (BATCH, SEQ, N), 0.02, 0.119628906, ((0, 4), (1, 64))),
        "steps_dt": jnp.clip(jnp.exp(math.log(2.0) - 1.3862944 * jax.random.uniform(splits[3], (BATCH, SEQ, H), jnp.float32) ** steps_of(splits[3], (BATCH, SEQ, H), ((0, 4), (1, 64)), -0.2, 0.2)), 0.5, 2.0),
        "decay_rate": jnp.clip(jnp.exp(jax.random.uniform(splits[4], (H,), jnp.float32, math.log(1.220703143189894e-05), math.log(0.04))), 1.220703143189894e-05, 0.04),
        "skip_gain": jnp.clip(1.0 + 0.1 * jax.random.normal(splits[5], (H,), jnp.float32), 0.5, 1.5),
        "level_weight": centred(splits[6], (INNER, LEVELS * H), INNER ** -0.5, 0.125),
        "grad_out": centred(splits[7], (BATCH, SEQ, INNER), 1.0, 6.0, ((0, 4), (1, 64))),
    }


HIGHEST = lax.Precision.HIGHEST

def level_table(length):
    places = jnp.arange(length, dtype=jnp.int32)
    distance = jnp.bitwise_xor(places[:, None], places[None, :])
    levels = jnp.zeros((length, length), jnp.int32)
    for bit_place in range(length.bit_length()):
        levels = levels + (distance >= 1 << bit_place).astype(jnp.int32)
    return levels

def block_state(inputs_x, inputs_b, steps_local, rates):
    decay_log = jnp.cumsum(steps_local * rates[None, :], axis=0)
    block_total = decay_log[-1]
    carried = jnp.exp(decay_log - block_total[None, :]) * steps_local
    states = jnp.einsum('sh,sn,shp->hnp', carried, inputs_b, inputs_x, precision=HIGHEST)
    return (states, block_total)

def block_output(inputs_x, inputs_b, inputs_c, steps_local, rates, skips, weights_f, carried_levels):
    length, head_count, head_size = inputs_x.shape
    flat_half = inputs_x.reshape(length, head_count * head_size).astype(jnp.bfloat16)
    level_logit = jnp.dot(flat_half, weights_f.astype(jnp.bfloat16), preferred_element_type=jnp.float32)
    mixing = jax.nn.softplus(level_logit).reshape(length, -1, head_count)
    decay_log = jnp.cumsum(steps_local * rates[None, :], axis=0)
    places = jnp.arange(length, dtype=jnp.int32)
    causal = (places[:, None] >= places[None, :]).astype(jnp.float32)
    gap_log = jnp.where(causal[:, :, None] > 0.5, decay_log[:, None, :] - decay_log[None, :, :], 0.0)
    fading = jnp.exp(-gap_log) * causal[:, :, None]
    onehot = (level_table(length)[:, :, None] == jnp.arange(mixing.shape[1], dtype=jnp.int32)[None, None, :]).astype(jnp.float32)
    chosen = jnp.einsum('tlh,tsl->tsh', mixing, onehot, precision=HIGHEST)
    scores = jnp.dot(inputs_c.astype(jnp.bfloat16), inputs_b.astype(jnp.bfloat16).T, preferred_element_type=jnp.float32)
    pair_weight = chosen * fading * scores[:, :, None]
    scaled = steps_local[:, :, None] * inputs_x
    inner_part = jnp.einsum('tsh,shp->thp', pair_weight, scaled, precision=HIGHEST)
    first_level = length.bit_length()
    span_count = carried_levels.shape[0]
    remote = mixing[:, first_level:first_level + span_count, :] * jnp.exp(-decay_log)[:, None, :]
    outer_part = jnp.einsum('tmh,tn,mhnp->thp', remote, inputs_c, carried_levels, precision=HIGHEST)
    return inner_part + outer_part + skips[None, :, None] * inputs_x

def sequence_forward(inputs_x, inputs_b, inputs_c, steps_local, rates, skips, weights_f):
    blocks = N_CTX
    block_x = inputs_x.reshape(blocks, TOK_DEV, H, P_SIZE)
    block_b = inputs_b.reshape(blocks, TOK_DEV, N)
    block_c = inputs_c.reshape(blocks, TOK_DEV, N)
    block_dt = steps_local.reshape(blocks, TOK_DEV, H)
    states, totals = jax.vmap(block_state, in_axes=(0, 0, 0, None))(block_x, block_b, block_dt, rates)
    ends = jnp.cumsum(totals, axis=0)
    starts = ends - totals
    block_index = jnp.arange(blocks, dtype=jnp.int32)
    earlier = (block_index[:, None] > block_index[None, :]).astype(jnp.float32)
    gap_log = jnp.where(earlier[:, :, None] > 0.5, starts[:, None, :] - ends[None, :, :], 0.0)
    fading = jnp.exp(-gap_log) * earlier[:, :, None]
    block_levels = level_table(blocks) - 1
    collected = []
    for span_index in range(blocks.bit_length() - 1):
        picked = (block_levels == span_index).astype(jnp.float32) * earlier
        collected.append(jnp.einsum('jih,ihnp->jhnp', fading * picked[:, :, None], states, precision=HIGHEST))
    carried = jnp.stack(collected, axis=1)

    def one_block(packed):
        part_x, part_b, part_c, part_dt, part_levels = packed
        return block_output(part_x, part_b, part_c, part_dt, rates, skips, weights_f, part_levels)
    outputs = lax.map(one_block, (block_x, block_b, block_c, block_dt, carried))
    return outputs.reshape(blocks * TOK_DEV, H * P_SIZE)

def reference(inputs, matrix_b, matrix_c, steps_dt, decay_rate, skip_gain, level_weight, grad_out):
    weights_f = level_weight.astype(jnp.float32)

    def one_sequence(packed):
        seq_x, seq_b, seq_c, seq_dt, seq_grad = packed
        result, pullback = jax.vjp(sequence_forward, seq_x.astype(jnp.float32), seq_b.astype(jnp.float32), seq_c.astype(jnp.float32), seq_dt, decay_rate, skip_gain, weights_f)
        grads = pullback(seq_grad.astype(jnp.float32))
        return (result,) + tuple(grads)
    results = lax.map(one_sequence, (inputs, matrix_b, matrix_c, steps_dt, grad_out))
    output = results[0].astype(jnp.bfloat16)
    grad_inputs = results[1].astype(jnp.bfloat16)
    grad_b = results[2].astype(jnp.bfloat16)
    grad_c = results[3].astype(jnp.bfloat16)
    grad_dt = results[4]
    grad_rate = lax.optimization_barrier(jnp.sum(results[5], axis=0))
    grad_skip = lax.optimization_barrier(jnp.sum(results[6], axis=0))
    grad_level = lax.optimization_barrier(jnp.sum(results[7], axis=0))
    return (output, grad_inputs, grad_b, grad_c, grad_dt, grad_rate, grad_skip, grad_level)
```

```python
import jax
import jax.numpy as jnp
import numpy as np
from jax import lax
from jax.experimental import pallas as pl
from jax.experimental.pallas import tpu as pltpu
from jax.sharding import PartitionSpec as P

F32 = jnp.float32
BF16 = jnp.bfloat16
HIGHEST = lax.Precision.HIGHEST
HEADS = 32
SIZE = 64
TOK = 128
NST = 128
FEAT = HEADS * SIZE
INTRA = 8
SPANS = 6
USED = INTRA + SPANS
CHUNK = 256
CHUNKS = FEAT // CHUNK
PAIRS = FEAT // 128
BLOCKS = 64
ROWS = FEAT // BLOCKS


def mm(a, b):
    return lax.dot_general(a, b, (((1,), (0,)), ((), ())), preferred_element_type=F32)


def mm_nt(a, b):
    return lax.dot_general(a, b, (((1,), (1,)), ((), ())), preferred_element_type=F32)


def mm_tn(a, b):
    return lax.dot_general(a, b, (((0,), (0,)), ((), ())), preferred_element_type=F32)


def onehot(chunk, quarter, rows=128):
    row = lax.broadcasted_iota(jnp.int32, (rows, CHUNK), 0)
    lane = lax.broadcasted_iota(jnp.int32, (rows, CHUNK), 1)
    if rows > 128:
        row = jnp.where(row >= 128, row - 128, row)
    head = chunk * (CHUNK // SIZE) + jnp.right_shift(lane, 6) + 32 * quarter
    return jnp.where(row == head, 1.0, 0.0).astype(BF16)


def split2(a):
    hi = a.astype(BF16)
    lo = (a - hi.astype(F32)).astype(BF16)
    return jnp.concatenate([hi, lo], axis=1)


def four(a):
    return jnp.concatenate([a, a, a, a], axis=1)


def sums_down():
    row = lax.broadcasted_iota(jnp.int32, (TOK, TOK), 0)
    col = lax.broadcasted_iota(jnp.int32, (TOK, TOK), 1)
    return jnp.where(row >= col, 1.0, 0.0).astype(F32)


def at_chunk(chunk):
    return pl.ds(pl.multiple_of(chunk * CHUNK, CHUNK), CHUNK)


def start_kernel(
    x_ref, g_ref, b_ref, c_ref, dt_ref, rate_ref, w_ref,
    u_ref, d_ref, lam_ref, sig_ref, cum_ref,
):
    dt4 = four(dt_ref[...])
    rate4 = four(rate_ref[...])
    cum = lax.dot_general(
        sums_down(), dt4 * rate4, (((1,), (0,)), ((), ())),
        precision=HIGHEST, preferred_element_type=F32,
    )
    cum_ref[...] = cum
    logit = mm(x_ref[...], w_ref[:, :512])
    soft = jnp.maximum(logit, 0.0) + jnp.log1p(jnp.exp(-jnp.abs(logit)))
    lam_ref[...] = soft
    sig_ref[...] = 1.0 / (1.0 + jnp.exp(-logit))
    fade = jnp.exp(-cum)
    far = jnp.concatenate([split2(soft[:, 256:384] * fade), split2(soft[:, 384:512] * fade)], axis=0)
    held = split2(jnp.exp(cum - cum[TOK - 1 : TOK]) * dt4)
    bmat = b_ref[...]
    cmat = c_ref[...]

    @pl.loop(0, CHUNKS)
    def _(chunk):
        cols = at_chunk(chunk)
        xs = x_ref[:, cols].astype(F32)
        gs = g_ref[:, cols].astype(F32)
        parts = [None] * SPANS
        for quarter in range(4):
            spread = onehot(chunk, quarter, 256)
            if quarter == 0:
                scaled = (xs * mm(held, spread)).astype(BF16)
            wide = mm(far if quarter < 2 else far[:TOK], spread)
            parts[quarter] = (wide[:TOK] * gs).astype(BF16)
            if quarter < 2:
                parts[4 + quarter] = (wide[TOK:] * gs).astype(BF16)
        state = mm_tn(bmat, scaled)
        cots = mm_tn(cmat, jnp.concatenate(parts, axis=1))
        for half in range(2):
            u_ref[2 * chunk + half] = state[:, 128 * half : 128 * half + 128]
            for span in range(SPANS):
                at = CHUNK * span + 128 * half
                d_ref[span, 2 * chunk + half] = cots[:, at : at + 128]


def near_kernel(
    x_ref, g_ref, b_ref, c_ref, dt_ref, skip_ref, lam_ref, sig_ref, cum_ref,
    y_ref, dx_ref, db_ref, dc_ref, dl_ref, gw_ref, q_ref, w_ref, sk_ref,
    kst_ref, dk_ref, da_ref,
):
    bmat = b_ref[...]
    cmat = c_ref[...]
    cum = cum_ref[...]
    fade = jnp.exp(-cum)
    score = mm_nt(cmat, bmat)
    row = lax.broadcasted_iota(jnp.int32, (TOK, TOK), 0)
    col = lax.broadcasted_iota(jnp.int32, (TOK, TOK), 1)
    apart = jnp.bitwise_xor(row, col)

    def mask_of(level):
        if level == 0:
            return row == col
        return (row > col) & (jnp.right_shift(apart, level - 1) == 1)

    for level in range(INTRA):
        kst_ref[level * TOK : (level + 1) * TOK] = jnp.where(mask_of(level), score, 0.0).astype(BF16)
    near = jnp.concatenate(
        [split2(lam_ref[:, :128] * fade), split2(lam_ref[:, 128:256] * fade)], axis=0
    )
    lift = split2(jnp.exp(cum) * four(dt_ref[...]))
    gain = split2(jnp.broadcast_to(four(skip_ref[...]), (8, 128)))
    dk_ref[...] = jnp.zeros_like(dk_ref)
    da_ref[...] = jnp.zeros_like(da_ref)
    q_ref[...] = jnp.zeros_like(q_ref)
    sk_ref[...] = jnp.zeros_like(sk_ref)

    @pl.loop(0, CHUNKS)
    def _(chunk):
        cols = at_chunk(chunk)
        xs = x_ref[:, cols].astype(F32)
        gs = g_ref[:, cols].astype(F32)
        spread0 = onehot(chunk, 0, 256)
        lifted = mm(lift, spread0)
        gains = mm(gain, spread0)[0:1]
        xd = (xs * lifted).astype(BF16)
        kst = kst_ref[...]
        mixed = mm(kst, xd)
        out = gains * xs
        parts = [None] * INTRA
        for quarter in range(4):
            wide = mm(near, onehot(chunk, quarter, 256))
            prods = []
            for part in range(2):
                level = 4 * part + quarter
                mult = wide[TOK * part : TOK * part + TOK]
                value = mixed[level * TOK : (level + 1) * TOK]
                out = out + mult * value
                prods.append((gs * value).astype(BF16))
                parts[level] = (mult * gs).astype(BF16)
            da_ref[...] += mm_nt(jnp.concatenate(prods, axis=0), onehot(chunk, quarter))
        y_ref[:, cols] = out
        agst = jnp.concatenate(parts, axis=0)
        dxd = mm_tn(kst, agst)
        dk_ref[...] += mm_nt(agst, xd)
        ones = onehot(chunk, 0)
        q_ref[...] += mm_nt((dxd * xs).astype(BF16), ones)
        dx_ref[:, cols] = dxd * lifted + gains * gs
        skrow = jnp.sum(xs * gs, axis=0, keepdims=True)
        sk_ref[...] += lax.dot_general(
            jnp.broadcast_to(skrow, (8, CHUNK)), ones.astype(F32), (((1,), (1,)), ((), ())),
            precision=HIGHEST, preferred_element_type=F32,
        )

    dscore = jnp.zeros((TOK, TOK), F32)
    for level in range(INTRA):
        dscore = dscore + jnp.where(mask_of(level), dk_ref[level * TOK : (level + 1) * TOK], 0.0)
    dscore = dscore.astype(BF16)
    dc_ref[...] = mm(dscore, bmat)
    db_ref[...] = mm_tn(dscore, cmat)
    dlam = []
    for part in range(2):
        da = da_ref[TOK * part : TOK * part + TOK]
        dlam.append(da * fade)
    w_ref[...] = dlam[0] * lam_ref[:, :128] + dlam[1] * lam_ref[:, 128:256]
    dlogit = (jnp.concatenate(dlam, axis=1) * sig_ref[:, :256]).astype(BF16)
    dl_ref[...] = dlogit
    for part in range(FEAT // 128):
        rows = mm_tn(x_ref[:, 128 * part : 128 * part + 128], dlogit)
        for block in range(128 // ROWS):
            at = part * (128 // ROWS) + block
            gw_ref[at % 2, at // 2] = rows[ROWS * block : ROWS * block + ROWS]


def far_kernel(
    core_ref, x_ref, g_ref, c_ref, lam_ref, sig_ref, fade_ref, y_ref, dc_ref,
    first_ref, m1_ref, m2_ref, m3_ref, m4_ref, m5_ref, o1_ref, o2_ref, o3_ref, o4_ref, o5_ref,
    out_ref, dcout_ref, dl_ref, gw_ref, w_ref,
    da_ref, dcs_ref,
):
    cmat = c_ref[...]
    far = jnp.concatenate(
        [split2(lam_ref[:, 256:384] * fade_ref[0]), split2(lam_ref[:, 384:512] * fade_ref[1])], axis=0
    )
    da_ref[...] = jnp.zeros_like(da_ref)
    dcs_ref[...] = dc_ref[...]
    core = core_ref[0]

    def step(local, chunk, sources):
        cols = at_chunk(chunk)
        gs = g_ref[:, cols].astype(F32)
        carried = jnp.concatenate(
            [first_ref[2 * chunk + half].astype(BF16) for half in range(2)]
            + [ref[2 * local + half].astype(BF16) for ref in sources for half in range(2)],
            axis=1,
        )
        mixed = mm(cmat, carried)
        out = y_ref[:, cols]
        parts = [None] * SPANS
        for quarter in range(4):
            count = 2 if quarter < 2 else 1
            wide = mm(far[: TOK * count], onehot(chunk, quarter, 256))
            prods = []
            for part in range(count):
                span = 4 * part + quarter
                mult = wide[TOK * part : TOK * part + TOK]
                value = mixed[:, CHUNK * span : CHUNK * span + CHUNK]
                out = out + mult * value
                prods.append((gs * value).astype(BF16))
                parts[span] = (mult * gs).astype(BF16)
            da_ref[: TOK * count] += mm_nt(jnp.concatenate(prods, axis=0), onehot(chunk, quarter))
        out_ref[:, cols] = out.astype(BF16)
        dcs_ref[...] += mm_nt(jnp.concatenate(parts, axis=1), carried)

    @pl.loop(0, CHUNKS // 2)
    def _(local):
        step(local, local + core * (CHUNKS // 2), (m1_ref, m2_ref, m3_ref, m4_ref, m5_ref))

    @pl.loop(0, CHUNKS // 2)
    def _(local):
        step(local, local + (1 - core) * (CHUNKS // 2), (o1_ref, o2_ref, o3_ref, o4_ref, o5_ref))

    dcout_ref[...] = dcs_ref[...].astype(BF16)
    dlam = [da_ref[TOK * part : TOK * part + TOK] * fade_ref[part] for part in range(2)]
    w_ref[0] = dlam[0] * lam_ref[:, 256:384]
    w_ref[1] = dlam[1] * lam_ref[:, 384:512]
    dlogit = (jnp.concatenate(dlam, axis=1) * sig_ref[:, 256:512]).astype(BF16)
    dl_ref[...] = dlogit
    lane = lax.broadcasted_iota(jnp.int32, (ROWS // 2, 128), 1)
    for part in range(FEAT // 128):
        rows = mm_tn(x_ref[:, 128 * part : 128 * part + 128], dlogit)
        turned = pltpu.roll(rows[:, 128:], 64, 1)
        for block in range(128 // ROWS):
            at = part * (128 // ROWS) + block
            top = ROWS * block
            mid = top + ROWS // 2
            gw_ref[at % 2, at // 2, :ROWS] = rows[top : top + ROWS, :128]
            gw_ref[at % 2, at // 2, ROWS:] = jnp.where(
                lane < 64, rows[top:mid, 128:], turned[mid : mid + ROWS // 2]
            )


def last_kernel(
    core_ref, x_ref, b_ref, dt_ref, cum_ref, rate_ref, w_ref, mine_ref, other_ref, cot_ref, lag_ref, dx_ref, db_ref,
    dl0_ref, dl1_ref, q_ref, w0_ref, w1_ref,
    dxout_ref, dbout_ref, ddt_ref, rate_out_ref,
    dbs_ref, q2_ref,
):
    bmat = b_ref[...]
    cum = cum_ref[...]
    dt4 = four(dt_ref[...])
    left = jnp.exp(cum - cum[TOK - 1 : TOK])
    held = split2(left * dt4)
    dlogit = jnp.concatenate([dl0_ref[...], dl1_ref[...]], axis=1)
    q2_ref[...] = jnp.zeros_like(q2_ref)
    dbs_ref[...] = db_ref[...]

    core = core_ref[0]

    def step(local, chunk, source):
        cols = at_chunk(chunk)
        xs = x_ref[:, cols].astype(F32)
        spread = mm(held, onehot(chunk, 0, 256))
        du = jnp.concatenate(
            [
                (source[2 * local + half] * lag_ref[2 * chunk + half] + cot_ref[2 * chunk + half]).astype(BF16)
                for half in range(2)
            ],
            axis=1,
        )
        dxs = mm(bmat, du)
        q2_ref[...] += mm_nt((dxs * xs).astype(BF16), onehot(chunk, 0))
        dbs_ref[...] += mm_nt((xs * spread).astype(BF16), du)
        rows = w_ref[at_chunk(chunk), :512]
        dx = dx_ref[:, cols] + dxs * spread + mm_nt(dlogit, rows)
        dxout_ref[:, cols] = dx.astype(BF16)

    @pl.loop(0, CHUNKS // 2)
    def _(local):
        step(local, local + core * (CHUNKS // 2), mine_ref)

    @pl.loop(0, CHUNKS // 2)
    def _(local):
        step(local, local + (1 - core) * (CHUNKS // 2), other_ref)

    dbout_ref[...] = dbs_ref[...].astype(BF16)
    q2 = q2_ref[...]
    q1 = q_ref[...]
    lift = jnp.exp(cum)
    gathered = w0_ref[...] + w1_ref[0] + w1_ref[1]
    queried = gathered + pltpu.roll(gathered, 32, 1)
    queried = queried + pltpu.roll(queried, 64, 1)
    keyed2 = q2 * left * dt4
    dcum = q1 * lift * dt4 + keyed2 - queried
    dlog = lax.dot_general(
        sums_down(), dcum, (((0,), (0,)), ((), ())), precision=HIGHEST, preferred_element_type=F32
    )
    dlog = dlog - jnp.sum(keyed2, axis=0, keepdims=True)
    ddt_ref[...] = rate_ref[...] * dlog[:, :32] + (q1 * lift + q2 * left)[:, :32]
    rate_out_ref[...] = jnp.sum(dt4 * dlog, axis=0, keepdims=True)


def call(kernel, outs, scratch=(), flops=0, moved=0):
    return pl.pallas_call(
        kernel,
        out_shape=outs,
        scratch_shapes=list(scratch),
        compiler_params=pltpu.CompilerParams(vmem_limit_bytes=56 * 1024 * 1024),
        cost_estimate=pl.CostEstimate(flops=flops, bytes_accessed=moved, transcendentals=0),
    )


def shaped(*dims, dtype=F32):
    return jax.ShapeDtypeStruct(dims, dtype)


def swap(value, bit, only=None):
    mask = 1 << bit
    pairs = []
    for source in range(1 << SPANS):
        if only is None or (source >> bit) % 2 != only:
            pairs.append((source, source ^ mask))
    return lax.ppermute(value, "ctx", pairs)


def turn(value, bit):
    mask = 1 << bit
    return lax.ppermute(value, "dp", [(source, source ^ mask) for source in range(lax.axis_size("dp"))])


def collect(value, bits):
    for span in range(SPANS):
        other = swap(value, span)
        value = jnp.where(
            bits[span] == 1,
            jnp.concatenate([other, value], axis=0),
            jnp.concatenate([value, other], axis=0),
        )
    return value


def fold(value, bits):
    for span in (0, 5, 4, 3, 2, 1):
        if span > 0:
            value = value.reshape((2, value.shape[0] // 2) + value.shape[1:])
        away = lax.dynamic_index_in_dim(value, 1 - bits[span], 0, keepdims=False)
        keep = lax.dynamic_index_in_dim(value, bits[span], 0, keepdims=False)
        value = keep + swap(away, span)
    value = value[0]
    for step in range(2):
        value = value + turn(value, step)
    return value


def row_of(per_head):
    pairs = per_head.reshape(per_head.shape[:-1] + (per_head.shape[-1] // 2, 1, 2))
    return jnp.repeat(pairs, SIZE, axis=-1)


def per_head(value):
    rows = jnp.sum(value, axis=1)
    return jnp.sum(rows.reshape(-1, 2, SIZE), axis=-1).reshape(-1)


def group_masks(blocks):
    place = np.arange(blocks)
    upper = np.zeros((SPANS, blocks, blocks), np.float32)
    before = np.zeros((SPANS, blocks, blocks), np.float32)
    after = np.zeros((SPANS, blocks, blocks), np.float32)
    parent = np.zeros((SPANS, blocks, blocks), np.float32)
    for span in range(SPANS):
        bit = (place >> span) % 2
        same_parent = (place[:, None] >> (span + 1)) == (place[None, :] >> (span + 1))
        same_group = (place[:, None] >> span) == (place[None, :] >> span)
        upper[span] = same_parent & (bit[None, :] == 1)
        before[span] = same_group & (place[None, :] < place[:, None])
        after[span] = same_group & (place[None, :] > place[:, None]) & (bit[:, None] == 1)
        parent[span] = same_parent & (bit[:, None] == 1)
    return upper, before, after, parent


def per_device(inputs, matrix_b, matrix_c, steps_dt, decay_rate, skip_gain, level_weight, grad_out):
    xs, bs, cs, dts, gs = inputs[0], matrix_b[0], matrix_c[0], steps_dt[0], grad_out[0]
    blocks = lax.axis_size("ctx")
    place = lax.axis_index("ctx")
    core = place % 2
    bits = [jnp.right_shift(place, span) % 2 for span in range(SPANS)]
    rate = decay_rate.reshape(1, HEADS)
    upper, before, after, parent = group_masks(blocks)

    dt_sum = jnp.sum(dts, axis=0)
    totals = collect((dt_sum * decay_rate)[None], bits)
    here = jnp.stack([upper, before], axis=0)[:, :, place]
    sums = jnp.sum(here[..., None] * totals[None, None], axis=2)
    fade_up = jnp.exp(-sums[0])
    on = jnp.stack(bits).astype(F32)[:, None]
    fade_in = jnp.exp(-sums[1]) * on

    states, cots, lam, sig, cum = call(
        start_kernel,
        (
            shaped(PAIRS, NST, 128),
            shaped(SPANS, PAIRS, NST, 128),
            shaped(TOK, 512),
            shaped(TOK, 512),
            shaped(TOK, 128),
        ),
        flops=2 * TOK * FEAT * (512 + 7 * NST),
        moved=12 << 20,
    )(xs, gs, bs, cs, dts, rate, level_weight)

    half_up = lax.dynamic_slice_in_dim(fade_up.reshape(SPANS, 2, HEADS // 2), core, 1, 1)[:, 0]
    row_up = row_of(half_up)

    first = swap(states, 0)

    def mine_of(value):
        return lax.dynamic_slice_in_dim(value, core * (PAIRS // 2), PAIRS // 2, 0)

    def yours_of(value):
        return lax.dynamic_slice_in_dim(value, (1 - core) * (PAIRS // 2), PAIRS // 2, 0)

    mine, yours = mine_of(states), mine_of(first)
    lower = jnp.where(bits[0] == 1, yours, mine)
    lowers = [lower]
    held = lower * row_up[0] + jnp.where(bits[0] == 1, mine, yours)
    carried = []
    for span in range(1, SPANS):
        other = swap(held, span, 1 if span == SPANS - 1 else None)
        carried.append(other)
        if span < SPANS - 1:
            lower = jnp.where(bits[span] == 1, other, held)
            upper_part = jnp.where(bits[span] == 1, held, other)
            lowers.append(lower)
            held = lower * row_up[span] + upper_part
        else:
            lowers.append(other)
    across = [swap(value, 0) for value in carried]

    near = call(
        near_kernel,
        (
            shaped(TOK, FEAT),
            shaped(TOK, FEAT),
            shaped(TOK, NST),
            shaped(TOK, NST),
            shaped(TOK, 256, dtype=BF16),
            shaped(2, BLOCKS // 2, ROWS, 256),
            shaped(TOK, 128),
            shaped(TOK, 128),
            shaped(8, 128),
        ),
        scratch=(
            pltpu.VMEM((INTRA * TOK, TOK), BF16),
            pltpu.VMEM((INTRA * TOK, TOK), F32),
            pltpu.VMEM((2 * TOK, 128), F32),
        ),
        flops=2 * TOK * FEAT * (5 * INTRA * NST),
        moved=12 << 20,
    )
    y_near, dx_near, db_near, dc_near, dl_near, gw_near, q_near, w_near, skip_sum = near(
        xs, gs, bs, cs, dts, skip_gain.reshape(1, HEADS), lam, sig, cum
    )

    in_row = row_of(fade_in)
    cot0 = swap(cots[0] * in_row[0], 0, 0)
    sent = [swap(yours_of(cots[span]) * yours_of(in_row[span]), 0) for span in range(1, SPANS)]
    level = [mine_of(cots[span]) * mine_of(in_row[span]) + sent[span - 1] for span in range(1, SPANS)]
    grad = None
    crossed = [None] * SPANS
    for span in reversed(range(1, SPANS)):
        if grad is None:
            back = swap(level[span - 1], span, 0)
            grad = back
            crossed[span] = jnp.zeros((HEADS // 2,), F32)
        else:
            crossed[span] = per_head(lowers[span] * row_up[span] * grad)
            back = swap(
                jnp.where(bits[span] == 1, grad * row_up[span] + level[span - 1], grad), span
            )
            grad = jnp.where(bits[span] == 1, grad, grad * row_up[span]) + back
    crossed[0] = per_head(lowers[0] * row_up[0] * grad)
    grad_other = swap(grad, 0)
    lag = jnp.where(bits[0] == 1, jnp.ones_like(fade_up[0]), fade_up[0])

    fade_t = jnp.exp(-cum)
    fade_far = fade_t[None] * jnp.concatenate([fade_in, jnp.zeros((2, HEADS), F32)]).reshape(2, 1, 128)
    where_am_i = core.astype(jnp.int32).reshape(1)
    far = pl.pallas_call(
        far_kernel,
        out_shape=(
            shaped(TOK, FEAT, dtype=BF16),
            shaped(TOK, NST, dtype=BF16),
            shaped(TOK, 256, dtype=BF16),
            shaped(2, BLOCKS // 2, ROWS + ROWS // 2, 128),
            shaped(2, TOK, 128),
        ),
        in_specs=[pl.BlockSpec(memory_space=pltpu.SMEM)] + [pl.BlockSpec(memory_space=pltpu.VMEM)] * 19,
        scratch_shapes=[pltpu.VMEM((2 * TOK, 128), F32), pltpu.VMEM((TOK, NST), F32)],
        compiler_params=pltpu.CompilerParams(vmem_limit_bytes=56 * 1024 * 1024),
        cost_estimate=pl.CostEstimate(flops=2 * TOK * FEAT * 24 * NST, bytes_accessed=14 << 20, transcendentals=0),
    )
    output, grad_c, dl_far, gw_far, w_far = far(
        where_am_i, xs, gs, cs, lam, sig, fade_far, y_near, dc_near, first, *carried, *across
    )

    near_rows = fold(gw_near, bits)
    far_rows = fold(gw_far, bits)
    packed = far_rows[ROWS:]
    tail = jnp.concatenate([packed[:, :64], packed[:, 64:]], axis=0)
    blank = jnp.zeros((ROWS, level_weight.shape[1] - 448), F32)
    grad_level = jnp.concatenate([near_rows, far_rows[:ROWS], tail, blank], axis=1)

    last = pl.pallas_call(
        last_kernel,
        out_shape=(
            shaped(TOK, FEAT, dtype=BF16),
            shaped(TOK, NST, dtype=BF16),
            shaped(TOK, HEADS),
            shaped(1, 128),
        ),
        in_specs=[pl.BlockSpec(memory_space=pltpu.SMEM)] + [pl.BlockSpec(memory_space=pltpu.VMEM)] * 17,
        scratch_shapes=[pltpu.VMEM((TOK, NST), F32), pltpu.VMEM((TOK, 128), F32)],
        compiler_params=pltpu.CompilerParams(vmem_limit_bytes=56 * 1024 * 1024),
        cost_estimate=pl.CostEstimate(flops=2 * TOK * FEAT * 7 * NST, bytes_accessed=14 << 20, transcendentals=0),
    )
    grad_inputs, grad_b, ddt, rate_row = last(
        where_am_i, xs, bs, dts, cum, rate, level_weight, grad, grad_other, cot0, row_of(lag),
        dx_near, db_near, dl_near, dl_far, q_near, w_near, w_far,
    )

    queried = jnp.sum(w_far, axis=1).reshape(8, HEADS)[:SPANS]
    halves = jnp.stack(crossed)
    spread = jnp.zeros((SPANS, 2, HEADS // 2), F32)
    spread = lax.dynamic_update_slice_in_dim(spread, halves[:, None], core, 1).reshape(SPANS, HEADS)
    note = jnp.concatenate(
        [queried, spread, rate_row[:, :HEADS], skip_sum[:1, :HEADS], dt_sum[None], jnp.zeros((1, HEADS), F32)]
    )
    notes = collect(note.reshape(1, 4, 128), bits).reshape(blocks, 16, HEADS)
    masks = jnp.asarray(np.concatenate([after, parent]))
    between = jnp.einsum("mid,dmh->ih", masks, notes[:, : 2 * SPANS], precision=HIGHEST)
    ends = jnp.stack([jnp.sum(notes[:, 12] - between * notes[:, 14], axis=0), jnp.sum(notes[:, 13], axis=0)])
    for step in range(2):
        ends = ends + turn(ends, step)
    grad_rate, grad_skip = ends[0], ends[1]
    own = lax.dynamic_slice_in_dim(between, place, 1, 0)
    grad_dt = (ddt - rate * own)[None]
    return (output[None], grad_inputs[None], grad_b[None], grad_c[None], grad_dt, grad_rate, grad_skip, grad_level)


def solution(mesh):
    split = P("dp", "ctx", None)
    return jax.shard_map(
        per_device,
        mesh=mesh,
        in_specs=(split, split, split, split, P(), P(), P(), split),
        out_specs=(split, split, split, split, split, P(), P(), P("ctx", None)),
        check_vma=False,
    )
```

```python
import jax
import jax.numpy as jnp
import numpy as np
from jax import lax
from jax.experimental import pallas as pl
from jax.experimental.pallas import tpu as pltpu
from jax.sharding import PartitionSpec as P

F32 = jnp.float32
BF16 = jnp.bfloat16
HIGHEST = lax.Precision.HIGHEST
HEADS = 32
SIZE = 64
TOK = 128
NST = 128
FEAT = HEADS * SIZE
INTRA = 8
SPANS = 6
USED = INTRA + SPANS
CHUNK = 256
CHUNKS = FEAT // CHUNK
PAIRS = FEAT // 128
BLOCKS = 64
ROWS = FEAT // BLOCKS


def mm(a, b):
    return lax.dot_general(a, b, (((1,), (0,)), ((), ())), preferred_element_type=F32)


def mm_nt(a, b):
    return lax.dot_general(a, b, (((1,), (1,)), ((), ())), preferred_element_type=F32)


def mm_tn(a, b):
    return lax.dot_general(a, b, (((0,), (0,)), ((), ())), preferred_element_type=F32)


def onehot(chunk, quarter, rows=128):
    row = lax.broadcasted_iota(jnp.int32, (rows, CHUNK), 0)
    lane = lax.broadcasted_iota(jnp.int32, (rows, CHUNK), 1)
    if rows > 128:
        row = jnp.where(row >= 128, row - 128, row)
    head = chunk * (CHUNK // SIZE) + jnp.right_shift(lane, 6) + 32 * quarter
    return jnp.where(row == head, 1.0, 0.0).astype(BF16)


def split2(a):
    hi = a.astype(BF16)
    lo = (a - hi.astype(F32)).astype(BF16)
    return jnp.concatenate([hi, lo], axis=1)


def four(a):
    return jnp.concatenate([a, a, a, a], axis=1)


def sums_down():
    row = lax.broadcasted_iota(jnp.int32, (TOK, TOK), 0)
    col = lax.broadcasted_iota(jnp.int32, (TOK, TOK), 1)
    return jnp.where(row >= col, 1.0, 0.0).astype(F32)


def at_chunk(chunk):
    return pl.ds(pl.multiple_of(chunk * CHUNK, CHUNK), CHUNK)


def state_kernel(x_ref, b_ref, dt_ref, rate_ref, u_ref, cum_ref, dt4_ref):
    turned = dt_ref[...]
    dt4 = jnp.concatenate([turned, turned, turned, turned], axis=0).T
    cum = lax.dot_general(
        sums_down(), dt4 * four(rate_ref[...]), (((1,), (0,)), ((), ())),
        precision=HIGHEST, preferred_element_type=F32,
    )
    cum_ref[...] = cum
    dt4_ref[...] = dt4
    held = split2(jnp.exp(cum - cum[TOK - 1 : TOK]) * dt4)
    bmat = b_ref[...]

    @pl.loop(0, CHUNKS)
    def _(chunk):
        xs = x_ref[:, at_chunk(chunk)].astype(F32)
        state = mm_tn(bmat, (xs * mm(held, onehot(chunk, 0, 256))).astype(BF16))
        for half in range(2):
            u_ref[2 * chunk + half] = state[:, 128 * half : 128 * half + 128]


def cot_kernel(x_ref, g_ref, c_ref, cum_ref, w_ref, _after_ref, d0_ref, d_ref, lam_ref, sig_ref):
    fade = jnp.exp(-cum_ref[...])
    logit = mm_nt(x_ref[...], w_ref[:512])
    soft = jnp.maximum(logit, 0.0) + jnp.log1p(jnp.exp(-jnp.abs(logit)))
    lam_ref[...] = soft
    sig_ref[...] = 1.0 / (1.0 + jnp.exp(-logit))
    far = jnp.concatenate([split2(soft[:, 256:384] * fade), split2(soft[:, 384:512] * fade)], axis=0)
    cmat = c_ref[...]

    @pl.loop(0, CHUNKS)
    def _(chunk):
        gs = g_ref[:, at_chunk(chunk)].astype(F32)
        parts = [None] * SPANS
        for quarter in range(4):
            wide = mm(far if quarter < 2 else far[:TOK], onehot(chunk, quarter, 256))
            parts[quarter] = (wide[:TOK] * gs).astype(BF16)
            if quarter < 2:
                parts[4 + quarter] = (wide[TOK:] * gs).astype(BF16)
        cots = mm_tn(cmat, jnp.concatenate(parts, axis=1))
        side = chunk // (CHUNKS // 2)
        local = chunk - side * (CHUNKS // 2)
        for half in range(2):
            d0_ref[2 * chunk + half] = cots[:, 128 * half : 128 * half + 128]
            for span in range(1, SPANS):
                at = CHUNK * span + 128 * half
                d_ref[side, span - 1, 2 * local + half] = cots[:, at : at + 128]


def near_kernel(
    x_ref, g_ref, b_ref, c_ref, dt_ref, skip_ref, lam_ref, sig_ref, cum_ref, _after_ref,
    y_ref, dx_ref, db_ref, dc_ref, dl_ref, gw_ref, q_ref, w_ref, sk_ref,
    kst_ref, dk_ref, da_ref,
):
    bmat = b_ref[...]
    cmat = c_ref[...]
    cum = cum_ref[...]
    fade = jnp.exp(-cum)
    score = mm_nt(cmat, bmat)
    row = lax.broadcasted_iota(jnp.int32, (TOK, TOK), 0)
    col = lax.broadcasted_iota(jnp.int32, (TOK, TOK), 1)
    apart = jnp.bitwise_xor(row, col)

    def mask_of(level):
        if level == 0:
            return row == col
        return (row > col) & (jnp.right_shift(apart, level - 1) == 1)

    for level in range(INTRA):
        kst_ref[level * TOK : (level + 1) * TOK] = jnp.where(mask_of(level), score, 0.0).astype(BF16)
    near = jnp.concatenate(
        [split2(lam_ref[:, :128] * fade), split2(lam_ref[:, 128:256] * fade)], axis=0
    )
    lift = split2(jnp.exp(cum) * dt_ref[...])
    gain = split2(jnp.broadcast_to(four(skip_ref[...]), (8, 128)))
    dk_ref[...] = jnp.zeros_like(dk_ref)
    da_ref[...] = jnp.zeros_like(da_ref)
    q_ref[...] = jnp.zeros_like(q_ref)
    sk_ref[...] = jnp.zeros_like(sk_ref)

    @pl.loop(0, CHUNKS)
    def _(chunk):
        cols = at_chunk(chunk)
        xs = x_ref[:, cols].astype(F32)
        gs = g_ref[:, cols].astype(F32)
        spread0 = onehot(chunk, 0, 256)
        lifted = mm(lift, spread0)
        gains = mm(gain, spread0)[0:1]
        xd = (xs * lifted).astype(BF16)
        kst = kst_ref[...]
        mixed = mm(kst, xd)
        out = gains * xs
        parts = [None] * INTRA
        for quarter in range(4):
            wide = mm(near, onehot(chunk, quarter, 256))
            prods = []
            for part in range(2):
                level = 4 * part + quarter
                mult = wide[TOK * part : TOK * part + TOK]
                value = mixed[level * TOK : (level + 1) * TOK]
                out = out + mult * value
                prods.append((gs * value).astype(BF16))
                parts[level] = (mult * gs).astype(BF16)
            da_ref[...] += mm_nt(jnp.concatenate(prods, axis=0), onehot(chunk, quarter))
        y_ref[:, cols] = out
        agst = jnp.concatenate(parts, axis=0)
        dxd = mm_tn(kst, agst)
        dk_ref[...] += mm_nt(agst, xd)
        ones = onehot(chunk, 0)
        q_ref[...] += mm_nt((dxd * xs).astype(BF16), ones)
        dx_ref[:, cols] = dxd * lifted + gains * gs
        skrow = jnp.sum(xs * gs, axis=0, keepdims=True)
        sk_ref[...] += lax.dot_general(
            jnp.broadcast_to(skrow, (8, CHUNK)), ones.astype(F32), (((1,), (1,)), ((), ())),
            precision=HIGHEST, preferred_element_type=F32,
        )

    dscore = jnp.zeros((TOK, TOK), F32)
    for level in range(INTRA):
        dscore = dscore + jnp.where(mask_of(level), dk_ref[level * TOK : (level + 1) * TOK], 0.0)
    dscore = dscore.astype(BF16)
    dc_ref[...] = mm(dscore, bmat)
    db_ref[...] = mm_tn(dscore, cmat)
    dlam = []
    for part in range(2):
        da = da_ref[TOK * part : TOK * part + TOK]
        dlam.append(da * fade)
    w_ref[...] = dlam[0] * lam_ref[:, :128] + dlam[1] * lam_ref[:, 128:256]
    dlogit = (jnp.concatenate(dlam, axis=1) * sig_ref[:, :256]).astype(BF16)
    dl_ref[...] = dlogit
    for part in range(FEAT // 128):
        rows = mm_tn(x_ref[:, 128 * part : 128 * part + 128], dlogit)
        for block in range(128 // ROWS):
            at = part * (128 // ROWS) + block
            gw_ref[at % 2, at // 2] = rows[ROWS * block : ROWS * block + ROWS]


def spread_level(core_ref, x_ref, g_ref, c_ref, lam, fade_ref, y_ref, out_ref, dcs_ref, da_ref, levels, picked):
    cmat = c_ref[...]
    far = split2(lam * fade_ref[...])
    da_ref[...] = jnp.zeros_like(da_ref)
    core = core_ref[0]

    def step(local, chunk, mine):
        cols = at_chunk(chunk)
        gs = g_ref[:, cols].astype(F32)
        carried = jnp.concatenate([v.astype(BF16) for v in picked(chunk, local, mine)], axis=1)
        mixed = mm(cmat, carried)
        out = y_ref[:, cols]
        parts = []
        for quarter in range(levels):
            ones = onehot(chunk, quarter, 256)
            mult = mm(far, ones)
            value = mixed[:, CHUNK * quarter : CHUNK * quarter + CHUNK]
            out = out + mult * value
            da_ref[...] += mm_nt((gs * value).astype(BF16), ones[:128])
            parts.append((mult * gs).astype(BF16))
        out_ref[:, cols] = out.astype(out_ref.dtype)
        dcs_ref[...] += mm_nt(jnp.concatenate(parts, axis=1), carried)

    @pl.loop(0, CHUNKS // 2)
    def _(local):
        step(local, local + core * (CHUNKS // 2), True)

    @pl.loop(0, CHUNKS // 2)
    def _(local):
        step(local, local + (1 - core) * (CHUNKS // 2), False)

    return da_ref[...] * fade_ref[...]


def far_kernel(
    core_ref, x_ref, g_ref, c_ref, lam_ref, sig_ref, fade_ref, y_ref, dc_ref,
    first_ref, m1_ref, m2_ref, m3_ref, other_ref,
    out_ref, dcs_ref, dl_ref, w_ref,
    da_ref,
):
    lam = lam_ref[:, 256:384]
    dcs_ref[...] = dc_ref[...]

    def picked(chunk, local, mine):
        values = [first_ref[2 * chunk + half] for half in range(2)]
        for span, ref in enumerate((m1_ref, m2_ref, m3_ref)):
            for half in range(2):
                if mine:
                    values.append(ref[2 * local + half])
                else:
                    values.append(other_ref[span * (PAIRS // 2) + 2 * local + half])
        return values

    dlam = spread_level(
        core_ref, x_ref, g_ref, c_ref, lam, fade_ref, y_ref, out_ref, dcs_ref, da_ref, 4, picked
    )
    w_ref[...] = dlam * lam
    dl_ref[...] = (dlam * sig_ref[:, 256:384]).astype(BF16)


def line_kernel(
    core_ref, x_ref, g_ref, c_ref, lam_ref, sig_ref, fade_ref, y_ref, dc_ref, dl1_ref,
    m4_ref, m5_ref, other_ref,
    out_ref, dcout_ref, dl_ref, gw_ref, w_ref,
    da_ref, dcs_ref,
):
    lam = lam_ref[:, 384:512]
    dcs_ref[...] = dc_ref[...]

    def picked(chunk, local, mine):
        values = []
        for span, ref in enumerate((m4_ref, m5_ref)):
            for half in range(2):
                if mine:
                    values.append(ref[2 * local + half])
                else:
                    values.append(other_ref[span * (PAIRS // 2) + 2 * local + half])
        return values

    dlam = spread_level(
        core_ref, x_ref, g_ref, c_ref, lam, fade_ref, y_ref, out_ref, dcs_ref, da_ref, 2, picked
    )
    dcout_ref[...] = dcs_ref[...].astype(BF16)
    w_ref[...] = dlam * lam
    dlogit = (dlam * sig_ref[:, 384:512]).astype(BF16)
    dl_ref[...] = dlogit
    both = jnp.concatenate([dl1_ref[...], dlogit], axis=1)
    lane = lax.broadcasted_iota(jnp.int32, (ROWS // 2, 128), 1)
    for part in range(FEAT // 128):
        rows = mm_tn(x_ref[:, 128 * part : 128 * part + 128], both)
        turned = pltpu.roll(rows[:, 128:], 64, 1)
        for block in range(128 // ROWS):
            at = part * (128 // ROWS) + block
            top = ROWS * block
            mid = top + ROWS // 2
            gw_ref[at % 2, at // 2, :ROWS] = rows[top : top + ROWS, :128]
            gw_ref[at % 2, at // 2, ROWS:] = jnp.where(
                lane < 64, rows[top:mid, 128:], turned[mid : mid + ROWS // 2]
            )


def last_kernel(
    core_ref, x_ref, b_ref, dt_ref, cum_ref, rate_ref, w_ref, mine_ref, came_ref, lag_ref, fresh_ref, dx_ref, db_ref,
    dl0_ref, dl1_ref, dl2_ref, q_ref, w0_ref, w1_ref, w2_ref,
    dxout_ref, dbout_ref, ddt_ref, rate_out_ref,
    dbs_ref, q2_ref,
):
    bmat = b_ref[...]
    cum = cum_ref[...]
    dt4 = dt_ref[...]
    left = jnp.exp(cum - cum[TOK - 1 : TOK])
    held = split2(left * dt4)
    dlogit = jnp.concatenate([dl0_ref[...], dl1_ref[...], dl2_ref[...]], axis=1)
    q2_ref[...] = jnp.zeros_like(q2_ref)
    dbs_ref[...] = db_ref[...]

    core = core_ref[0]

    def step(local, chunk, source):
        cols = at_chunk(chunk)
        xs = x_ref[:, cols].astype(F32)
        spread = mm(held, onehot(chunk, 0, 256))
        du = jnp.concatenate(
            [
                (
                    source[2 * local + half] * lag_ref[2 * chunk + half]
                    + came_ref[PAIRS // 2 + 2 * chunk + half] * fresh_ref[0]
                ).astype(BF16)
                for half in range(2)
            ],
            axis=1,
        )
        dxs = mm(bmat, du)
        q2_ref[...] += mm_nt((dxs * xs).astype(BF16), onehot(chunk, 0))
        dbs_ref[...] += mm_nt((xs * spread).astype(BF16), du)
        dx = dx_ref[:, cols] + dxs * spread + mm(dlogit, w_ref[:512, cols])
        dxout_ref[:, cols] = dx.astype(BF16)

    @pl.loop(0, CHUNKS // 2)
    def _(local):
        step(local, local + core * (CHUNKS // 2), mine_ref)

    @pl.loop(0, CHUNKS // 2)
    def _(local):
        step(local, local + (1 - core) * (CHUNKS // 2), came_ref)

    dbout_ref[...] = dbs_ref[...].astype(BF16)
    q2 = q2_ref[...]
    q1 = q_ref[...]
    lift = jnp.exp(cum)
    gathered = w0_ref[...] + w1_ref[...] + w2_ref[...]
    queried = gathered + pltpu.roll(gathered, 32, 1)
    queried = queried + pltpu.roll(queried, 64, 1)
    keyed2 = q2 * left * dt4
    dcum = q1 * lift * dt4 + keyed2 - queried
    dlog = lax.dot_general(
        sums_down(), dcum, (((0,), (0,)), ((), ())), precision=HIGHEST, preferred_element_type=F32
    )
    dlog = dlog - jnp.sum(keyed2, axis=0, keepdims=True)
    ddt_ref[...] = rate_ref[...] * dlog[:, :32] + (q1 * lift + q2 * left)[:, :32]
    rate_out_ref[...] = jnp.sum(dt4 * dlog, axis=0, keepdims=True)


VMEM_LIMIT = 56 * 1024 * 1024
HALF = PAIRS // 2
FOLD = ROWS + ROWS // 2


def call(kernel, outs, scratch=(), flops=0, moved=1 << 20, specs=None):
    extra = {} if specs is None else {"in_specs": specs}
    return pl.pallas_call(
        kernel,
        out_shape=outs,
        scratch_shapes=list(scratch),
        compiler_params=pltpu.CompilerParams(vmem_limit_bytes=VMEM_LIMIT),
        cost_estimate=pl.CostEstimate(flops=flops, bytes_accessed=moved, transcendentals=0),
        **extra,
    )


def shaped(*dims, dtype=F32):
    return jax.ShapeDtypeStruct(dims, dtype)


def swap(value, bit, only=None):
    pairs = []
    for source in range(BLOCKS):
        if only is None or (source >> bit) % 2 == only:
            pairs.append((source, source ^ (1 << bit)))
    return lax.ppermute(value, "ctx", pairs)


def turn(value, bit):
    count = lax.axis_size("dp")
    return lax.ppermute(value, "dp", [(source, source ^ (1 << bit)) for source in range(count)])


def after(kernel, inputs):
    def body(row_ref, *refs):
        refs[inputs][...] = row_ref[...]
        kernel(*refs[:inputs], *refs[inputs + 1 :])

    return body


def row_of(per_head):
    pairs = per_head.reshape(per_head.shape[:-1] + (per_head.shape[-1] // 2, 1, 2))
    return jnp.repeat(pairs, SIZE, axis=-1)


def per_head(value):
    rows = jnp.sum(value, axis=1)
    return jnp.sum(rows.reshape(-1, 2, SIZE), axis=-1).reshape(-1)


def part(value, start, count):
    return lax.dynamic_slice_in_dim(value, start, count, 0)


def fold(rows, bits, steps=(0, 5, 4, 3, 2, 1)):
    for step in steps:
        half = rows.shape[0] // 2
        other = swap(part(rows, (1 - bits[step]) * half, half), step)
        rows = part(rows, bits[step] * half, half) + other
    return rows


def per_device(inputs, matrix_b, matrix_c, steps_dt, decay_rate, skip_gain, level_weight, grad_out):
    xs, bs, cs, gs = inputs[0], matrix_b[0], matrix_c[0], grad_out[0]
    turned_dt, turned_w = steps_dt[0].T, level_weight.T
    place = lax.axis_index("ctx")
    core = place % 2
    bits = [jnp.right_shift(place, span) % 2 for span in range(SPANS)]
    rate = decay_rate.reshape(1, HEADS)
    core_here = core.astype(jnp.int32).reshape(1)
    vmem = pl.BlockSpec(memory_space=pltpu.VMEM)
    smem = pl.BlockSpec(memory_space=pltpu.SMEM)
    anywhere = pl.BlockSpec(memory_space=pl.ANY)

    def choose(bit, low, high):
        return jnp.where(bits[bit] == 1, high, low)

    def mine_of(value):
        return part(value, core * HALF, HALF)

    def yours_of(value):
        return part(value, (1 - core) * HALF, HALF)

    states, cum, dt4 = call(
        state_kernel,
        (shaped(PAIRS, NST, 128), shaped(TOK, 128), shaped(TOK, 128)),
        flops=2 * TOK * FEAT * 2 * NST,
        moved=2 << 20,
    )(xs, bs, turned_dt, rate)
    first = swap(states, 0)

    own_sum = jnp.sum(turned_dt, axis=1)
    earlier = jnp.zeros_like(own_sum)
    sum_up, sum_in = [], []
    for span in range(SPANS):
        sum_in.append(earlier)
        if span < SPANS - 1:
            other = swap(own_sum[None], span)[0]
            sum_up.append(choose(span, other, own_sum))
            earlier = earlier + choose(span, jnp.zeros_like(other), other)
            own_sum = own_sum + other
    on = jnp.stack(bits).astype(F32)[:, None]
    half_up = [mine_of(row_of(jnp.exp(-value * decay_rate))) for value in sum_up]
    sum_in = jnp.stack(sum_in)
    fade_in = jnp.exp(-sum_in * rate) * on
    row_in = row_of(fade_in)

    mine, yours = mine_of(states), mine_of(first)
    lower = choose(0, mine, yours)
    lowers = [lower]
    held = lower * half_up[0] + choose(0, yours, mine)
    step_row, cot0, cots, lam, sig = call(
        after(cot_kernel, 6),
        (
            shaped(HALF, 1, 128),
            shaped(PAIRS, NST, 128),
            shaped(2, SPANS - 1, HALF, NST, 128),
            shaped(TOK, 512),
            shaped(TOK, 512),
        ),
        flops=2 * TOK * FEAT * (512 + 10 * NST),
        moved=10 << 20,
        specs=[vmem] * 6 + [anywhere],
    )(half_up[1], xs, gs, cs, cum, turned_w, held)
    carried = []
    for span in range(1, SPANS):
        other = swap(held, span, 0 if span == SPANS - 1 else None)
        carried.append(other)
        lower = choose(span, held, other)
        lowers.append(lower)
        if span < SPANS - 1:
            held = lower * (step_row if span == 1 else half_up[span]) + choose(span, other, held)
    across_near = swap(jnp.concatenate(carried[:3]), 0)
    across_far = swap(jnp.concatenate(carried[3:]), 0)

    row_far = jnp.stack([row_in[1:, :HALF], row_in[1:, HALF:]])
    away = lax.dynamic_index_in_dim(cots, 1 - core, 0, keepdims=False)
    away = away * lax.dynamic_index_in_dim(row_far, 1 - core, 0, keepdims=False)
    came = swap(away, 0)
    level = lax.dynamic_index_in_dim(cots, core, 0, keepdims=False)
    level = level * lax.dynamic_index_in_dim(row_far, core, 0, keepdims=False) + came

    back4, y_near, dx_near, db_near, dc_near, dl_near, gw_near, q_near, w_near, skip_sum = call(
        after(near_kernel, 10),
        (
            shaped(HALF, 1, 128),
            shaped(TOK, FEAT),
            shaped(TOK, FEAT),
            shaped(TOK, NST),
            shaped(TOK, NST),
            shaped(TOK, 256, dtype=BF16),
            shaped(2, BLOCKS // 2, ROWS, 256),
            shaped(TOK, 128),
            shaped(TOK, 128),
            shaped(8, 128),
        ),
        scratch=(
            pltpu.VMEM((INTRA * TOK, TOK), BF16),
            pltpu.VMEM((INTRA * TOK, TOK), F32),
            pltpu.VMEM((2 * TOK, 128), F32),
        ),
        flops=2 * TOK * FEAT * (5 * INTRA * NST),
        moved=12 << 20,
        specs=[vmem] * 10 + [anywhere],
    )(half_up[4], xs, gs, bs, cs, dt4, skip_gain.reshape(1, HEADS), lam, sig, cum, level)
    near_rows = fold(gw_near.reshape(FEAT, 256), bits)

    fade_t = jnp.exp(-cum)
    fade_far = fade_t[None] * jnp.concatenate([fade_in, jnp.zeros((2, HEADS), F32)]).reshape(2, 1, 128)
    back2, y_far, dc_far, dl_far, w_far = call(
        after(far_kernel, 14),
        (shaped(HALF, 1, 128), shaped(TOK, FEAT), shaped(TOK, NST), shaped(TOK, 128, dtype=BF16), shaped(TOK, 128)),
        scratch=[pltpu.VMEM((TOK, 128), F32)],
        flops=2 * TOK * FEAT * 16 * NST,
        moved=10 << 20,
        specs=[vmem, smem] + [vmem] * 13,
    )(
        half_up[2], core_here, xs, gs, cs, lam, sig, fade_far[0], y_near, dc_near,
        first, carried[0], carried[1], carried[2], across_near,
    )
    back1, output, grad_c, dl_line, gw_line, w_line = call(
        after(line_kernel, 13),
        (
            shaped(HALF, 1, 128),
            shaped(TOK, FEAT, dtype=BF16),
            shaped(TOK, NST, dtype=BF16),
            shaped(TOK, 128, dtype=BF16),
            shaped(2, BLOCKS // 2, FOLD, 128),
            shaped(TOK, 128),
        ),
        scratch=[pltpu.VMEM((TOK, 128), F32), pltpu.VMEM((TOK, NST), F32)],
        flops=2 * TOK * FEAT * 10 * NST,
        moved=6 << 20,
        specs=[vmem, smem] + [vmem] * 12,
    )(
        half_up[1], core_here, xs, gs, cs, lam, sig, fade_far[1], y_far, dc_far, dl_far,
        carried[3], carried[4], across_far,
    )
    grad = swap(level[SPANS - 2], SPANS - 1, 1)
    crossed = [None] * (SPANS - 1)
    for span in reversed(range(1, SPANS - 1)):
        row = {4: back4, 3: half_up[3], 2: back2, 1: back1}[span]
        crossed[span] = per_head(lowers[span] * row * grad)
        back = swap(choose(span, grad, grad * row + level[span - 1]), span)
        grad = choose(span, grad * row, grad) + back
    crossed[0] = per_head(lowers[0] * half_up[0] * grad)
    last_came = swap(jnp.concatenate([grad, cot0 * row_in[0]]), 0)
    lag = choose(0, row_of(jnp.exp(-sum_up[0] * decay_rate)), jnp.ones((PAIRS, 1, 128), F32))
    fresh = choose(0, jnp.ones((1, 1, 128), F32), jnp.zeros((1, 1, 128), F32))
    late_place, grad_inputs, grad_b, ddt, rate_row = call(
        after(last_kernel, 20),
        (
            shaped(1, 128, dtype=jnp.int32),
            shaped(TOK, FEAT, dtype=BF16),
            shaped(TOK, NST, dtype=BF16),
            shaped(TOK, HEADS),
            shaped(1, 128),
        ),
        scratch=[pltpu.VMEM((TOK, NST), F32), pltpu.VMEM((TOK, 128), F32)],
        flops=2 * TOK * FEAT * 8 * NST,
        moved=10 << 20,
        specs=[vmem, smem] + [vmem] * 19,
    )(
        jnp.full((1, 128), place, jnp.int32), core_here, xs, bs, dt4, cum, rate, turned_w, grad, last_came, lag, fresh,
        dx_near, db_near, dl_near, dl_far, dl_line, q_near, w_near, w_far, w_line,
    )

    late_bits = [jnp.right_shift(late_place[0, 0], span) % 2 for span in range(SPANS)]
    rows = fold(gw_line.reshape(BLOCKS * FOLD, 128), bits, (0, 5))
    rows = fold(rows, late_bits, (4, 3, 2, 1))
    rows = jnp.concatenate([rows, near_rows.reshape(2 * ROWS, 128)])
    for step in range(2):
        rows = rows + turn(rows, step)
    near_rows = rows[FOLD:]

    queried = jnp.concatenate([jnp.sum(w_far, axis=0), jnp.sum(w_line, axis=0)]).reshape(8, HEADS)[:SPANS] * on
    halves = jnp.concatenate([jnp.stack(crossed), jnp.zeros((1, HEADS // 2), F32)])
    keyed = jnp.zeros((SPANS, 2, HEADS // 2), F32)
    keyed = lax.dynamic_update_slice_in_dim(keyed, halves[:, None], core, 1).reshape(SPANS, HEADS)
    inside = jnp.sum(sum_in * queried, axis=0) + jnp.sum(jnp.stack(sum_up) * keyed[: SPANS - 1], axis=0)
    extra = jnp.concatenate(
        [
            queried,
            keyed,
            (rate_row[0, :HEADS] - inside)[None],
            skip_sum[:1, :HEADS],
            jnp.zeros((2, HEADS), F32),
        ]
    )
    between = jnp.zeros((HEADS,), F32)
    for step in range(SPANS):
        came = swap(extra, step)
        if step + 1 < SPANS:
            later = jnp.sum(on[step + 1 :] * came[step + 1 : SPANS], axis=0)
            between = between + choose(step, later, jnp.zeros_like(later))
        extra = extra + came
        between = between + on[step] * extra[SPANS + step]
    ends = extra[2 * SPANS : 2 * SPANS + 2]
    for step in range(2):
        ends = ends + turn(ends, step)
    packed = rows[ROWS:FOLD]
    grad_level = jnp.concatenate(
        [
            near_rows.reshape(ROWS, 256),
            rows[:ROWS],
            jnp.concatenate([packed[:, :64], packed[:, 64:]], axis=0),
            jnp.zeros((ROWS, level_weight.shape[1] - 448), F32),
        ],
        axis=1,
    )
    grad_dt = (ddt - rate * between[None])[None]
    return (output[None], grad_inputs[None], grad_b[None], grad_c[None], grad_dt, ends[0], ends[1], grad_level)


def solution(mesh):
    split = P("dp", "ctx", None)
    return jax.shard_map(
        per_device,
        mesh=mesh,
        in_specs=(split, split, split, split, P(), P(), P(), split),
        out_specs=(split, split, split, split, split, P(), P(), P("ctx", None)),
        check_vma=False,
    )
```

```python
import jax
import jax.numpy as jnp
import numpy as np
from jax import lax
from jax.experimental import pallas as pl
from jax.experimental.pallas import tpu as pltpu
from jax.sharding import PartitionSpec as P

F32 = jnp.float32
BF16 = jnp.bfloat16
HIGHEST = lax.Precision.HIGHEST
HEADS = 32
SIZE = 64
TOK = 128
NST = 128
FEAT = HEADS * SIZE
INTRA = 8
SPANS = 6
USED = INTRA + SPANS
CHUNK = 256
CHUNKS = FEAT // CHUNK
PAIRS = FEAT // 128
HALF = PAIRS // 2
BLOCKS = 64
ROWS = FEAT // BLOCKS


def mm(a, b):
    return lax.dot_general(a, b, (((1,), (0,)), ((), ())), preferred_element_type=F32)


def mm_nt(a, b):
    return lax.dot_general(a, b, (((1,), (1,)), ((), ())), preferred_element_type=F32)


def mm_tn(a, b):
    return lax.dot_general(a, b, (((0,), (0,)), ((), ())), preferred_element_type=F32)


def onehot(chunk, quarter, rows=128):
    row = lax.broadcasted_iota(jnp.int32, (rows, CHUNK), 0)
    lane = lax.broadcasted_iota(jnp.int32, (rows, CHUNK), 1)
    if rows > 128:
        row = jnp.where(row >= 128, row - 128, row)
    head = chunk * (CHUNK // SIZE) + jnp.right_shift(lane, 6) + 32 * quarter
    return jnp.where(row == head, 1.0, 0.0).astype(BF16)


def split2(a):
    hi = a.astype(BF16)
    lo = (a - hi.astype(F32)).astype(BF16)
    return jnp.concatenate([hi, lo], axis=1)


def four(a):
    return jnp.concatenate([a, a, a, a], axis=1)


def sums_down():
    row = lax.broadcasted_iota(jnp.int32, (TOK, TOK), 0)
    col = lax.broadcasted_iota(jnp.int32, (TOK, TOK), 1)
    return jnp.where(row >= col, 1.0, 0.0).astype(F32)


def at_chunk(chunk):
    return pl.ds(pl.multiple_of(chunk * CHUNK, CHUNK), CHUNK)


def rows_of(per_head):
    pair = lax.broadcasted_iota(jnp.int32, (PAIRS, HEADS), 0)
    head = lax.broadcasted_iota(jnp.int32, (PAIRS, HEADS), 1)
    picked = jnp.where(jnp.right_shift(head, 1) == pair, per_head, 0.0)
    side = lax.broadcasted_iota(jnp.int32, (HEADS, 128), 0) % 2
    lane = lax.broadcasted_iota(jnp.int32, (HEADS, 128), 1)
    spread = jnp.where(side == jnp.right_shift(lane, 6), 1.0, 0.0).astype(F32)
    return lax.dot_general(
        picked, spread, (((1,), (0,)), ((), ())), precision=HIGHEST, preferred_element_type=F32
    )


def rows_kernel(up_ref, in_ref, there_ref, on_ref, rate_ref, rows_up_ref, rows_own_ref, rows_there_ref, fade_ref):
    rate = rate_ref[...]
    fade_ref[...] = jnp.exp(-in_ref[...] * rate) * on_ref[...]
    for span in range(1, SPANS - 1):
        rows_up_ref[span - 1] = rows_of(jnp.exp(-up_ref[span : span + 1] * rate))
    for span in range(1, SPANS):
        on = on_ref[span : span + 1]
        rows_own_ref[span - 1] = rows_of(jnp.exp(-in_ref[span : span + 1] * rate) * on)
        rows_there_ref[span - 1] = rows_of(jnp.exp(-(in_ref[span : span + 1] + there_ref[...]) * rate) * on)


def state_kernel(x_ref, b_ref, dt_ref, rate_ref, up_ref, u_ref, cum_ref, dt4_ref, row_ref):
    row_ref[...] = rows_of(jnp.exp(-up_ref[...] * rate_ref[...]))
    turned = dt_ref[...]
    dt4 = jnp.concatenate([turned, turned, turned, turned], axis=0).T
    cum = lax.dot_general(
        sums_down(), dt4 * four(rate_ref[...]), (((1,), (0,)), ((), ())),
        precision=HIGHEST, preferred_element_type=F32,
    )
    cum_ref[...] = cum
    dt4_ref[...] = dt4
    held = split2(jnp.exp(cum - cum[TOK - 1 : TOK]) * dt4)
    bmat = b_ref[...]

    @pl.loop(0, CHUNKS, unroll=CHUNKS)
    def _(chunk):
        xs = x_ref[:, at_chunk(chunk)].astype(F32)
        state = mm_tn(bmat, (xs * mm(held, onehot(chunk, 0, 256))).astype(BF16))
        for half in range(2):
            u_ref[2 * chunk + half] = state[:, 128 * half : 128 * half + 128]


def cot_kernel(core_ref, x_ref, g_ref, c_ref, cum_ref, w_ref, d0_ref, own_ref, away_ref, lam_ref, sig_ref):
    fade = jnp.exp(-cum_ref[...])
    logit = mm_nt(x_ref[...], w_ref[:512])
    soft = jnp.maximum(logit, 0.0) + jnp.log1p(jnp.exp(-jnp.abs(logit)))
    lam_ref[...] = soft
    sig_ref[...] = 1.0 / (1.0 + jnp.exp(-logit))
    far = jnp.concatenate([split2(soft[:, 256:384] * fade), split2(soft[:, 384:512] * fade)], axis=0)
    cmat = c_ref[...]

    core = core_ref[0]

    def step(local, chunk, d_ref):
        gs = g_ref[:, at_chunk(chunk)].astype(F32)
        parts = [None] * SPANS
        for quarter in range(4):
            wide = mm(far if quarter < 2 else far[:TOK], onehot(chunk, quarter, 256))
            parts[quarter] = (wide[:TOK] * gs).astype(BF16)
            if quarter < 2:
                parts[4 + quarter] = (wide[TOK:] * gs).astype(BF16)
        cots = mm_tn(cmat, jnp.concatenate(parts, axis=1))
        for half in range(2):
            d0_ref[2 * chunk + half] = cots[:, 128 * half : 128 * half + 128]
            for span in range(1, SPANS):
                at = CHUNK * span + 128 * half
                d_ref[span - 1, 2 * local + half] = cots[:, at : at + 128]

    @pl.loop(0, CHUNKS // 2, unroll=CHUNKS // 2)
    def _(local):
        step(local, local + (1 - core) * (CHUNKS // 2), away_ref)

    @pl.loop(0, CHUNKS // 2, unroll=CHUNKS // 2)
    def _(local):
        step(local, local + core * (CHUNKS // 2), own_ref)


def near_kernel(
    x_ref, g_ref, b_ref, c_ref, dt_ref, skip_ref, lam_ref, sig_ref, cum_ref, _after_ref,
    y_ref, dx_ref, db_ref, dc_ref, dl_ref, gw_ref, q_ref, w_ref, sk_ref,
    kst_ref, dk_ref, da_ref,
):
    bmat = b_ref[...]
    cmat = c_ref[...]
    cum = cum_ref[...]
    fade = jnp.exp(-cum)
    score = mm_nt(cmat, bmat)
    row = lax.broadcasted_iota(jnp.int32, (TOK, TOK), 0)
    col = lax.broadcasted_iota(jnp.int32, (TOK, TOK), 1)
    apart = jnp.bitwise_xor(row, col)

    def mask_of(level):
        if level == 0:
            return row == col
        return (row > col) & (jnp.right_shift(apart, level - 1) == 1)

    for level in range(INTRA):
        kst_ref[level * TOK : (level + 1) * TOK] = jnp.where(mask_of(level), score, 0.0).astype(BF16)
    near = jnp.concatenate(
        [split2(lam_ref[:, :128] * fade), split2(lam_ref[:, 128:256] * fade)], axis=0
    )
    lift = split2(jnp.exp(cum) * dt_ref[...])
    gain = split2(jnp.broadcast_to(four(skip_ref[...]), (8, 128)))
    dk_ref[...] = jnp.zeros_like(dk_ref)
    da_ref[...] = jnp.zeros_like(da_ref)
    q_ref[...] = jnp.zeros_like(q_ref)
    sk_ref[...] = jnp.zeros_like(sk_ref)

    @pl.loop(0, CHUNKS, unroll=CHUNKS)
    def _(chunk):
        cols = at_chunk(chunk)
        xs = x_ref[:, cols].astype(F32)
        gs = g_ref[:, cols].astype(F32)
        spread0 = onehot(chunk, 0, 256)
        lifted = mm(lift, spread0)
        gains = mm(gain, spread0)[0:1]
        xd = (xs * lifted).astype(BF16)
        kst = kst_ref[...]
        mixed = mm(kst, xd)
        out = gains * xs
        parts = [None] * INTRA
        for quarter in range(4):
            wide = mm(near, onehot(chunk, quarter, 256))
            prods = []
            for part in range(2):
                level = 4 * part + quarter
                mult = wide[TOK * part : TOK * part + TOK]
                value = mixed[level * TOK : (level + 1) * TOK]
                out = out + mult * value
                prods.append((gs * value).astype(BF16))
                parts[level] = (mult * gs).astype(BF16)
            da_ref[...] += mm_nt(jnp.concatenate(prods, axis=0), onehot(chunk, quarter))
        y_ref[:, cols] = out
        agst = jnp.concatenate(parts, axis=0)
        dxd = mm_tn(kst, agst)
        dk_ref[...] += mm_nt(agst, xd)
        ones = onehot(chunk, 0)
        q_ref[...] += mm_nt((dxd * xs).astype(BF16), ones)
        dx_ref[:, cols] = dxd * lifted + gains * gs
        skrow = jnp.sum(xs * gs, axis=0, keepdims=True)
        sk_ref[...] += lax.dot_general(
            jnp.broadcast_to(skrow, (8, CHUNK)), ones.astype(F32), (((1,), (1,)), ((), ())),
            precision=HIGHEST, preferred_element_type=F32,
        )

    dscore = jnp.zeros((TOK, TOK), F32)
    for level in range(INTRA):
        dscore = dscore + jnp.where(mask_of(level), dk_ref[level * TOK : (level + 1) * TOK], 0.0)
    dscore = dscore.astype(BF16)
    dc_ref[...] = mm(dscore, bmat)
    db_ref[...] = mm_tn(dscore, cmat)
    dlam = []
    for part in range(2):
        da = da_ref[TOK * part : TOK * part + TOK]
        dlam.append(da * fade)
    w_ref[...] = dlam[0] * lam_ref[:, :128] + dlam[1] * lam_ref[:, 128:256]
    dlogit = (jnp.concatenate(dlam, axis=1) * sig_ref[:, :256]).astype(BF16)
    dl_ref[...] = dlogit
    for part in range(FEAT // 128):
        rows = mm_tn(x_ref[:, 128 * part : 128 * part + 128], dlogit)
        for block in range(128 // ROWS):
            at = part * (128 // ROWS) + block
            gw_ref[at % 2, at // 2] = rows[ROWS * block : ROWS * block + ROWS]


def spread_level(core_ref, x_ref, g_ref, c_ref, lam, fade_ref, y_ref, out_ref, dcs_ref, da_ref, levels, picked):
    cmat = c_ref[...]
    far = split2(lam * fade_ref[...])
    da_ref[...] = jnp.zeros_like(da_ref)
    core = core_ref[0]

    def step(local, chunk, mine):
        cols = at_chunk(chunk)
        gs = g_ref[:, cols].astype(F32)
        carried = jnp.concatenate([v.astype(BF16) for v in picked(chunk, local, mine)], axis=1)
        mixed = mm(cmat, carried)
        out = y_ref[:, cols]
        parts = []
        for quarter in range(levels):
            ones = onehot(chunk, quarter, 256)
            mult = mm(far, ones)
            value = mixed[:, CHUNK * quarter : CHUNK * quarter + CHUNK]
            out = out + mult * value
            da_ref[...] += mm_nt((gs * value).astype(BF16), ones[:128])
            parts.append((mult * gs).astype(BF16))
        out_ref[:, cols] = out.astype(out_ref.dtype)
        dcs_ref[...] += mm_nt(jnp.concatenate(parts, axis=1), carried)

    @pl.loop(0, CHUNKS // 2, unroll=CHUNKS // 2)
    def _(local):
        step(local, local + core * (CHUNKS // 2), True)

    @pl.loop(0, CHUNKS // 2, unroll=CHUNKS // 2)
    def _(local):
        step(local, local + (1 - core) * (CHUNKS // 2), False)

    return da_ref[...] * fade_ref[...]


def far_kernel(
    core_ref, x_ref, g_ref, c_ref, lam_ref, sig_ref, fade_ref, y_ref, dc_ref,
    first_ref, m1_ref, m2_ref, m3_ref, other_ref, _after_ref,
    out_ref, dcs_ref, dl_ref, w_ref,
    da_ref,
):
    lam = lam_ref[:, 256:384]
    dcs_ref[...] = dc_ref[...]

    def picked(chunk, local, mine):
        values = [first_ref[2 * chunk + half] for half in range(2)]
        for span, ref in enumerate((m1_ref, m2_ref, m3_ref)):
            for half in range(2):
                if mine:
                    values.append(ref[2 * local + half])
                else:
                    values.append(other_ref[span * (PAIRS // 2) + 2 * local + half])
        return values

    dlam = spread_level(
        core_ref, x_ref, g_ref, c_ref, lam, fade_ref, y_ref, out_ref, dcs_ref, da_ref, 4, picked
    )
    w_ref[...] = dlam * lam
    dl_ref[...] = (dlam * sig_ref[:, 256:384]).astype(BF16)


def line_kernel(
    core_ref, x_ref, g_ref, c_ref, lam_ref, sig_ref, fade_ref, y_ref, dc_ref, dl1_ref,
    m4_ref, m5_ref, other_ref, _after_ref,
    out_ref, dcout_ref, dl_ref, gw_ref, w_ref,
    da_ref, dcs_ref,
):
    lam = lam_ref[:, 384:512]
    dcs_ref[...] = dc_ref[...]

    def picked(chunk, local, mine):
        values = []
        for span, ref in enumerate((m4_ref, m5_ref)):
            for half in range(2):
                if mine:
                    values.append(ref[2 * local + half])
                else:
                    values.append(other_ref[span * (PAIRS // 2) + 2 * local + half])
        return values

    dlam = spread_level(
        core_ref, x_ref, g_ref, c_ref, lam, fade_ref, y_ref, out_ref, dcs_ref, da_ref, 2, picked
    )
    dcout_ref[...] = dcs_ref[...].astype(BF16)
    w_ref[...] = dlam * lam
    dlogit = (dlam * sig_ref[:, 384:512]).astype(BF16)
    dl_ref[...] = dlogit
    both = jnp.concatenate([dl1_ref[...], dlogit], axis=1)
    lane = lax.broadcasted_iota(jnp.int32, (ROWS // 2, 128), 1)
    for part in range(FEAT // 128):
        rows = mm_tn(x_ref[:, 128 * part : 128 * part + 128], both)
        turned = pltpu.roll(rows[:, 128:], 64, 1)
        for block in range(128 // ROWS):
            at = part * (128 // ROWS) + block
            top = ROWS * block
            mid = top + ROWS // 2
            gw_ref[at % 2, at // 2, :ROWS] = rows[top : top + ROWS, :128]
            gw_ref[at % 2, at // 2, ROWS:] = jnp.where(
                lane < 64, rows[top:mid, 128:], turned[mid : mid + ROWS // 2]
            )


def last_kernel(
    core_ref, x_ref, b_ref, dt_ref, cum_ref, rate_ref, w_ref, mine_ref, came_ref, lag_ref, fresh_ref, dx_ref, db_ref,
    dl0_ref, dl1_ref, dl2_ref, q_ref, w0_ref, w1_ref, w2_ref,
    dxout_ref, dbout_ref, ddt_ref, rate_out_ref,
    dbs_ref, q2_ref,
):
    bmat = b_ref[...]
    cum = cum_ref[...]
    dt4 = dt_ref[...]
    left = jnp.exp(cum - cum[TOK - 1 : TOK])
    held = split2(left * dt4)
    dlogit = jnp.concatenate([dl0_ref[...], dl1_ref[...], dl2_ref[...]], axis=1)
    q2_ref[...] = jnp.zeros_like(q2_ref)
    dbs_ref[...] = db_ref[...]

    core = core_ref[0]

    def step(local, chunk, source):
        cols = at_chunk(chunk)
        xs = x_ref[:, cols].astype(F32)
        spread = mm(held, onehot(chunk, 0, 256))
        du = jnp.concatenate(
            [
                (
                    source[2 * local + half] * lag_ref[2 * chunk + half]
                    + came_ref[PAIRS // 2 + 2 * chunk + half] * fresh_ref[0]
                ).astype(BF16)
                for half in range(2)
            ],
            axis=1,
        )
        dxs = mm(bmat, du)
        q2_ref[...] += mm_nt((dxs * xs).astype(BF16), onehot(chunk, 0))
        dbs_ref[...] += mm_nt((xs * spread).astype(BF16), du)
        dx = dx_ref[:, cols] + dxs * spread + mm(dlogit, w_ref[:512, cols])
        dxout_ref[:, cols] = dx.astype(BF16)

    @pl.loop(0, CHUNKS // 2, unroll=CHUNKS // 2)
    def _(local):
        step(local, local + core * (CHUNKS // 2), mine_ref)

    @pl.loop(0, CHUNKS // 2, unroll=CHUNKS // 2)
    def _(local):
        step(local, local + (1 - core) * (CHUNKS // 2), came_ref)

    dbout_ref[...] = dbs_ref[...].astype(BF16)
    q2 = q2_ref[...]
    q1 = q_ref[...]
    lift = jnp.exp(cum)
    gathered = w0_ref[...] + w1_ref[...] + w2_ref[...]
    queried = gathered + pltpu.roll(gathered, 32, 1)
    queried = queried + pltpu.roll(queried, 64, 1)
    keyed2 = q2 * left * dt4
    dcum = q1 * lift * dt4 + keyed2 - queried
    dlog = lax.dot_general(
        sums_down(), dcum, (((0,), (0,)), ((), ())), precision=HIGHEST, preferred_element_type=F32
    )
    dlog = dlog - jnp.sum(keyed2, axis=0, keepdims=True)
    ddt_ref[...] = rate_ref[...] * dlog[:, :32] + (q1 * lift + q2 * left)[:, :32]
    rate_out_ref[...] = jnp.sum(dt4 * dlog, axis=0, keepdims=True)


def bit_of(place_ref, span):
    return jnp.right_shift(place_ref[0], span) % 2


def half_of(rows_ref, index, place_ref):
    return rows_ref[index, pl.ds(pl.multiple_of(bit_of(place_ref, 0) * HALF, HALF), HALF), :]


def up_step(span, place_ref, held_ref, other_ref, rows_ref, lower_ref, next_ref):
    upper = bit_of(place_ref, span) == 1
    rows = half_of(rows_ref, span - 1, place_ref)
    for pair in range(HALF):
        mine, other = held_ref[pair], other_ref[pair]
        lower = jnp.where(upper, other, mine)
        lower_ref[pair] = lower
        next_ref[pair] = lower * rows[pair : pair + 1] + jnp.where(upper, mine, other)


def level_of(span, place_ref, own_ref, came_ref, rows_own_ref, rows_there_ref):
    rows_own = half_of(rows_own_ref, span - 1, place_ref)
    rows_there = half_of(rows_there_ref, span - 1, place_ref)

    def piece(pair):
        return own_ref[0, pair] * rows_own[pair : pair + 1] + came_ref[0, pair] * rows_there[pair : pair + 1]

    return piece


def down_step(span, place_ref, grad, piece, rows_ref, send_ref, keep_ref, crossed_ref=None, lower_ref=None):
    upper = bit_of(place_ref, span) == 1
    rows = half_of(rows_ref, span - 1, place_ref)
    for pair in range(HALF):
        here = grad(pair)
        faded = here * rows[pair : pair + 1]
        send_ref[pair] = jnp.where(upper, faded + piece(pair), here)
        keep_ref[pair] = jnp.where(upper, here, faded)
        if crossed_ref is not None:
            crossed_ref[pair : pair + 1] = jnp.sum(lower_ref[pair] * faded, axis=0, keepdims=True)


def step1_kernel(place_ref, rows_ref, rows_own_ref, rows_there_ref, held_ref, other_ref, own_ref, came_ref, lower_ref, next_ref, send_ref):
    up_step(1, place_ref, held_ref, other_ref, rows_ref, lower_ref, next_ref)
    piece = level_of(5, place_ref, own_ref, came_ref, rows_own_ref, rows_there_ref)
    for pair in range(HALF):
        send_ref[pair] = piece(pair)


def step2_kernel(place_ref, rows_ref, rows_own_ref, rows_there_ref, held_ref, other_ref, own_ref, came_ref, back_ref, lower_ref, next_ref, send_ref, keep_ref):
    up_step(2, place_ref, held_ref, other_ref, rows_ref, lower_ref, next_ref)
    piece = level_of(4, place_ref, own_ref, came_ref, rows_own_ref, rows_there_ref)
    down_step(4, place_ref, lambda pair: back_ref[pair], piece, rows_ref, send_ref, keep_ref)


def step3_kernel(place_ref, rows_ref, rows_own_ref, rows_there_ref, held_ref, other_ref, own_ref, came_ref, kept_ref, back_ref, _after_ref, lower_ref, next_ref, send_ref, keep_ref, crossed_ref, place_out_ref):
    place_out_ref[...] = jnp.full((1, 128), place_ref[0], jnp.int32)
    up_step(3, place_ref, held_ref, other_ref, rows_ref, lower_ref, next_ref)
    piece = level_of(3, place_ref, own_ref, came_ref, rows_own_ref, rows_there_ref)
    down_step(3, place_ref, lambda pair: kept_ref[pair] + back_ref[pair], piece, rows_ref, send_ref, keep_ref, crossed_ref, lower_ref)


def step4_kernel(place_ref, rows_ref, rows_own_ref, rows_there_ref, held_ref, other_ref, own_ref, came_ref, kept_ref, back_ref, first_ref, lower2_ref, next_ref, send_ref, keep_ref, crossed_ref, crossed4_ref):
    upper = bit_of(place_ref, 4) == 1
    rows = half_of(rows_ref, 3, place_ref)
    for pair in range(HALF):
        mine, other = held_ref[pair], other_ref[pair]
        faded = jnp.where(upper, other, mine) * rows[pair : pair + 1]
        next_ref[pair] = faded + jnp.where(upper, mine, other)
        crossed4_ref[pair : pair + 1] = jnp.sum(faded * first_ref[pair], axis=0, keepdims=True)
    piece = level_of(2, place_ref, own_ref, came_ref, rows_own_ref, rows_there_ref)
    down_step(2, place_ref, lambda pair: kept_ref[pair] + back_ref[pair], piece, rows_ref, send_ref, keep_ref, crossed_ref, lower2_ref)


def step5_kernel(place_ref, rows_ref, rows_own_ref, rows_there_ref, own_ref, came_ref, kept_ref, back_ref, lower1_ref, level4_ref, level5_ref, _after_ref, send_ref, keep_ref, crossed_ref, both_ref):
    for pair in range(HALF):
        both_ref[pair] = level4_ref[pair]
        both_ref[HALF + pair] = level5_ref[pair]
    piece = level_of(1, place_ref, own_ref, came_ref, rows_own_ref, rows_there_ref)
    down_step(1, place_ref, lambda pair: kept_ref[pair] + back_ref[pair], piece, rows_ref, send_ref, keep_ref, crossed_ref, lower1_ref)


def step6_kernel(place_ref, row_ref, kept_ref, back_ref, lower0_ref, cot_ref, _after_ref, send_ref, crossed_ref):
    rows = row_ref[pl.ds(pl.multiple_of(bit_of(place_ref, 0) * HALF, HALF), HALF), :]
    upper = bit_of(place_ref, 0) == 1
    for pair in range(HALF):
        grad = kept_ref[pair] + back_ref[pair]
        send_ref[pair] = grad
        crossed_ref[pair : pair + 1] = jnp.sum(lower0_ref[pair] * rows[pair : pair + 1] * grad, axis=0, keepdims=True)
    for pair in range(PAIRS):
        send_ref[HALF + pair] = jnp.where(upper, cot_ref[pair], 0.0)


VMEM_LIMIT = 56 * 1024 * 1024
FOLD = ROWS + ROWS // 2


def call(kernel, outs, scratch=(), flops=0, moved=1 << 20, specs=None):
    extra = {} if specs is None else {"in_specs": specs}
    return pl.pallas_call(
        kernel,
        out_shape=outs,
        scratch_shapes=list(scratch),
        compiler_params=pltpu.CompilerParams(vmem_limit_bytes=VMEM_LIMIT),
        cost_estimate=pl.CostEstimate(flops=flops, bytes_accessed=moved, transcendentals=0),
        **extra,
    )


def one_step(kernel, outs, *operands):
    specs, arrays = [pl.BlockSpec(memory_space=pltpu.SMEM)], [operands[0]]
    for operand in operands[1:]:
        if not isinstance(operand, tuple):
            arrays.append(operand)
            specs.append(pl.BlockSpec(operand.shape, lambda _, rank=operand.ndim: (0,) * rank))
        elif operand[0] == "slab":
            arrays.append(operand[2])
            specs.append(pl.BlockSpec((1,) + operand[2].shape[1:], lambda _, at=operand[1]: (at, 0, 0, 0)))
        else:
            arrays.append(operand[1])
            specs.append(pl.BlockSpec(memory_space=pl.ANY))
    return pl.pallas_call(
        kernel,
        grid=(1,),
        out_shape=tuple(outs),
        in_specs=specs,
        out_specs=tuple(pl.BlockSpec(out.shape, lambda _, rank=len(out.shape): (0,) * rank) for out in outs),
        compiler_params=pltpu.CompilerParams(vmem_limit_bytes=VMEM_LIMIT),
        cost_estimate=pl.CostEstimate(flops=1 << 22, bytes_accessed=4 << 20, transcendentals=0),
    )(*arrays)


def shaped(*dims, dtype=F32):
    return jax.ShapeDtypeStruct(dims, dtype)


def swap(value, bit, only=None):
    pairs = []
    for source in range(BLOCKS):
        if only is None or (source >> bit) % 2 == only:
            pairs.append((source, source ^ (1 << bit)))
    return lax.ppermute(value, "ctx", pairs)


def turn(value, bit):
    count = lax.axis_size("dp")
    return lax.ppermute(value, "dp", [(source, source ^ (1 << bit)) for source in range(count)])


def after(kernel, inputs):
    def body(row_ref, *refs):
        refs[inputs][...] = row_ref[...]
        kernel(*refs[:inputs], *refs[inputs + 1 :])

    return body


def part(value, start, count):
    return lax.dynamic_slice_in_dim(value, start, count, 0)


def bits_of(place):
    return [jnp.right_shift(place[0, 0], span) % 2 for span in range(SPANS)]


def fold(rows, bits, steps=(0, 5, 4, 3, 2, 1)):
    for step in steps:
        half = rows.shape[0] // 2
        other = swap(part(rows, (1 - bits[step]) * half, half), step)
        rows = part(rows, bits[step] * half, half) + other
    return rows


def per_device(inputs, matrix_b, matrix_c, steps_dt, decay_rate, skip_gain, level_weight, grad_out):
    xs, bs, cs, gs = inputs[0], matrix_b[0], matrix_c[0], grad_out[0]
    turned_dt, turned_w = steps_dt[0].T, level_weight.T
    place = lax.axis_index("ctx")
    core = place % 2
    bits = [jnp.right_shift(place, span) % 2 for span in range(SPANS)]
    rate = decay_rate.reshape(1, HEADS)
    core_here = core.astype(jnp.int32).reshape(1)
    vmem = pl.BlockSpec(memory_space=pltpu.VMEM)
    smem = pl.BlockSpec(memory_space=pltpu.SMEM)
    anywhere = pl.BlockSpec(memory_space=pl.ANY)

    def choose(bit, low, high):
        return jnp.where(bits[bit] == 1, high, low)

    def mine_of(value):
        return part(value, core * HALF, HALF)

    def yours_of(value):
        return part(value, (1 - core) * HALF, HALF)

    own_sum = jnp.sum(turned_dt, axis=1)[None]
    other = swap(own_sum, 0)
    sum_up = [choose(0, other, own_sum)]
    sum_in = [jnp.zeros_like(own_sum), choose(0, jnp.zeros_like(other), other)]
    there = choose(0, own_sum, -other)
    states, cum, dt4, row_first = call(
        state_kernel,
        (shaped(PAIRS, NST, 128), shaped(TOK, 128), shaped(TOK, 128), shaped(PAIRS, 128)),
        flops=2 * TOK * FEAT * 2 * NST,
        moved=2 << 20,
    )(xs, bs, turned_dt, rate, sum_up[0])
    first = swap(states, 0)
    group_sum, cot0, own, away, lam, sig = call(
        after(cot_kernel, 6),
        (
            shaped(1, HEADS),
            shaped(PAIRS, NST, 128),
            shaped(SPANS - 1, HALF, NST, 128),
            shaped(SPANS - 1, HALF, NST, 128),
            shaped(TOK, 512),
            shaped(TOK, 512),
        ),
        flops=2 * TOK * FEAT * (512 + 10 * NST),
        moved=10 << 20,
        specs=[vmem, smem] + [vmem] * 5,
    )(own_sum + other, core_here, xs, gs, cs, cum, turned_w)
    for span in range(1, SPANS - 1):
        other = swap(group_sum, span)
        sum_up.append(choose(span, other, group_sum))
        sum_in.append(sum_in[-1] + choose(span, jnp.zeros_like(other), other))
        group_sum = group_sum + other
    on = jnp.stack(bits).astype(F32)[:, None]
    sum_up, sum_in = jnp.concatenate(sum_up), jnp.concatenate(sum_in)
    rows_up, rows_own, rows_there, fade_in = call(
        rows_kernel,
        (
            shaped(SPANS - 2, PAIRS, 128),
            shaped(SPANS - 1, PAIRS, 128),
            shaped(SPANS - 1, PAIRS, 128),
            shaped(SPANS, HEADS),
        ),
    )(sum_up, sum_in, there, jnp.broadcast_to(on, (SPANS, HEADS)), rate)
    place_here = place.astype(jnp.int32).reshape(1)
    rows = (rows_up, rows_own, rows_there)
    slab = shaped(HALF, NST, 128)
    crossed = shaped(HALF, 128)

    mine, yours = mine_of(states), mine_of(first)
    row = mine_of(row_first)[:, None]
    lower0 = choose(0, mine, yours)
    held0 = lower0 * row + choose(0, yours, mine)
    came = swap(away, 0)
    level1 = swap(held0, 1)
    lower1, held1, send = one_step(
        step1_kernel, [slab] * 3, place_here, *rows, held0, level1, ("slab", 4, own), ("slab", 4, came)
    )
    level2, back4 = swap(held1, 2), swap(send, 5, 1)
    lower2, held2, send, keep = one_step(
        step2_kernel, [slab] * 4, place_here, *rows, held1, level2, ("slab", 3, own), ("slab", 3, came), back4
    )
    level3, back = swap(held2, 3), swap(send, 4)
    y_near, dx_near, db_near, dc_near, dl_near, gw_near, q_near, w_near, skip_sum = call(
        near_kernel,
        (
            shaped(TOK, FEAT),
            shaped(TOK, FEAT),
            shaped(TOK, NST),
            shaped(TOK, NST),
            shaped(TOK, 256, dtype=BF16),
            shaped(2, BLOCKS // 2, ROWS, 256),
            shaped(TOK, 128),
            shaped(TOK, 128),
            shaped(8, 128),
        ),
        scratch=(
            pltpu.VMEM((INTRA * TOK, TOK), BF16),
            pltpu.VMEM((INTRA * TOK, TOK), F32),
            pltpu.VMEM((2 * TOK, 128), F32),
        ),
        flops=2 * TOK * FEAT * (5 * INTRA * NST),
        moved=12 << 20,
        specs=[vmem] * 9 + [anywhere],
    )(xs, gs, bs, cs, dt4, skip_gain.reshape(1, HEADS), lam, sig, cum, send)
    _, held3, send, keep, crossed3, place3 = one_step(
        step3_kernel, [slab] * 4 + [crossed, shaped(1, 128, dtype=jnp.int32)], place_here, *rows, held2, level3,
        ("slab", 2, own), ("slab", 2, came), keep, back, ("after", w_near),
    )
    near_rows = fold(gw_near.reshape(FEAT, 256), bits_of(place3))
    level4, back = swap(held3, 4), swap(send, 3)
    held4, send, keep, crossed2, crossed4 = one_step(
        step4_kernel, [slab] * 3 + [crossed] * 2, place_here, *rows, held3, level4,
        ("slab", 1, own), ("slab", 1, came), keep, back, back4, lower2,
    )
    level5, back = swap(held4, 5, 0), swap(send, 2)
    across_near = swap(jnp.concatenate([level1, level2, level3]), 0)

    fade_t = jnp.exp(-cum)
    fade_far = fade_t[None] * jnp.concatenate([fade_in, jnp.zeros((2, HEADS), F32)]).reshape(2, 1, 128)
    y_far, dc_far, dl_far, w_far = call(
        far_kernel,
        (shaped(TOK, FEAT), shaped(TOK, NST), shaped(TOK, 128, dtype=BF16), shaped(TOK, 128)),
        scratch=[pltpu.VMEM((TOK, 128), F32)],
        flops=2 * TOK * FEAT * 16 * NST,
        moved=10 << 20,
        specs=[smem] + [vmem] * 13 + [anywhere],
    )(
        core_here, xs, gs, cs, lam, sig, fade_far[0], y_near, dc_near,
        first, level1, level2, level3, across_near, send,
    )
    send, keep, crossed1, both = one_step(
        step5_kernel, [slab] * 2 + [crossed, shaped(PAIRS, NST, 128)], place_here, *rows,
        ("slab", 0, own), ("slab", 0, came), keep, back, lower1, level4, level5, ("after", w_far),
    )
    back = swap(send, 1)
    across_far = swap(both, 0)
    output, grad_c, dl_line, gw_line, w_line = call(
        line_kernel,
        (
            shaped(TOK, FEAT, dtype=BF16),
            shaped(TOK, NST, dtype=BF16),
            shaped(TOK, 128, dtype=BF16),
            shaped(2, BLOCKS // 2, FOLD, 128),
            shaped(TOK, 128),
        ),
        scratch=[pltpu.VMEM((TOK, 128), F32), pltpu.VMEM((TOK, NST), F32)],
        flops=2 * TOK * FEAT * 10 * NST,
        moved=6 << 20,
        specs=[smem] + [vmem] * 12 + [anywhere],
    )(
        core_here, xs, gs, cs, lam, sig, fade_far[1], y_far, dc_far, dl_far,
        level4, level5, across_far, send,
    )
    going, crossed0 = one_step(
        step6_kernel, [shaped(HALF + PAIRS, NST, 128), crossed], place_here, row_first,
        keep, back, lower0, cot0, ("after", w_line),
    )
    last_came = swap(going, 0)
    lag = choose(0, row_first, jnp.ones_like(row_first))[:, None]
    fresh = choose(0, jnp.ones((1, 1, 128), F32), jnp.zeros((1, 1, 128), F32))
    late_place, grad_inputs, grad_b, ddt, rate_row = call(
        after(last_kernel, 20),
        (
            shaped(1, 128, dtype=jnp.int32),
            shaped(TOK, FEAT, dtype=BF16),
            shaped(TOK, NST, dtype=BF16),
            shaped(TOK, HEADS),
            shaped(1, 128),
        ),
        scratch=[pltpu.VMEM((TOK, NST), F32), pltpu.VMEM((TOK, 128), F32)],
        flops=2 * TOK * FEAT * 8 * NST,
        moved=10 << 20,
        specs=[vmem, smem] + [vmem] * 19,
    )(
        jnp.full((1, 128), place, jnp.int32), core_here, xs, bs, dt4, cum, rate, turned_w, going, last_came, lag, fresh,
        dx_near, db_near, dl_near, dl_far, dl_line, q_near, w_near, w_far, w_line,
    )

    rows = fold(gw_line.reshape(BLOCKS * FOLD, 128), bits, (0, 5))
    rows = fold(rows, bits_of(late_place), (4, 3, 2, 1))
    rows = jnp.concatenate([rows, near_rows.reshape(2 * ROWS, 128)])
    for step in range(2):
        rows = rows + turn(rows, step)
    near_rows = rows[FOLD:]

    queried = jnp.concatenate([jnp.sum(w_far, axis=0), jnp.sum(w_line, axis=0)]).reshape(8, HEADS)[:SPANS] * on
    halves = jnp.stack([crossed0, crossed1, crossed2, crossed3, crossed4, jnp.zeros_like(crossed0)])
    halves = jnp.sum(halves.reshape(SPANS, HEADS // 2, SIZE), axis=2)
    keyed = jnp.zeros((SPANS, 2, HEADS // 2), F32)
    keyed = lax.dynamic_update_slice_in_dim(keyed, halves[:, None], core, 1).reshape(SPANS, HEADS)
    inside = jnp.sum(sum_in * queried, axis=0) + jnp.sum(sum_up * keyed[: SPANS - 1], axis=0)
    extra = jnp.concatenate(
        [
            queried,
            keyed,
            (rate_row[0, :HEADS] - inside)[None],
            skip_sum[:1, :HEADS],
            jnp.zeros((2, HEADS), F32),
        ]
    )
    between = jnp.zeros((HEADS,), F32)
    for step in range(SPANS):
        came = swap(extra, step)
        if step + 1 < SPANS:
            later = jnp.sum(on[step + 1 :] * came[step + 1 : SPANS], axis=0)
            between = between + choose(step, later, jnp.zeros_like(later))
        extra = extra + came
        between = between + on[step] * extra[SPANS + step]
    ends = extra[2 * SPANS : 2 * SPANS + 2]
    for step in range(2):
        ends = ends + turn(ends, step)
    packed = rows[ROWS:FOLD]
    grad_level = jnp.concatenate(
        [
            near_rows.reshape(ROWS, 256),
            rows[:ROWS],
            jnp.concatenate([packed[:, :64], packed[:, 64:]], axis=0),
            jnp.zeros((ROWS, level_weight.shape[1] - 448), F32),
        ],
        axis=1,
    )
    grad_dt = (ddt - rate * between[None])[None]
    return (output[None], grad_inputs[None], grad_b[None], grad_c[None], grad_dt, ends[0], ends[1], grad_level)


def solution(mesh):
    split = P("dp", "ctx", None)
    return jax.shard_map(
        per_device,
        mesh=mesh,
        in_specs=(split, split, split, split, P(), P(), P(), split),
        out_specs=(split, split, split, split, split, P(), P(), P("ctx", None)),
        check_vma=False,
    )
```

```python
import jax
import jax.numpy as jnp
import numpy as np
from jax import lax
from jax.experimental import pallas as pl
from jax.experimental.pallas import tpu as pltpu
from jax.sharding import PartitionSpec as P

F32 = jnp.float32
BF16 = jnp.bfloat16
HIGHEST = lax.Precision.HIGHEST
HEADS = 32
SIZE = 64
TOK = 128
NST = 128
FEAT = HEADS * SIZE
INTRA = 8
SPANS = 6
USED = INTRA + SPANS
CHUNK = 256
CHUNKS = FEAT // CHUNK
PAIRS = FEAT // 128
HALF = PAIRS // 2
BLOCKS = 64
ROWS = FEAT // BLOCKS


def mm(a, b):
    return lax.dot_general(a, b, (((1,), (0,)), ((), ())), preferred_element_type=F32)


def mm_nt(a, b):
    return lax.dot_general(a, b, (((1,), (1,)), ((), ())), preferred_element_type=F32)


def mm_tn(a, b):
    return lax.dot_general(a, b, (((0,), (0,)), ((), ())), preferred_element_type=F32)


def onehot(chunk, quarter, rows=128):
    row = lax.broadcasted_iota(jnp.int32, (rows, CHUNK), 0)
    lane = lax.broadcasted_iota(jnp.int32, (rows, CHUNK), 1)
    if rows > 128:
        row = jnp.where(row >= 128, row - 128, row)
    head = chunk * (CHUNK // SIZE) + jnp.right_shift(lane, 6) + 32 * quarter
    return jnp.where(row == head, 1.0, 0.0).astype(BF16)


def split2(a):
    hi = a.astype(BF16)
    lo = (a - hi.astype(F32)).astype(BF16)
    return jnp.concatenate([hi, lo], axis=1)


def four(a):
    return jnp.concatenate([a, a, a, a], axis=1)


def sums_down():
    row = lax.broadcasted_iota(jnp.int32, (TOK, TOK), 0)
    col = lax.broadcasted_iota(jnp.int32, (TOK, TOK), 1)
    return jnp.where(row >= col, 1.0, 0.0).astype(F32)


def at_chunk(chunk):
    return pl.ds(pl.multiple_of(chunk * CHUNK, CHUNK), CHUNK)


def rows_of(per_head):
    pair = lax.broadcasted_iota(jnp.int32, (PAIRS, HEADS), 0)
    head = lax.broadcasted_iota(jnp.int32, (PAIRS, HEADS), 1)
    picked = jnp.where(jnp.right_shift(head, 1) == pair, per_head, 0.0)
    side = lax.broadcasted_iota(jnp.int32, (HEADS, 128), 0) % 2
    lane = lax.broadcasted_iota(jnp.int32, (HEADS, 128), 1)
    spread = jnp.where(side == jnp.right_shift(lane, 6), 1.0, 0.0).astype(F32)
    return lax.dot_general(
        picked, spread, (((1,), (0,)), ((), ())), precision=HIGHEST, preferred_element_type=F32
    )


def state_kernel(x_ref, b_ref, dt_ref, rate_ref, up_ref, u_ref, cum_ref, dt4_ref, row_ref):
    row_ref[...] = rows_of(jnp.exp(-up_ref[...] * rate_ref[...]))
    turned = dt_ref[...]
    dt4 = jnp.concatenate([turned, turned, turned, turned], axis=0).T
    cum = lax.dot_general(
        sums_down(), dt4 * four(rate_ref[...]), (((1,), (0,)), ((), ())),
        precision=HIGHEST, preferred_element_type=F32,
    )
    cum_ref[...] = cum
    dt4_ref[...] = dt4
    held = split2(jnp.exp(cum - cum[TOK - 1 : TOK]) * dt4)
    bmat = b_ref[...]

    @pl.loop(0, CHUNKS, unroll=CHUNKS)
    def _(chunk):
        xs = x_ref[:, at_chunk(chunk)].astype(F32)
        state = mm_tn(bmat, (xs * mm(held, onehot(chunk, 0, 256))).astype(BF16))
        for half in range(2):
            u_ref[2 * chunk + half] = state[:, 128 * half : 128 * half + 128]


def cot_kernel(
    core_ref, x_ref, g_ref, c_ref, cum_ref, w_ref, up_ref, in_ref, there_ref, on_ref, rate_ref,
    d0_ref, own_ref, away_ref, lam_ref, sig_ref, rows_up_ref, rows_own_ref, rows_there_ref, fade_ref,
):
    rate = rate_ref[...]
    fade_ref[...] = jnp.exp(-in_ref[...] * rate) * on_ref[...]
    for span in range(1, SPANS - 1):
        rows_up_ref[span - 1] = rows_of(jnp.exp(-up_ref[span : span + 1] * rate))
    for span in range(1, SPANS):
        on = on_ref[span : span + 1]
        rows_own_ref[span - 1] = rows_of(jnp.exp(-in_ref[span : span + 1] * rate) * on)
        rows_there_ref[span - 1] = rows_of(jnp.exp(-(in_ref[span : span + 1] + there_ref[...]) * rate) * on)
    fade = jnp.exp(-cum_ref[...])
    logit = mm_nt(x_ref[...], w_ref[:512])
    soft = jnp.maximum(logit, 0.0) + jnp.log1p(jnp.exp(-jnp.abs(logit)))
    lam_ref[...] = soft
    sig_ref[...] = 1.0 / (1.0 + jnp.exp(-logit))
    far = jnp.concatenate([split2(soft[:, 256:384] * fade), split2(soft[:, 384:512] * fade)], axis=0)
    cmat = c_ref[...]

    core = core_ref[0]

    def step(local, chunk, d_ref):
        gs = g_ref[:, at_chunk(chunk)].astype(F32)
        parts = [None] * SPANS
        for quarter in range(4):
            wide = mm(far if quarter < 2 else far[:TOK], onehot(chunk, quarter, 256))
            parts[quarter] = (wide[:TOK] * gs).astype(BF16)
            if quarter < 2:
                parts[4 + quarter] = (wide[TOK:] * gs).astype(BF16)
        cots = mm_tn(cmat, jnp.concatenate(parts, axis=1))
        for half in range(2):
            d0_ref[2 * chunk + half] = cots[:, 128 * half : 128 * half + 128]
            for span in range(1, SPANS):
                at = CHUNK * span + 128 * half
                d_ref[span - 1, 2 * local + half] = cots[:, at : at + 128]

    @pl.loop(0, CHUNKS // 2, unroll=CHUNKS // 2)
    def _(local):
        step(local, local + (1 - core) * (CHUNKS // 2), away_ref)

    @pl.loop(0, CHUNKS // 2, unroll=CHUNKS // 2)
    def _(local):
        step(local, local + core * (CHUNKS // 2), own_ref)


def near_kernel(
    place_ref, x_ref, g_ref, b_ref, c_ref, dt_ref, skip_ref, lam_ref, sig_ref, cum_ref, _after_ref,
    y_ref, dx_ref, db_ref, dc_ref, dl_ref, keep_ref, away_ref, q_ref, w_ref, sk_ref,
    kst_ref, dk_ref, da_ref,
):
    bmat = b_ref[...]
    cmat = c_ref[...]
    cum = cum_ref[...]
    fade = jnp.exp(-cum)
    score = mm_nt(cmat, bmat)
    row = lax.broadcasted_iota(jnp.int32, (TOK, TOK), 0)
    col = lax.broadcasted_iota(jnp.int32, (TOK, TOK), 1)
    apart = jnp.bitwise_xor(row, col)

    def mask_of(level):
        if level == 0:
            return row == col
        return (row > col) & (jnp.right_shift(apart, level - 1) == 1)

    for level in range(INTRA):
        kst_ref[level * TOK : (level + 1) * TOK] = jnp.where(mask_of(level), score, 0.0).astype(BF16)
    near = jnp.concatenate(
        [split2(lam_ref[:, :128] * fade), split2(lam_ref[:, 128:256] * fade)], axis=0
    )
    lift = split2(jnp.exp(cum) * dt_ref[...])
    gain = split2(jnp.broadcast_to(four(skip_ref[...]), (8, 128)))
    dk_ref[...] = jnp.zeros_like(dk_ref)
    da_ref[...] = jnp.zeros_like(da_ref)
    q_ref[...] = jnp.zeros_like(q_ref)
    sk_ref[...] = jnp.zeros_like(sk_ref)

    @pl.loop(0, CHUNKS, unroll=CHUNKS)
    def _(chunk):
        cols = at_chunk(chunk)
        xs = x_ref[:, cols].astype(F32)
        gs = g_ref[:, cols].astype(F32)
        spread0 = onehot(chunk, 0, 256)
        lifted = mm(lift, spread0)
        gains = mm(gain, spread0)[0:1]
        xd = (xs * lifted).astype(BF16)
        kst = kst_ref[...]
        mixed = mm(kst, xd)
        out = gains * xs
        parts = [None] * INTRA
        for quarter in range(4):
            wide = mm(near, onehot(chunk, quarter, 256))
            prods = []
            for part in range(2):
                level = 4 * part + quarter
                mult = wide[TOK * part : TOK * part + TOK]
                value = mixed[level * TOK : (level + 1) * TOK]
                out = out + mult * value
                prods.append((gs * value).astype(BF16))
                parts[level] = (mult * gs).astype(BF16)
            da_ref[...] += mm_nt(jnp.concatenate(prods, axis=0), onehot(chunk, quarter))
        y_ref[:, cols] = out
        agst = jnp.concatenate(parts, axis=0)
        dxd = mm_tn(kst, agst)
        dk_ref[...] += mm_nt(agst, xd)
        ones = onehot(chunk, 0)
        q_ref[...] += mm_nt((dxd * xs).astype(BF16), ones)
        dx_ref[:, cols] = dxd * lifted + gains * gs
        skrow = jnp.sum(xs * gs, axis=0, keepdims=True)
        sk_ref[...] += lax.dot_general(
            jnp.broadcast_to(skrow, (8, CHUNK)), ones.astype(F32), (((1,), (1,)), ((), ())),
            precision=HIGHEST, preferred_element_type=F32,
        )

    dscore = jnp.zeros((TOK, TOK), F32)
    for level in range(INTRA):
        dscore = dscore + jnp.where(mask_of(level), dk_ref[level * TOK : (level + 1) * TOK], 0.0)
    dscore = dscore.astype(BF16)
    dc_ref[...] = mm(dscore, bmat)
    db_ref[...] = mm_tn(dscore, cmat)
    dlam = []
    for part in range(2):
        da = da_ref[TOK * part : TOK * part + TOK]
        dlam.append(da * fade)
    w_ref[...] = dlam[0] * lam_ref[:, :128] + dlam[1] * lam_ref[:, 128:256]
    dlogit = (jnp.concatenate(dlam, axis=1) * sig_ref[:, :256]).astype(BF16)
    dl_ref[...] = dlogit
    second = bit_of(place_ref, 0) == 1
    for part in range(FEAT // 128):
        rows = mm_tn(x_ref[:, 128 * part : 128 * part + 128], dlogit)
        for pair in range(64 // ROWS):
            at = part * (64 // ROWS) + pair
            low, high = rows[64 * pair : 64 * pair + ROWS], rows[64 * pair + ROWS : 64 * pair + 64]
            keep, away = jnp.where(second, high, low), jnp.where(second, low, high)
            for side in range(2):
                keep_ref[at, ROWS * side : ROWS * side + ROWS] = keep[:, 128 * side : 128 * side + 128]
                away_ref[at, ROWS * side : ROWS * side + ROWS] = away[:, 128 * side : 128 * side + 128]


def spread_level(core_ref, x_ref, g_ref, c_ref, lam, fade_ref, y_ref, out_ref, dcs_ref, da_ref, levels, picked):
    cmat = c_ref[...]
    far = split2(lam * fade_ref[...])
    da_ref[...] = jnp.zeros_like(da_ref)
    core = core_ref[0]

    def step(local, chunk, mine):
        cols = at_chunk(chunk)
        gs = g_ref[:, cols].astype(F32)
        carried = jnp.concatenate([v.astype(BF16) for v in picked(chunk, local, mine)], axis=1)
        mixed = mm(cmat, carried)
        out = y_ref[:, cols]
        parts = []
        for quarter in range(levels):
            ones = onehot(chunk, quarter, 256)
            mult = mm(far, ones)
            value = mixed[:, CHUNK * quarter : CHUNK * quarter + CHUNK]
            out = out + mult * value
            da_ref[...] += mm_nt((gs * value).astype(BF16), ones[:128])
            parts.append((mult * gs).astype(BF16))
        out_ref[:, cols] = out.astype(out_ref.dtype)
        dcs_ref[...] += mm_nt(jnp.concatenate(parts, axis=1), carried)

    @pl.loop(0, CHUNKS // 2, unroll=CHUNKS // 2)
    def _(local):
        step(local, local + core * (CHUNKS // 2), True)

    @pl.loop(0, CHUNKS // 2, unroll=CHUNKS // 2)
    def _(local):
        step(local, local + (1 - core) * (CHUNKS // 2), False)

    return da_ref[...] * fade_ref[...]


def far_kernel(
    core_ref, x_ref, g_ref, c_ref, lam_ref, sig_ref, fade_ref, y_ref, dc_ref,
    first_ref, m1_ref, m2_ref, m3_ref, other_ref, _after_ref,
    out_ref, dcs_ref, dl_ref, w_ref,
    da_ref,
):
    lam = lam_ref[:, 256:384]
    dcs_ref[...] = dc_ref[...]

    def picked(chunk, local, mine):
        values = [first_ref[2 * chunk + half] for half in range(2)]
        for span, ref in enumerate((m1_ref, m2_ref, m3_ref)):
            for half in range(2):
                if mine:
                    values.append(ref[2 * local + half])
                else:
                    values.append(other_ref[span * (PAIRS // 2) + 2 * local + half])
        return values

    dlam = spread_level(
        core_ref, x_ref, g_ref, c_ref, lam, fade_ref, y_ref, out_ref, dcs_ref, da_ref, 4, picked
    )
    w_ref[...] = dlam * lam
    dl_ref[...] = (dlam * sig_ref[:, 256:384]).astype(BF16)


def line_kernel(
    core_ref, x_ref, g_ref, c_ref, lam_ref, sig_ref, fade_ref, y_ref, dc_ref, dl1_ref,
    m4_ref, m5_ref, other_ref, _after_ref,
    out_ref, dcout_ref, dl_ref, keep_ref, away_ref, w_ref,
    da_ref, dcs_ref,
):
    lam = lam_ref[:, 384:512]
    dcs_ref[...] = dc_ref[...]

    def picked(chunk, local, mine):
        values = []
        for span, ref in enumerate((m4_ref, m5_ref)):
            for half in range(2):
                if mine:
                    values.append(ref[2 * local + half])
                else:
                    values.append(other_ref[span * (PAIRS // 2) + 2 * local + half])
        return values

    dlam = spread_level(
        core_ref, x_ref, g_ref, c_ref, lam, fade_ref, y_ref, out_ref, dcs_ref, da_ref, 2, picked
    )
    dcout_ref[...] = dcs_ref[...].astype(BF16)
    w_ref[...] = dlam * lam
    dlogit = (dlam * sig_ref[:, 384:512]).astype(BF16)
    dl_ref[...] = dlogit
    both = jnp.concatenate([dl1_ref[...], dlogit], axis=1)
    lane = lax.broadcasted_iota(jnp.int32, (ROWS // 2, 128), 1)
    second = core_ref[0] == 1
    for part in range(FEAT // 128):
        rows = mm_tn(x_ref[:, 128 * part : 128 * part + 128], both)
        turned = pltpu.roll(rows[:, 128:], 64, 1)

        def packed(top):
            mid = top + ROWS // 2
            return jnp.where(lane < 64, rows[top:mid, 128:], turned[mid : mid + ROWS // 2])

        for pair in range(64 // ROWS):
            at = part * (64 // ROWS) + pair
            low, high = rows[64 * pair : 64 * pair + ROWS, :128], rows[64 * pair + ROWS : 64 * pair + 64, :128]
            keep_ref[at, :ROWS], away_ref[at, :ROWS] = jnp.where(second, high, low), jnp.where(second, low, high)
            low, high = packed(64 * pair), packed(64 * pair + ROWS)
            keep_ref[at, ROWS:], away_ref[at, ROWS:] = jnp.where(second, high, low), jnp.where(second, low, high)


def last_kernel(
    place_ref, x_ref, b_ref, dt_ref, cum_ref, rate_ref, w_ref, mine_ref, came_ref, lag_ref, fresh_ref, dx_ref, db_ref,
    dl0_ref, dl1_ref, dl2_ref, q_ref, w0_ref, w1_ref, w2_ref, far_ref, far_came_ref,
    dxout_ref, dbout_ref, ddt_ref, rate_out_ref, far_keep_ref, far_away_ref,
    dbs_ref, q2_ref,
):
    halve(bit_of(place_ref, 5), far_ref, far_came_ref, far_keep_ref, far_away_ref)
    bmat = b_ref[...]
    cum = cum_ref[...]
    dt4 = dt_ref[...]
    left = jnp.exp(cum - cum[TOK - 1 : TOK])
    held = split2(left * dt4)
    dlogit = jnp.concatenate([dl0_ref[...], dl1_ref[...], dl2_ref[...]], axis=1)
    q2_ref[...] = jnp.zeros_like(q2_ref)
    dbs_ref[...] = db_ref[...]

    core = bit_of(place_ref, 0)

    def step(local, chunk, source):
        cols = at_chunk(chunk)
        xs = x_ref[:, cols].astype(F32)
        spread = mm(held, onehot(chunk, 0, 256))
        du = jnp.concatenate(
            [
                (
                    source[2 * local + half] * lag_ref[2 * chunk + half]
                    + came_ref[PAIRS // 2 + 2 * chunk + half] * fresh_ref[0]
                ).astype(BF16)
                for half in range(2)
            ],
            axis=1,
        )
        dxs = mm(bmat, du)
        q2_ref[...] += mm_nt((dxs * xs).astype(BF16), onehot(chunk, 0))
        dbs_ref[...] += mm_nt((xs * spread).astype(BF16), du)
        dx = dx_ref[:, cols] + dxs * spread + mm(dlogit, w_ref[:512, cols])
        dxout_ref[:, cols] = dx.astype(BF16)

    @pl.loop(0, CHUNKS // 2, unroll=CHUNKS // 2)
    def _(local):
        step(local, local + core * (CHUNKS // 2), mine_ref)

    @pl.loop(0, CHUNKS // 2, unroll=CHUNKS // 2)
    def _(local):
        step(local, local + (1 - core) * (CHUNKS // 2), came_ref)

    dbout_ref[...] = dbs_ref[...].astype(BF16)
    q2 = q2_ref[...]
    q1 = q_ref[...]
    lift = jnp.exp(cum)
    gathered = w0_ref[...] + w1_ref[...] + w2_ref[...]
    queried = gathered + pltpu.roll(gathered, 32, 1)
    queried = queried + pltpu.roll(queried, 64, 1)
    keyed2 = q2 * left * dt4
    dcum = q1 * lift * dt4 + keyed2 - queried
    dlog = lax.dot_general(
        sums_down(), dcum, (((0,), (0,)), ((), ())), precision=HIGHEST, preferred_element_type=F32
    )
    dlog = dlog - jnp.sum(keyed2, axis=0, keepdims=True)
    ddt_ref[...] = rate_ref[...] * dlog[:, :32] + (q1 * lift + q2 * left)[:, :32]
    rate_out_ref[...] = jnp.sum(dt4 * dlog, axis=0, keepdims=True)


def bit_of(place_ref, span):
    return jnp.right_shift(place_ref[0], span) % 2


def half_of(rows_ref, index, place_ref):
    return rows_ref[index, pl.ds(pl.multiple_of(bit_of(place_ref, 0) * HALF, HALF), HALF), :]


def up_step(span, place_ref, held_ref, other_ref, rows_ref, lower_ref, next_ref):
    upper = bit_of(place_ref, span) == 1
    rows = half_of(rows_ref, span - 1, place_ref)
    for pair in range(HALF):
        mine, other = held_ref[pair], other_ref[pair]
        lower = jnp.where(upper, other, mine)
        lower_ref[pair] = lower
        next_ref[pair] = lower * rows[pair : pair + 1] + jnp.where(upper, mine, other)


def level_of(span, place_ref, own_ref, came_ref, rows_own_ref, rows_there_ref):
    rows_own = half_of(rows_own_ref, span - 1, place_ref)
    rows_there = half_of(rows_there_ref, span - 1, place_ref)

    def piece(pair):
        return own_ref[0, pair] * rows_own[pair : pair + 1] + came_ref[0, pair] * rows_there[pair : pair + 1]

    return piece


def down_step(span, place_ref, grad, piece, rows_ref, send_ref, keep_ref, crossed_ref=None, lower_ref=None):
    upper = bit_of(place_ref, span) == 1
    rows = half_of(rows_ref, span - 1, place_ref)
    for pair in range(HALF):
        here = grad(pair)
        faded = here * rows[pair : pair + 1]
        send_ref[pair] = jnp.where(upper, faded + piece(pair), here)
        keep_ref[pair] = jnp.where(upper, here, faded)
        if crossed_ref is not None:
            crossed_ref[pair : pair + 1] = jnp.sum(lower_ref[pair] * faded, axis=0, keepdims=True)


def halve(bit, keep_ref, came_ref, keep_out_ref, away_out_ref):
    half = keep_out_ref.shape[0]
    for block in range(half):
        stay, go = bit * half + block, (1 - bit) * half + block
        keep_out_ref[block] = keep_ref[stay] + came_ref[stay]
        away_out_ref[block] = keep_ref[go] + came_ref[go]


def step1_kernel(place_ref, rows_ref, rows_own_ref, rows_there_ref, held_ref, other_ref, own_ref, came_ref, lower_ref, next_ref, send_ref):
    up_step(1, place_ref, held_ref, other_ref, rows_ref, lower_ref, next_ref)
    piece = level_of(5, place_ref, own_ref, came_ref, rows_own_ref, rows_there_ref)
    for pair in range(HALF):
        send_ref[pair] = piece(pair)


def step2_kernel(place_ref, rows_ref, rows_own_ref, rows_there_ref, held_ref, other_ref, own_ref, came_ref, back_ref, lower_ref, next_ref, send_ref, keep_ref):
    up_step(2, place_ref, held_ref, other_ref, rows_ref, lower_ref, next_ref)
    piece = level_of(4, place_ref, own_ref, came_ref, rows_own_ref, rows_there_ref)
    down_step(4, place_ref, lambda pair: back_ref[pair], piece, rows_ref, send_ref, keep_ref)


def step3_kernel(place_ref, rows_ref, rows_own_ref, rows_there_ref, held_ref, other_ref, own_ref, came_ref, kept_ref, back_ref, near_ref, level1_ref, level2_ref, lower_ref, next_ref, send_ref, keep_ref, crossed_ref, near_away_ref, levels_ref):
    near_away_ref[...] = near_ref[...]
    for index, level_ref in enumerate((level1_ref, level2_ref, other_ref)):
        for pair in range(HALF):
            levels_ref[index * HALF + pair] = level_ref[pair]
    up_step(3, place_ref, held_ref, other_ref, rows_ref, lower_ref, next_ref)
    piece = level_of(3, place_ref, own_ref, came_ref, rows_own_ref, rows_there_ref)
    down_step(3, place_ref, lambda pair: kept_ref[pair] + back_ref[pair], piece, rows_ref, send_ref, keep_ref, crossed_ref, lower_ref)


def step4_kernel(place_ref, rows_ref, rows_own_ref, rows_there_ref, held_ref, other_ref, own_ref, came_ref, kept_ref, back_ref, first_ref, lower2_ref, near_ref, near_came_ref, next_ref, send_ref, keep_ref, crossed_ref, crossed4_ref, near_keep_ref, near_away_ref):
    halve(bit_of(place_ref, 5), near_ref, near_came_ref, near_keep_ref, near_away_ref)
    upper = bit_of(place_ref, 4) == 1
    rows = half_of(rows_ref, 3, place_ref)
    for pair in range(HALF):
        mine, other = held_ref[pair], other_ref[pair]
        faded = jnp.where(upper, other, mine) * rows[pair : pair + 1]
        next_ref[pair] = faded + jnp.where(upper, mine, other)
        crossed4_ref[pair : pair + 1] = jnp.sum(faded * first_ref[pair], axis=0, keepdims=True)
    piece = level_of(2, place_ref, own_ref, came_ref, rows_own_ref, rows_there_ref)
    down_step(2, place_ref, lambda pair: kept_ref[pair] + back_ref[pair], piece, rows_ref, send_ref, keep_ref, crossed_ref, lower2_ref)


def step5_kernel(place_ref, rows_ref, rows_own_ref, rows_there_ref, own_ref, came_ref, kept_ref, back_ref, lower1_ref, level4_ref, level5_ref, near_ref, near_came_ref, _after_ref, send_ref, keep_ref, crossed_ref, both_ref, near_keep_ref, near_away_ref):
    halve(bit_of(place_ref, 4), near_ref, near_came_ref, near_keep_ref, near_away_ref)
    for pair in range(HALF):
        both_ref[pair] = level4_ref[pair]
        both_ref[HALF + pair] = level5_ref[pair]
    piece = level_of(1, place_ref, own_ref, came_ref, rows_own_ref, rows_there_ref)
    down_step(1, place_ref, lambda pair: kept_ref[pair] + back_ref[pair], piece, rows_ref, send_ref, keep_ref, crossed_ref, lower1_ref)


def step6_kernel(place_ref, row_ref, kept_ref, back_ref, lower0_ref, cot_ref, near_ref, near_came_ref, _after_ref, send_ref, crossed_ref, near_out_ref):
    near_out_ref[...] = near_ref[...] + near_came_ref[...]
    rows = row_ref[pl.ds(pl.multiple_of(bit_of(place_ref, 0) * HALF, HALF), HALF), :]
    upper = bit_of(place_ref, 0) == 1
    for pair in range(HALF):
        grad = kept_ref[pair] + back_ref[pair]
        send_ref[pair] = grad
        crossed_ref[pair : pair + 1] = jnp.sum(lower0_ref[pair] * rows[pair : pair + 1] * grad, axis=0, keepdims=True)
    for pair in range(PAIRS):
        send_ref[HALF + pair] = jnp.where(upper, cot_ref[pair], 0.0)


VMEM_LIMIT = 56 * 1024 * 1024
FOLD = ROWS + ROWS // 2


def call(kernel, outs, scratch=(), flops=0, moved=1 << 20, specs=None):
    extra = {} if specs is None else {"in_specs": specs}
    return pl.pallas_call(
        kernel,
        out_shape=outs,
        scratch_shapes=list(scratch),
        compiler_params=pltpu.CompilerParams(vmem_limit_bytes=VMEM_LIMIT),
        cost_estimate=pl.CostEstimate(flops=flops, bytes_accessed=moved, transcendentals=0),
        **extra,
    )


def one_step(kernel, outs, *operands):
    specs, arrays = [pl.BlockSpec(memory_space=pltpu.SMEM)], [operands[0]]
    for operand in operands[1:]:
        if not isinstance(operand, tuple):
            arrays.append(operand)
            specs.append(pl.BlockSpec(operand.shape, lambda _, rank=operand.ndim: (0,) * rank))
        elif operand[0] == "slab":
            arrays.append(operand[2])
            specs.append(pl.BlockSpec((1,) + operand[2].shape[1:], lambda _, at=operand[1]: (at, 0, 0, 0)))
        else:
            arrays.append(operand[1])
            specs.append(pl.BlockSpec(memory_space=pl.ANY))
    return pl.pallas_call(
        kernel,
        grid=(1,),
        out_shape=tuple(outs),
        in_specs=specs,
        out_specs=tuple(pl.BlockSpec(out.shape, lambda _, rank=len(out.shape): (0,) * rank) for out in outs),
        compiler_params=pltpu.CompilerParams(vmem_limit_bytes=VMEM_LIMIT),
        cost_estimate=pl.CostEstimate(flops=1 << 22, bytes_accessed=4 << 20, transcendentals=0),
    )(*arrays)


def shaped(*dims, dtype=F32):
    return jax.ShapeDtypeStruct(dims, dtype)


def swap(value, bit, only=None):
    pairs = []
    for source in range(BLOCKS):
        if only is None or (source >> bit) % 2 == only:
            pairs.append((source, source ^ (1 << bit)))
    return lax.ppermute(value, "ctx", pairs)


def turn(value, bit):
    count = lax.axis_size("dp")
    return lax.ppermute(value, "dp", [(source, source ^ (1 << bit)) for source in range(count)])


def part(value, start, count):
    return lax.dynamic_slice_in_dim(value, start, count, 0)


def per_device(inputs, matrix_b, matrix_c, steps_dt, decay_rate, skip_gain, level_weight, grad_out):
    xs, bs, cs, gs = inputs[0], matrix_b[0], matrix_c[0], grad_out[0]
    turned_dt, turned_w = steps_dt[0].T, level_weight.T
    place = lax.axis_index("ctx")
    core = place % 2
    bits = [jnp.right_shift(place, span) % 2 for span in range(SPANS)]
    rate = decay_rate.reshape(1, HEADS)
    core_here = core.astype(jnp.int32).reshape(1)
    vmem = pl.BlockSpec(memory_space=pltpu.VMEM)
    smem = pl.BlockSpec(memory_space=pltpu.SMEM)
    anywhere = pl.BlockSpec(memory_space=pl.ANY)

    def choose(bit, low, high):
        return jnp.where(bits[bit] == 1, high, low)

    def mine_of(value):
        return part(value, core * HALF, HALF)

    def yours_of(value):
        return part(value, (1 - core) * HALF, HALF)

    own_sum = jnp.sum(turned_dt, axis=1)[None]
    other = swap(own_sum, 0)
    sum_up = [choose(0, other, own_sum)]
    sum_in = [jnp.zeros_like(own_sum), choose(0, jnp.zeros_like(other), other)]
    there = choose(0, own_sum, -other)
    states, cum, dt4, row_first = call(
        state_kernel,
        (shaped(PAIRS, NST, 128), shaped(TOK, 128), shaped(TOK, 128), shaped(PAIRS, 128)),
        flops=2 * TOK * FEAT * 2 * NST,
        moved=2 << 20,
    )(xs, bs, turned_dt, rate, sum_up[0])
    first = swap(states, 0)
    group_sum = own_sum + other
    for span in range(1, SPANS - 1):
        other = swap(group_sum, span)
        sum_up.append(choose(span, other, group_sum))
        sum_in.append(sum_in[-1] + choose(span, jnp.zeros_like(other), other))
        group_sum = group_sum + other
    on = jnp.stack(bits).astype(F32)[:, None]
    sum_up, sum_in = jnp.concatenate(sum_up), jnp.concatenate(sum_in)
    cot0, own, away, lam, sig, rows_up, rows_own, rows_there, fade_in = call(
        cot_kernel,
        (
            shaped(PAIRS, NST, 128),
            shaped(SPANS - 1, HALF, NST, 128),
            shaped(SPANS - 1, HALF, NST, 128),
            shaped(TOK, 512),
            shaped(TOK, 512),
            shaped(SPANS - 2, PAIRS, 128),
            shaped(SPANS - 1, PAIRS, 128),
            shaped(SPANS - 1, PAIRS, 128),
            shaped(SPANS, HEADS),
        ),
        flops=2 * TOK * FEAT * (512 + 10 * NST),
        moved=10 << 20,
        specs=[smem] + [vmem] * 10,
    )(core_here, xs, gs, cs, cum, turned_w, sum_up, sum_in, there, jnp.broadcast_to(on, (SPANS, HEADS)), rate)
    place_here = place.astype(jnp.int32).reshape(1)
    rows = (rows_up, rows_own, rows_there)
    slab = shaped(HALF, NST, 128)
    crossed = shaped(HALF, 128)

    mine, yours = mine_of(states), mine_of(first)
    row = mine_of(row_first)[:, None]
    lower0 = choose(0, mine, yours)
    held0 = lower0 * row + choose(0, yours, mine)
    came = swap(away, 0)
    level1 = swap(held0, 1)
    lower1, held1, send = one_step(
        step1_kernel, [slab] * 3, place_here, *rows, held0, level1, ("slab", 4, own), ("slab", 4, came)
    )
    level2, back4 = swap(held1, 2), swap(send, 5, 1)
    lower2, held2, send, keep = one_step(
        step2_kernel, [slab] * 4, place_here, *rows, held1, level2, ("slab", 3, own), ("slab", 3, came), back4
    )
    level3, back = swap(held2, 3), swap(send, 4)
    y_near, dx_near, db_near, dc_near, dl_near, near_keep, near_away, q_near, w_near, skip_sum = call(
        near_kernel,
        (
            shaped(TOK, FEAT),
            shaped(TOK, FEAT),
            shaped(TOK, NST),
            shaped(TOK, NST),
            shaped(TOK, 256, dtype=BF16),
            shaped(BLOCKS // 2, 2 * ROWS, 128),
            shaped(BLOCKS // 2, 2 * ROWS, 128),
            shaped(TOK, 128),
            shaped(TOK, 128),
            shaped(8, 128),
        ),
        scratch=(
            pltpu.VMEM((INTRA * TOK, TOK), BF16),
            pltpu.VMEM((INTRA * TOK, TOK), F32),
            pltpu.VMEM((2 * TOK, 128), F32),
        ),
        flops=2 * TOK * FEAT * (5 * INTRA * NST),
        moved=12 << 20,
        specs=[smem] + [vmem] * 9 + [anywhere],
    )(place_here, xs, gs, bs, cs, dt4, skip_gain.reshape(1, HEADS), lam, sig, cum, send)
    _, held3, send, keep, crossed3, near_away, levels = one_step(
        step3_kernel,
        [slab] * 4 + [crossed, shaped(BLOCKS // 2, 2 * ROWS, 128), shaped(3 * HALF, NST, 128)],
        place_here, *rows, held2, level3,
        ("slab", 2, own), ("slab", 2, came), keep, back, near_away, level1, level2,
    )
    near_came = swap(near_away, 0)
    level4, back = swap(held3, 4), swap(send, 3)
    held4, send, keep, crossed2, crossed4, near_keep, near_away = one_step(
        step4_kernel, [slab] * 3 + [crossed] * 2 + [shaped(16, 2 * ROWS, 128)] * 2, place_here, *rows, held3, level4,
        ("slab", 1, own), ("slab", 1, came), keep, back, back4, lower2, near_keep, near_came,
    )
    near_came = swap(near_away, 5)
    level5, back = swap(held4, 5, 0), swap(send, 2)
    across_near = swap(levels, 0)

    fade_t = jnp.exp(-cum)
    fade_far = fade_t[None] * jnp.concatenate([fade_in, jnp.zeros((2, HEADS), F32)]).reshape(2, 1, 128)
    y_far, dc_far, dl_far, w_far = call(
        far_kernel,
        (shaped(TOK, FEAT), shaped(TOK, NST), shaped(TOK, 128, dtype=BF16), shaped(TOK, 128)),
        scratch=[pltpu.VMEM((TOK, 128), F32)],
        flops=2 * TOK * FEAT * 16 * NST,
        moved=10 << 20,
        specs=[smem] + [vmem] * 13 + [anywhere],
    )(
        core_here, xs, gs, cs, lam, sig, fade_far[0], y_near, dc_near,
        first, level1, level2, level3, across_near, send,
    )
    send, keep, crossed1, both, near_keep, near_away = one_step(
        step5_kernel, [slab] * 2 + [crossed, shaped(PAIRS, NST, 128)] + [shaped(8, 2 * ROWS, 128)] * 2, place_here, *rows,
        ("slab", 0, own), ("slab", 0, came), keep, back, lower1, level4, level5, near_keep, near_came, ("after", w_far),
    )
    near_came = swap(near_away, 4)
    back = swap(send, 1)
    across_far = swap(both, 0)
    output, grad_c, dl_line, far_keep, far_away, w_line = call(
        line_kernel,
        (
            shaped(TOK, FEAT, dtype=BF16),
            shaped(TOK, NST, dtype=BF16),
            shaped(TOK, 128, dtype=BF16),
            shaped(BLOCKS // 2, FOLD, 128),
            shaped(BLOCKS // 2, FOLD, 128),
            shaped(TOK, 128),
        ),
        scratch=[pltpu.VMEM((TOK, 128), F32), pltpu.VMEM((TOK, NST), F32)],
        flops=2 * TOK * FEAT * 10 * NST,
        moved=6 << 20,
        specs=[smem] + [vmem] * 12 + [anywhere],
    )(
        core_here, xs, gs, cs, lam, sig, fade_far[1], y_far, dc_far, dl_far,
        level4, level5, across_far, send,
    )
    far_came = swap(far_away, 0)
    going, crossed0, near_rows = one_step(
        step6_kernel,
        [shaped(HALF + PAIRS, NST, 128), crossed, shaped(8, 2 * ROWS, 128)],
        place_here, row_first,
        keep, back, lower0, cot0, near_keep, near_came, ("after", w_line),
    )
    last_came = swap(going, 0)
    lag = choose(0, row_first, jnp.ones_like(row_first))[:, None]
    fresh = choose(0, jnp.ones((1, 1, 128), F32), jnp.zeros((1, 1, 128), F32))
    grad_inputs, grad_b, ddt, rate_row, far_keep, far_away = call(
        last_kernel,
        (
            shaped(TOK, FEAT, dtype=BF16),
            shaped(TOK, NST, dtype=BF16),
            shaped(TOK, HEADS),
            shaped(1, 128),
            shaped(16, FOLD, 128),
            shaped(16, FOLD, 128),
        ),
        scratch=[pltpu.VMEM((TOK, NST), F32), pltpu.VMEM((TOK, 128), F32)],
        flops=2 * TOK * FEAT * 8 * NST,
        moved=10 << 20,
        specs=[smem] + [vmem] * 21,
    )(
        place_here, xs, bs, dt4, cum, rate, turned_w, going, last_came, lag, fresh,
        dx_near, db_near, dl_near, dl_far, dl_line, q_near, w_near, w_far, w_line, far_keep, far_came,
    )
    far_came = swap(far_away, 5)

    queried = jnp.concatenate([jnp.sum(w_far, axis=0), jnp.sum(w_line, axis=0)]).reshape(8, HEADS)[:SPANS] * on
    halves = jnp.stack([crossed0, crossed1, crossed2, crossed3, crossed4, jnp.zeros_like(crossed0)])
    halves = jnp.sum(halves.reshape(SPANS, HEADS // 2, SIZE), axis=2)
    keyed = jnp.zeros((SPANS, 2, HEADS // 2), F32)
    keyed = lax.dynamic_update_slice_in_dim(keyed, halves[:, None], core, 1).reshape(SPANS, HEADS)
    inside = jnp.sum(sum_in * queried, axis=0) + jnp.sum(sum_up * keyed[: SPANS - 1], axis=0)
    extra = jnp.concatenate(
        [
            queried,
            keyed,
            (rate_row[0, :HEADS] - inside)[None],
            skip_sum[:1, :HEADS],
            jnp.zeros((2, HEADS), F32),
        ]
    )
    extra = extra.reshape(4, 128)
    far_rows = None
    between = jnp.zeros((HEADS,), F32)
    for step in range(SPANS):
        sent, keep = [extra], []
        if step == 1:
            far_rows = far_keep + far_came
        if 1 <= step <= 4:
            for rows in (far_rows, near_rows) if step <= 3 else (far_rows,):
                split = rows.reshape(rows.shape[0] // 2, 2, rows.shape[1], 128)
                keep.append(lax.dynamic_index_in_dim(split, bits[step], 1, keepdims=False))
                sent.append(lax.dynamic_index_in_dim(split, 1 - bits[step], 1, keepdims=False).reshape(-1, 128))
        came = swap(jnp.concatenate(sent), step)
        at = 4
        added = []
        for rows in keep:
            size = rows.shape[0] * rows.shape[1]
            added.append(rows + came[at : at + size].reshape(rows.shape))
            at += size
        if added:
            far_rows = added[0]
            near_rows = added[1] if len(added) > 1 else near_rows
        told = came[:4].reshape(16, HEADS)
        if step + 1 < SPANS:
            later = jnp.sum(on[step + 1 :] * told[step + 1 : SPANS], axis=0)
            between = between + choose(step, later, jnp.zeros_like(later))
        extra = extra + came[:4]
        between = between + on[step] * extra.reshape(16, HEADS)[SPANS + step]
    total = jnp.concatenate([extra, far_rows[0], near_rows[0]])
    for step in range(2):
        total = total + turn(total, step)
    ends = total[3].reshape(4, HEADS)
    rows, near_rows = total[4 : 4 + FOLD], total[4 + FOLD :]
    packed = rows[ROWS:FOLD]
    grad_level = jnp.concatenate(
        [
            near_rows[:ROWS],
            near_rows[ROWS:],
            rows[:ROWS],
            jnp.concatenate([packed[:, :64], packed[:, 64:]], axis=0),
            jnp.zeros((ROWS, level_weight.shape[1] - 448), F32),
        ],
        axis=1,
    )
    grad_dt = (ddt - rate * between[None])[None]
    return (output[None], grad_inputs[None], grad_b[None], grad_c[None], grad_dt, ends[0], ends[1], grad_level)


def solution(mesh):
    split = P("dp", "ctx", None)
    return jax.shard_map(
        per_device,
        mesh=mesh,
        in_specs=(split, split, split, split, P(), P(), P(), split),
        out_specs=(split, split, split, split, split, P(), P(), P("ctx", None)),
        check_vma=False,
    )
```

```python
import jax
import jax.numpy as jnp
import numpy as np
from jax import lax
from jax.experimental import pallas as pl
from jax.experimental.pallas import tpu as pltpu
from jax.sharding import PartitionSpec as P

F32 = jnp.float32
BF16 = jnp.bfloat16
HIGHEST = lax.Precision.HIGHEST
HEADS = 32
SIZE = 64
TOK = 128
NST = 128
FEAT = HEADS * SIZE
INTRA = 8
SPANS = 6
USED = INTRA + SPANS
CHUNK = 256
CHUNKS = FEAT // CHUNK
PAIRS = FEAT // 128
HALF = PAIRS // 2
BLOCKS = 64
ROWS = FEAT // BLOCKS


def mm(a, b):
    return lax.dot_general(a, b, (((1,), (0,)), ((), ())), preferred_element_type=F32)


def mm_nt(a, b):
    return lax.dot_general(a, b, (((1,), (1,)), ((), ())), preferred_element_type=F32)


def mm_tn(a, b):
    return lax.dot_general(a, b, (((0,), (0,)), ((), ())), preferred_element_type=F32)


def onehot(chunk, quarter, rows=128):
    row = lax.broadcasted_iota(jnp.int32, (rows, CHUNK), 0)
    lane = lax.broadcasted_iota(jnp.int32, (rows, CHUNK), 1)
    if rows > 128:
        row = jnp.where(row >= 128, row - 128, row)
    head = chunk * (CHUNK // SIZE) + jnp.right_shift(lane, 6) + 32 * quarter
    return jnp.where(row == head, 1.0, 0.0).astype(BF16)


def split2(a):
    hi = a.astype(BF16)
    lo = (a - hi.astype(F32)).astype(BF16)
    return jnp.concatenate([hi, lo], axis=1)


def four(a):
    return jnp.concatenate([a, a, a, a], axis=1)


def sums_down():
    row = lax.broadcasted_iota(jnp.int32, (TOK, TOK), 0)
    col = lax.broadcasted_iota(jnp.int32, (TOK, TOK), 1)
    return jnp.where(row >= col, 1.0, 0.0).astype(F32)


def at_chunk(chunk):
    return pl.ds(pl.multiple_of(chunk * CHUNK, CHUNK), CHUNK)


def rows_of(per_head):
    pair = lax.broadcasted_iota(jnp.int32, (PAIRS, HEADS), 0)
    head = lax.broadcasted_iota(jnp.int32, (PAIRS, HEADS), 1)
    picked = jnp.where(jnp.right_shift(head, 1) == pair, per_head, 0.0)
    side = lax.broadcasted_iota(jnp.int32, (HEADS, 128), 0) % 2
    lane = lax.broadcasted_iota(jnp.int32, (HEADS, 128), 1)
    spread = jnp.where(side == jnp.right_shift(lane, 6), 1.0, 0.0).astype(F32)
    return lax.dot_general(
        picked, spread, (((1,), (0,)), ((), ())), precision=HIGHEST, preferred_element_type=F32
    )


def sum_kernel(own_ref, other_ref, row_ref, _first_ref, _second_ref, out_ref, row_out_ref):
    out_ref[...] = own_ref[...] + other_ref[...]
    row_out_ref[...] = row_ref[...]


def state_kernel(x_ref, b_ref, dt_ref, rate_ref, up_ref, u_ref, cum_ref, dt4_ref, row_ref):
    row_ref[...] = rows_of(jnp.exp(-up_ref[...] * rate_ref[...]))
    turned = dt_ref[...]
    dt4 = jnp.concatenate([turned, turned, turned, turned], axis=0).T
    cum = lax.dot_general(
        sums_down(), dt4 * four(rate_ref[...]), (((1,), (0,)), ((), ())),
        precision=HIGHEST, preferred_element_type=F32,
    )
    cum_ref[...] = cum
    dt4_ref[...] = dt4
    held = split2(jnp.exp(cum - cum[TOK - 1 : TOK]) * dt4)
    bmat = b_ref[...]

    @pl.loop(0, CHUNKS, unroll=CHUNKS)
    def _(chunk):
        xs = x_ref[:, at_chunk(chunk)].astype(F32)
        state = mm_tn(bmat, (xs * mm(held, onehot(chunk, 0, 256))).astype(BF16))
        for half in range(2):
            u_ref[2 * chunk + half] = state[:, 128 * half : 128 * half + 128]


def rows_kernel(up_ref, in_ref, there_ref, on_ref, rate_ref, rows_up_ref, rows_own_ref, rows_there_ref, fade_ref):
    rate = rate_ref[...]
    fade_ref[...] = jnp.exp(-in_ref[...] * rate) * on_ref[...]
    for span in range(1, SPANS - 1):
        rows_up_ref[span - 1] = rows_of(jnp.exp(-up_ref[span : span + 1] * rate))
    for span in range(1, SPANS):
        on = on_ref[span : span + 1]
        rows_own_ref[span - 1] = rows_of(jnp.exp(-in_ref[span : span + 1] * rate) * on)
        rows_there_ref[span - 1] = rows_of(jnp.exp(-(in_ref[span : span + 1] + there_ref[...]) * rate) * on)


def cot_kernel(core_ref, x_ref, g_ref, c_ref, cum_ref, w_ref, _after_ref, d0_ref, own_ref, away_ref, lam_ref, sig_ref):
    fade = jnp.exp(-cum_ref[...])
    logit = mm_nt(x_ref[...], w_ref[:512])
    soft = jnp.maximum(logit, 0.0) + jnp.log1p(jnp.exp(-jnp.abs(logit)))
    lam_ref[...] = soft
    sig_ref[...] = 1.0 / (1.0 + jnp.exp(-logit))
    far = jnp.concatenate([split2(soft[:, 256:384] * fade), split2(soft[:, 384:512] * fade)], axis=0)
    cmat = c_ref[...]

    core = core_ref[0]

    def step(local, chunk, d_ref):
        gs = g_ref[:, at_chunk(chunk)].astype(F32)
        parts = [None] * SPANS
        for quarter in range(4):
            wide = mm(far if quarter < 2 else far[:TOK], onehot(chunk, quarter, 256))
            parts[quarter] = (wide[:TOK] * gs).astype(BF16)
            if quarter < 2:
                parts[4 + quarter] = (wide[TOK:] * gs).astype(BF16)
        cots = mm_tn(cmat, jnp.concatenate(parts, axis=1))
        for half in range(2):
            d0_ref[2 * chunk + half] = cots[:, 128 * half : 128 * half + 128]
            for span in range(1, SPANS):
                at = CHUNK * span + 128 * half
                d_ref[span - 1, 2 * local + half] = cots[:, at : at + 128]

    @pl.loop(0, CHUNKS // 2, unroll=CHUNKS // 2)
    def _(local):
        step(local, local + (1 - core) * (CHUNKS // 2), away_ref)

    @pl.loop(0, CHUNKS // 2, unroll=CHUNKS // 2)
    def _(local):
        step(local, local + core * (CHUNKS // 2), own_ref)


def near_kernel(
    place_ref, x_ref, g_ref, b_ref, c_ref, dt_ref, skip_ref, lam_ref, sig_ref, cum_ref, _after_ref,
    y_ref, dx_ref, db_ref, dc_ref, dl_ref, keep_ref, away_ref, q_ref, w_ref, sk_ref,
    kst_ref, dk_ref, da_ref,
):
    bmat = b_ref[...]
    cmat = c_ref[...]
    cum = cum_ref[...]
    fade = jnp.exp(-cum)
    score = mm_nt(cmat, bmat)
    row = lax.broadcasted_iota(jnp.int32, (TOK, TOK), 0)
    col = lax.broadcasted_iota(jnp.int32, (TOK, TOK), 1)
    apart = jnp.bitwise_xor(row, col)

    def mask_of(level):
        if level == 0:
            return row == col
        return (row > col) & (jnp.right_shift(apart, level - 1) == 1)

    for level in range(INTRA):
        kst_ref[level * TOK : (level + 1) * TOK] = jnp.where(mask_of(level), score, 0.0).astype(BF16)
    near = jnp.concatenate(
        [split2(lam_ref[:, :128] * fade), split2(lam_ref[:, 128:256] * fade)], axis=0
    )
    lift = split2(jnp.exp(cum) * dt_ref[...])
    gain = split2(jnp.broadcast_to(four(skip_ref[...]), (8, 128)))
    dk_ref[...] = jnp.zeros_like(dk_ref)
    da_ref[...] = jnp.zeros_like(da_ref)
    q_ref[...] = jnp.zeros_like(q_ref)
    sk_ref[...] = jnp.zeros_like(sk_ref)

    @pl.loop(0, CHUNKS, unroll=CHUNKS)
    def _(chunk):
        cols = at_chunk(chunk)
        xs = x_ref[:, cols].astype(F32)
        gs = g_ref[:, cols].astype(F32)
        spread0 = onehot(chunk, 0, 256)
        lifted = mm(lift, spread0)
        gains = mm(gain, spread0)[0:1]
        xd = (xs * lifted).astype(BF16)
        kst = kst_ref[...]
        mixed = mm(kst, xd)
        out = gains * xs
        parts = [None] * INTRA
        for quarter in range(4):
            wide = mm(near, onehot(chunk, quarter, 256))
            prods = []
            for part in range(2):
                level = 4 * part + quarter
                mult = wide[TOK * part : TOK * part + TOK]
                value = mixed[level * TOK : (level + 1) * TOK]
                out = out + mult * value
                prods.append((gs * value).astype(BF16))
                parts[level] = (mult * gs).astype(BF16)
            da_ref[...] += mm_nt(jnp.concatenate(prods, axis=0), onehot(chunk, quarter))
        y_ref[:, cols] = out
        agst = jnp.concatenate(parts, axis=0)
        dxd = mm_tn(kst, agst)
        dk_ref[...] += mm_nt(agst, xd)
        ones = onehot(chunk, 0)
        q_ref[...] += mm_nt((dxd * xs).astype(BF16), ones)
        dx_ref[:, cols] = dxd * lifted + gains * gs
        skrow = jnp.sum(xs * gs, axis=0, keepdims=True)
        sk_ref[...] += lax.dot_general(
            jnp.broadcast_to(skrow, (8, CHUNK)), ones.astype(F32), (((1,), (1,)), ((), ())),
            precision=HIGHEST, preferred_element_type=F32,
        )

    dscore = jnp.zeros((TOK, TOK), F32)
    for level in range(INTRA):
        dscore = dscore + jnp.where(mask_of(level), dk_ref[level * TOK : (level + 1) * TOK], 0.0)
    dscore = dscore.astype(BF16)
    dc_ref[...] = mm(dscore, bmat)
    db_ref[...] = mm_tn(dscore, cmat)
    dlam = []
    for part in range(2):
        da = da_ref[TOK * part : TOK * part + TOK]
        dlam.append(da * fade)
    w_ref[...] = dlam[0] * lam_ref[:, :128] + dlam[1] * lam_ref[:, 128:256]
    dlogit = (jnp.concatenate(dlam, axis=1) * sig_ref[:, :256]).astype(BF16)
    dl_ref[...] = dlogit
    second = bit_of(place_ref, 0) == 1
    for part in range(FEAT // 128):
        rows = mm_tn(x_ref[:, 128 * part : 128 * part + 128], dlogit)
        for pair in range(64 // ROWS):
            at = part * (64 // ROWS) + pair
            low, high = rows[64 * pair : 64 * pair + ROWS], rows[64 * pair + ROWS : 64 * pair + 64]
            keep, away = jnp.where(second, high, low), jnp.where(second, low, high)
            for side in range(2):
                keep_ref[at, ROWS * side : ROWS * side + ROWS] = keep[:, 128 * side : 128 * side + 128]
                away_ref[at, ROWS * side : ROWS * side + ROWS] = away[:, 128 * side : 128 * side + 128]


def spread_level(core_ref, x_ref, g_ref, c_ref, lam, fade_ref, y_ref, out_ref, dcs_ref, da_ref, levels, picked):
    cmat = c_ref[...]
    far = split2(lam * fade_ref[...])
    da_ref[...] = jnp.zeros_like(da_ref)
    core = core_ref[0]

    def step(local, chunk, mine):
        cols = at_chunk(chunk)
        gs = g_ref[:, cols].astype(F32)
        carried = jnp.concatenate([v.astype(BF16) for v in picked(chunk, local, mine)], axis=1)
        mixed = mm(cmat, carried)
        out = y_ref[:, cols]
        parts = []
        for quarter in range(levels):
            ones = onehot(chunk, quarter, 256)
            mult = mm(far, ones)
            value = mixed[:, CHUNK * quarter : CHUNK * quarter + CHUNK]
            out = out + mult * value
            da_ref[...] += mm_nt((gs * value).astype(BF16), ones[:128])
            parts.append((mult * gs).astype(BF16))
        out_ref[:, cols] = out.astype(out_ref.dtype)
        dcs_ref[...] += mm_nt(jnp.concatenate(parts, axis=1), carried)

    @pl.loop(0, CHUNKS // 2, unroll=CHUNKS // 2)
    def _(local):
        step(local, local + core * (CHUNKS // 2), True)

    @pl.loop(0, CHUNKS // 2, unroll=CHUNKS // 2)
    def _(local):
        step(local, local + (1 - core) * (CHUNKS // 2), False)

    return da_ref[...] * fade_ref[...]


def far_kernel(
    core_ref, x_ref, g_ref, c_ref, lam_ref, sig_ref, fade_ref, y_ref, dc_ref,
    first_ref, m1_ref, m2_ref, m3_ref, other_ref, _after_ref,
    out_ref, dcs_ref, dl_ref, w_ref,
    da_ref,
):
    lam = lam_ref[:, 256:384]
    dcs_ref[...] = dc_ref[...]

    def picked(chunk, local, mine):
        values = [first_ref[2 * chunk + half] for half in range(2)]
        for span, ref in enumerate((m1_ref, m2_ref, m3_ref)):
            for half in range(2):
                if mine:
                    values.append(ref[2 * local + half])
                else:
                    values.append(other_ref[span * (PAIRS // 2) + 2 * local + half])
        return values

    dlam = spread_level(
        core_ref, x_ref, g_ref, c_ref, lam, fade_ref, y_ref, out_ref, dcs_ref, da_ref, 4, picked
    )
    w_ref[...] = dlam * lam
    dl_ref[...] = (dlam * sig_ref[:, 256:384]).astype(BF16)


def line_kernel(
    core_ref, x_ref, g_ref, c_ref, lam_ref, sig_ref, fade_ref, y_ref, dc_ref, dl1_ref,
    m4_ref, m5_ref, other_ref, _after_ref,
    out_ref, dcout_ref, dl_ref, keep_ref, away_ref, w_ref,
    da_ref, dcs_ref,
):
    lam = lam_ref[:, 384:512]
    dcs_ref[...] = dc_ref[...]

    def picked(chunk, local, mine):
        values = []
        for span, ref in enumerate((m4_ref, m5_ref)):
            for half in range(2):
                if mine:
                    values.append(ref[2 * local + half])
                else:
                    values.append(other_ref[span * (PAIRS // 2) + 2 * local + half])
        return values

    dlam = spread_level(
        core_ref, x_ref, g_ref, c_ref, lam, fade_ref, y_ref, out_ref, dcs_ref, da_ref, 2, picked
    )
    dcout_ref[...] = dcs_ref[...].astype(BF16)
    w_ref[...] = dlam * lam
    dlogit = (dlam * sig_ref[:, 384:512]).astype(BF16)
    dl_ref[...] = dlogit
    both = jnp.concatenate([dl1_ref[...], dlogit], axis=1)
    lane = lax.broadcasted_iota(jnp.int32, (ROWS // 2, 128), 1)
    second = core_ref[0] == 1
    for part in range(FEAT // 128):
        rows = mm_tn(x_ref[:, 128 * part : 128 * part + 128], both)
        turned = pltpu.roll(rows[:, 128:], 64, 1)

        def packed(top):
            mid = top + ROWS // 2
            return jnp.where(lane < 64, rows[top:mid, 128:], turned[mid : mid + ROWS // 2])

        for pair in range(64 // ROWS):
            at = part * (64 // ROWS) + pair
            low, high = rows[64 * pair : 64 * pair + ROWS, :128], rows[64 * pair + ROWS : 64 * pair + 64, :128]
            keep_ref[at, :ROWS], away_ref[at, :ROWS] = jnp.where(second, high, low), jnp.where(second, low, high)
            low, high = packed(64 * pair), packed(64 * pair + ROWS)
            keep_ref[at, ROWS:], away_ref[at, ROWS:] = jnp.where(second, high, low), jnp.where(second, low, high)


def last_kernel(
    place_ref, x_ref, b_ref, dt_ref, cum_ref, rate_ref, w_ref, mine_ref, came_ref, lag_ref, fresh_ref, dx_ref, db_ref,
    dl0_ref, dl1_ref, dl2_ref, q_ref, w0_ref, w1_ref, w2_ref,
    dxout_ref, dbout_ref, ddt_ref, rate_out_ref,
    dbs_ref, q2_ref,
):
    bmat = b_ref[...]
    cum = cum_ref[...]
    dt4 = dt_ref[...]
    left = jnp.exp(cum - cum[TOK - 1 : TOK])
    held = split2(left * dt4)
    dlogit = jnp.concatenate([dl0_ref[...], dl1_ref[...], dl2_ref[...]], axis=1)
    q2_ref[...] = jnp.zeros_like(q2_ref)
    dbs_ref[...] = db_ref[...]

    core = bit_of(place_ref, 0)

    def step(local, chunk, source):
        cols = at_chunk(chunk)
        xs = x_ref[:, cols].astype(F32)
        spread = mm(held, onehot(chunk, 0, 256))
        du = jnp.concatenate(
            [
                (
                    source[2 * local + half] * lag_ref[2 * chunk + half]
                    + came_ref[PAIRS // 2 + 2 * chunk + half] * fresh_ref[0]
                ).astype(BF16)
                for half in range(2)
            ],
            axis=1,
        )
        dxs = mm(bmat, du)
        q2_ref[...] += mm_nt((dxs * xs).astype(BF16), onehot(chunk, 0))
        dbs_ref[...] += mm_nt((xs * spread).astype(BF16), du)
        dx = dx_ref[:, cols] + dxs * spread + mm(dlogit, w_ref[:512, cols])
        dxout_ref[:, cols] = dx.astype(BF16)

    @pl.loop(0, CHUNKS // 2, unroll=CHUNKS // 2)
    def _(local):
        step(local, local + core * (CHUNKS // 2), mine_ref)

    @pl.loop(0, CHUNKS // 2, unroll=CHUNKS // 2)
    def _(local):
        step(local, local + (1 - core) * (CHUNKS // 2), came_ref)

    dbout_ref[...] = dbs_ref[...].astype(BF16)
    q2 = q2_ref[...]
    q1 = q_ref[...]
    lift = jnp.exp(cum)
    gathered = w0_ref[...] + w1_ref[...] + w2_ref[...]
    queried = gathered + pltpu.roll(gathered, 32, 1)
    queried = queried + pltpu.roll(queried, 64, 1)
    keyed2 = q2 * left * dt4
    dcum = q1 * lift * dt4 + keyed2 - queried
    dlog = lax.dot_general(
        sums_down(), dcum, (((0,), (0,)), ((), ())), precision=HIGHEST, preferred_element_type=F32
    )
    dlog = dlog - jnp.sum(keyed2, axis=0, keepdims=True)
    ddt_ref[...] = rate_ref[...] * dlog[:, :32] + (q1 * lift + q2 * left)[:, :32]
    rate_out_ref[...] = jnp.sum(dt4 * dlog, axis=0, keepdims=True)


def bit_of(place_ref, span):
    return jnp.right_shift(place_ref[0], span) % 2


def half_of(rows_ref, index, place_ref):
    return rows_ref[index, pl.ds(pl.multiple_of(bit_of(place_ref, 0) * HALF, HALF), HALF), :]


def up_step(span, place_ref, held_ref, other_ref, rows_ref, lower_ref, next_ref):
    upper = bit_of(place_ref, span) == 1
    rows = half_of(rows_ref, span - 1, place_ref)
    for pair in range(HALF):
        mine, other = held_ref[pair], other_ref[pair]
        lower = jnp.where(upper, other, mine)
        lower_ref[pair] = lower
        next_ref[pair] = lower * rows[pair : pair + 1] + jnp.where(upper, mine, other)


def level_of(span, place_ref, own_ref, came_ref, rows_own_ref, rows_there_ref):
    rows_own = half_of(rows_own_ref, span - 1, place_ref)
    rows_there = half_of(rows_there_ref, span - 1, place_ref)

    def piece(pair):
        return own_ref[0, pair] * rows_own[pair : pair + 1] + came_ref[0, pair] * rows_there[pair : pair + 1]

    return piece


def down_step(span, place_ref, grad, piece, rows_ref, send_ref, keep_ref, crossed_ref=None, lower_ref=None):
    upper = bit_of(place_ref, span) == 1
    rows = half_of(rows_ref, span - 1, place_ref)
    for pair in range(HALF):
        here = grad(pair)
        faded = here * rows[pair : pair + 1]
        send_ref[pair] = jnp.where(upper, faded + piece(pair), here)
        keep_ref[pair] = jnp.where(upper, here, faded)
        if crossed_ref is not None:
            crossed_ref[pair : pair + 1] = jnp.sum(lower_ref[pair] * faded, axis=0, keepdims=True)


def halve(bit, keep_ref, came_ref, keep_out_ref, away_out_ref):
    half = keep_out_ref.shape[0]
    for block in range(half):
        stay, go = bit * half + block, (1 - bit) * half + block
        keep_out_ref[block] = keep_ref[stay] + came_ref[stay]
        away_out_ref[block] = keep_ref[go] + came_ref[go]


def rest_kernel(place_ref, keep_ref, came_ref, _after_ref, keep_out_ref, away_out_ref):
    halve(bit_of(place_ref, 4), keep_ref, came_ref, keep_out_ref, away_out_ref)


def step1_kernel(place_ref, rows_ref, rows_own_ref, rows_there_ref, held_ref, other_ref, own_ref, came_ref, lower_ref, next_ref, send_ref):
    up_step(1, place_ref, held_ref, other_ref, rows_ref, lower_ref, next_ref)
    piece = level_of(5, place_ref, own_ref, came_ref, rows_own_ref, rows_there_ref)
    for pair in range(HALF):
        send_ref[pair] = piece(pair)


def step2_kernel(place_ref, rows_ref, rows_own_ref, rows_there_ref, held_ref, other_ref, own_ref, came_ref, back_ref, near_ref, lower_ref, next_ref, send_ref, keep_ref, near_away_ref):
    near_away_ref[...] = near_ref[...]
    up_step(2, place_ref, held_ref, other_ref, rows_ref, lower_ref, next_ref)
    piece = level_of(4, place_ref, own_ref, came_ref, rows_own_ref, rows_there_ref)
    down_step(4, place_ref, lambda pair: back_ref[pair], piece, rows_ref, send_ref, keep_ref)


def step3_kernel(place_ref, rows_ref, rows_own_ref, rows_there_ref, held_ref, other_ref, own_ref, came_ref, kept_ref, back_ref, near_ref, near_came_ref, level1_ref, level2_ref, lower_ref, next_ref, send_ref, keep_ref, crossed_ref, near_keep_ref, near_away_ref, levels_ref, part_ref):
    halve(bit_of(place_ref, 5), near_ref, near_came_ref, near_keep_ref, near_away_ref)
    for index, level_ref in enumerate((level1_ref, level2_ref, other_ref)):
        for pair in range(HALF):
            levels_ref[index * HALF + pair] = level_ref[pair]
    up_step(3, place_ref, held_ref, other_ref, rows_ref, lower_ref, next_ref)
    upper = bit_of(place_ref, 4) == 1
    rows = half_of(rows_ref, 3, place_ref)
    for pair in range(HALF):
        part_ref[pair] = jnp.where(upper, next_ref[pair], next_ref[pair] * rows[pair : pair + 1])
    piece = level_of(3, place_ref, own_ref, came_ref, rows_own_ref, rows_there_ref)
    down_step(3, place_ref, lambda pair: kept_ref[pair] + back_ref[pair], piece, rows_ref, send_ref, keep_ref, crossed_ref, lower_ref)


def step4_kernel(place_ref, rows_ref, rows_own_ref, rows_there_ref, held_ref, other_ref, direct_ref, cross_ref, own_ref, came_ref, kept_ref, back_ref, first_ref, lower2_ref, near_ref, near_came_ref, _after_ref, level_ref, both_ref, send_ref, keep_ref, crossed_ref, crossed4_ref, near_keep_ref, near_away_ref):
    halve(bit_of(place_ref, 4), near_ref, near_came_ref, near_keep_ref, near_away_ref)
    upper = bit_of(place_ref, 4) == 1
    rows = half_of(rows_ref, 3, place_ref)
    for pair in range(HALF):
        mine, other = held_ref[pair], other_ref[pair]
        faded = jnp.where(upper, other, mine) * rows[pair : pair + 1]
        crossed4_ref[pair : pair + 1] = jnp.sum(faded * first_ref[pair], axis=0, keepdims=True)
        whole = direct_ref[pair] + cross_ref[pair]
        level_ref[pair] = whole
        both_ref[pair] = other
        both_ref[HALF + pair] = whole
    piece = level_of(2, place_ref, own_ref, came_ref, rows_own_ref, rows_there_ref)
    down_step(2, place_ref, lambda pair: kept_ref[pair] + back_ref[pair], piece, rows_ref, send_ref, keep_ref, crossed_ref, lower2_ref)


def step5_kernel(place_ref, rows_ref, rows_own_ref, rows_there_ref, own_ref, came_ref, kept_ref, back_ref, lower1_ref, near_ref, near_came_ref, far_ref, send_ref, keep_ref, crossed_ref, near_keep_ref, near_away_ref, far_away_ref):
    halve(bit_of(place_ref, 3), near_ref, near_came_ref, near_keep_ref, near_away_ref)
    far_away_ref[...] = far_ref[...]
    piece = level_of(1, place_ref, own_ref, came_ref, rows_own_ref, rows_there_ref)
    down_step(1, place_ref, lambda pair: kept_ref[pair] + back_ref[pair], piece, rows_ref, send_ref, keep_ref, crossed_ref, lower1_ref)


def step6_kernel(place_ref, row_ref, kept_ref, back_ref, lower0_ref, cot_ref, near_ref, near_came_ref, far_ref, far_came_ref, send_ref, crossed_ref, near_out_ref, far_keep_ref, far_away_ref):
    near_out_ref[...] = near_ref[...] + near_came_ref[...]
    halve(bit_of(place_ref, 5), far_ref, far_came_ref, far_keep_ref, far_away_ref)
    rows = row_ref[pl.ds(pl.multiple_of(bit_of(place_ref, 0) * HALF, HALF), HALF), :]
    upper = bit_of(place_ref, 0) == 1
    for pair in range(HALF):
        grad = kept_ref[pair] + back_ref[pair]
        send_ref[pair] = grad
        crossed_ref[pair : pair + 1] = jnp.sum(lower0_ref[pair] * rows[pair : pair + 1] * grad, axis=0, keepdims=True)
    for pair in range(PAIRS):
        send_ref[HALF + pair] = jnp.where(upper, cot_ref[pair], 0.0)


VMEM_LIMIT = 56 * 1024 * 1024
FOLD = ROWS + ROWS // 2


def call(kernel, outs, scratch=(), flops=0, moved=1 << 20, specs=None):
    extra = {} if specs is None else {"in_specs": specs}
    return pl.pallas_call(
        kernel,
        out_shape=outs,
        scratch_shapes=list(scratch),
        compiler_params=pltpu.CompilerParams(vmem_limit_bytes=VMEM_LIMIT),
        cost_estimate=pl.CostEstimate(flops=flops, bytes_accessed=moved, transcendentals=0),
        **extra,
    )


def one_step(kernel, outs, *operands):
    specs, arrays = [pl.BlockSpec(memory_space=pltpu.SMEM)], [operands[0]]
    for operand in operands[1:]:
        if not isinstance(operand, tuple):
            arrays.append(operand)
            specs.append(pl.BlockSpec(operand.shape, lambda _, rank=operand.ndim: (0,) * rank))
        elif operand[0] == "slab":
            arrays.append(operand[2])
            specs.append(pl.BlockSpec((1,) + operand[2].shape[1:], lambda _, at=operand[1]: (at, 0, 0, 0)))
        else:
            arrays.append(operand[1])
            specs.append(pl.BlockSpec(memory_space=pl.ANY))
    return pl.pallas_call(
        kernel,
        grid=(1,),
        out_shape=tuple(outs),
        in_specs=specs,
        out_specs=tuple(pl.BlockSpec(out.shape, lambda _, rank=len(out.shape): (0,) * rank) for out in outs),
        compiler_params=pltpu.CompilerParams(vmem_limit_bytes=VMEM_LIMIT),
        cost_estimate=pl.CostEstimate(flops=1 << 22, bytes_accessed=4 << 20, transcendentals=0),
    )(*arrays)


def shaped(*dims, dtype=F32):
    return jax.ShapeDtypeStruct(dims, dtype)


def swap(value, bit, only=None, more=0):
    pairs = []
    for source in range(BLOCKS):
        if only is None or (source >> bit) % 2 == only:
            pairs.append((source, source ^ (1 << bit) ^ more))
    return lax.ppermute(value, "ctx", pairs)


def turn(value, bit):
    count = lax.axis_size("dp")
    return lax.ppermute(value, "dp", [(source, source ^ (1 << bit)) for source in range(count)])


def part(value, start, count):
    return lax.dynamic_slice_in_dim(value, start, count, 0)


def per_device(inputs, matrix_b, matrix_c, steps_dt, decay_rate, skip_gain, level_weight, grad_out):
    xs, bs, cs, gs = inputs[0], matrix_b[0], matrix_c[0], grad_out[0]
    turned_dt, turned_w = steps_dt[0].T, level_weight.T
    place = lax.axis_index("ctx")
    core = place % 2
    bits = [jnp.right_shift(place, span) % 2 for span in range(SPANS)]
    rate = decay_rate.reshape(1, HEADS)
    core_here = core.astype(jnp.int32).reshape(1)
    vmem = pl.BlockSpec(memory_space=pltpu.VMEM)
    smem = pl.BlockSpec(memory_space=pltpu.SMEM)
    anywhere = pl.BlockSpec(memory_space=pl.ANY)

    def choose(bit, low, high):
        return jnp.where(bits[bit] == 1, high, low)

    def mine_of(value):
        return part(value, core * HALF, HALF)

    def yours_of(value):
        return part(value, (1 - core) * HALF, HALF)

    own_sum = jnp.sum(turned_dt, axis=1)[None]
    other = swap(own_sum, 0)
    sum_up = [choose(0, other, own_sum)]
    sum_in = [jnp.zeros_like(own_sum), choose(0, jnp.zeros_like(other), other)]
    there = choose(0, own_sum, -other)
    states, cum, dt4, row_first = call(
        state_kernel,
        (shaped(PAIRS, NST, 128), shaped(TOK, 128), shaped(TOK, 128), shaped(PAIRS, 128)),
        flops=2 * TOK * FEAT * 2 * NST,
        moved=2 << 20,
    )(xs, bs, turned_dt, rate, sum_up[0])
    first = swap(states, 0)
    group_sum = own_sum + other
    for span in range(1, SPANS - 1):
        other = swap(group_sum, span)
        sum_up.append(choose(span, other, group_sum))
        sum_in.append(sum_in[-1] + choose(span, jnp.zeros_like(other), other))
        if span in (2, 3):
            beside = (cum, cum) if span == 2 else (lam, first)
            group_sum, row_first = call(
                sum_kernel,
                (shaped(1, HEADS), shaped(PAIRS, 128)),
                specs=[vmem] * 3 + [anywhere] * 2,
                moved=1024,
            )(group_sum, other, row_first, *beside)
        else:
            group_sum = group_sum + other
        if span == 2:
            cot0, own, away, lam, sig = call(
                cot_kernel,
                (
                    shaped(PAIRS, NST, 128),
                    shaped(SPANS - 1, HALF, NST, 128),
                    shaped(SPANS - 1, HALF, NST, 128),
                    shaped(TOK, 512),
                    shaped(TOK, 512),
                ),
                flops=2 * TOK * FEAT * (512 + 10 * NST),
                moved=10 << 20,
                specs=[smem] + [vmem] * 5 + [anywhere],
            )(core_here, xs, gs, cs, cum, turned_w, group_sum)
    on = jnp.stack(bits).astype(F32)[:, None]
    sum_up, sum_in = jnp.concatenate(sum_up), jnp.concatenate(sum_in)
    rows_up, rows_own, rows_there, fade_in = call(
        rows_kernel,
        (
            shaped(SPANS - 2, PAIRS, 128),
            shaped(SPANS - 1, PAIRS, 128),
            shaped(SPANS - 1, PAIRS, 128),
            shaped(SPANS, HEADS),
        ),
        moved=1024,
    )(sum_up, sum_in, there, jnp.broadcast_to(on, (SPANS, HEADS)), rate)
    place_here = place.astype(jnp.int32).reshape(1)
    rows = (rows_up, rows_own, rows_there)
    slab = shaped(HALF, NST, 128)
    crossed = shaped(HALF, 128)

    mine, yours = mine_of(states), mine_of(first)
    row = mine_of(row_first)[:, None]
    lower0 = choose(0, mine, yours)
    held0 = lower0 * row + choose(0, yours, mine)
    came = swap(away, 0)
    level1 = swap(held0, 1)
    lower1, held1, send = one_step(
        step1_kernel, [slab] * 3, place_here, *rows, held0, level1, ("slab", 4, own), ("slab", 4, came)
    )
    fade_t = jnp.exp(-cum)
    fade_far = fade_t[None] * jnp.concatenate([fade_in, jnp.zeros((2, HEADS), F32)]).reshape(2, 1, 128)
    level2, back4 = swap(held1, 2), swap(send, 5, 1)
    y_near, dx_near, db_near, dc_near, dl_near, near_keep, near_away, q_near, w_near, skip_sum = call(
        near_kernel,
        (
            shaped(TOK, FEAT),
            shaped(TOK, FEAT),
            shaped(TOK, NST),
            shaped(TOK, NST),
            shaped(TOK, 256, dtype=BF16),
            shaped(BLOCKS // 2, 2 * ROWS, 128),
            shaped(BLOCKS // 2, 2 * ROWS, 128),
            shaped(TOK, 128),
            shaped(TOK, 128),
            shaped(8, 128),
        ),
        scratch=(
            pltpu.VMEM((INTRA * TOK, TOK), BF16),
            pltpu.VMEM((INTRA * TOK, TOK), F32),
            pltpu.VMEM((2 * TOK, 128), F32),
        ),
        flops=2 * TOK * FEAT * (5 * INTRA * NST),
        moved=12 << 20,
        specs=[smem] + [vmem] * 9 + [anywhere],
    )(place_here, xs, gs, bs, cs, dt4, skip_gain.reshape(1, HEADS), lam, sig, cum, send)
    lower2, held2, send, keep, near_away = one_step(
        step2_kernel, [slab] * 4 + [shaped(BLOCKS // 2, 2 * ROWS, 128)], place_here, *rows, held1, level2,
        ("slab", 3, own), ("slab", 3, came), back4, near_away,
    )
    level3, back, near_came = swap(held2, 3), swap(send, 4), swap(near_away, 0)
    _, held3, send, keep, crossed3, near_keep, near_away, levels, part3 = one_step(
        step3_kernel,
        [slab] * 4 + [crossed] + [shaped(16, 2 * ROWS, 128)] * 2 + [shaped(3 * HALF, NST, 128), slab],
        place_here, *rows, held2, level3, ("slab", 2, own), ("slab", 2, came), keep, back,
        near_keep, near_came, level1, level2,
    )
    level4, back, near_came = swap(held3, 4), swap(send, 3), swap(near_away, 5)
    direct, cross = swap(part3, 5, 0), swap(part3, 5, 0, 16)
    across_near = swap(levels, 0)
    y_far, dc_far, dl_far, w_far = call(
        far_kernel,
        (shaped(TOK, FEAT), shaped(TOK, NST), shaped(TOK, 128, dtype=BF16), shaped(TOK, 128)),
        scratch=[pltpu.VMEM((TOK, 128), F32)],
        flops=2 * TOK * FEAT * 16 * NST,
        moved=10 << 20,
        specs=[smem] + [vmem] * 13 + [anywhere],
    )(
        core_here, xs, gs, cs, lam, sig, fade_far[0], y_near, dc_near,
        first, level1, level2, level3, across_near, send,
    )
    level5, both, send, keep, crossed2, crossed4, near_keep, near_away = one_step(
        step4_kernel, [slab, shaped(PAIRS, NST, 128)] + [slab] * 2 + [crossed] * 2 + [shaped(8, 2 * ROWS, 128)] * 2,
        place_here, *rows, held3, level4, direct, cross, ("slab", 1, own), ("slab", 1, came), keep, back,
        back4, lower2, near_keep, near_came, ("after", w_far),
    )
    back, across_far, near_came = swap(send, 2), swap(both, 0), swap(near_away, 4)
    output, grad_c, dl_line, far_keep, far_away, w_line = call(
        line_kernel,
        (
            shaped(TOK, FEAT, dtype=BF16),
            shaped(TOK, NST, dtype=BF16),
            shaped(TOK, 128, dtype=BF16),
            shaped(BLOCKS // 2, FOLD, 128),
            shaped(BLOCKS // 2, FOLD, 128),
            shaped(TOK, 128),
        ),
        scratch=[pltpu.VMEM((TOK, 128), F32), pltpu.VMEM((TOK, NST), F32)],
        flops=2 * TOK * FEAT * 10 * NST,
        moved=6 << 20,
        specs=[smem] + [vmem] * 12 + [anywhere],
    )(
        core_here, xs, gs, cs, lam, sig, fade_far[1], y_far, dc_far, dl_far,
        level4, level5, across_far, send,
    )
    send, keep, crossed1, near_keep, near_away, far_away = one_step(
        step5_kernel,
        [slab] * 2 + [crossed] + [shaped(4, 2 * ROWS, 128)] * 2 + [shaped(BLOCKS // 2, FOLD, 128)],
        place_here, *rows, ("slab", 0, own), ("slab", 0, came), keep, back, lower1,
        near_keep, near_came, far_away,
    )
    back, near_came, far_came = swap(send, 1), swap(near_away, 3), swap(far_away, 0)
    going, crossed0, near_rows, far_keep, far_away = one_step(
        step6_kernel,
        [shaped(HALF + PAIRS, NST, 128), crossed, shaped(4, 2 * ROWS, 128)] + [shaped(16, FOLD, 128)] * 2,
        place_here, row_first, keep, back, lower0, cot0, near_keep, near_came, far_keep, far_came,
    )
    last_came, far_came = swap(going, 0), swap(far_away, 5)
    lag = choose(0, row_first, jnp.ones_like(row_first))[:, None]
    fresh = choose(0, jnp.ones((1, 1, 128), F32), jnp.zeros((1, 1, 128), F32))
    grad_inputs, grad_b, ddt, rate_row = call(
        last_kernel,
        (
            shaped(TOK, FEAT, dtype=BF16),
            shaped(TOK, NST, dtype=BF16),
            shaped(TOK, HEADS),
            shaped(1, 128),
        ),
        scratch=[pltpu.VMEM((TOK, NST), F32), pltpu.VMEM((TOK, 128), F32)],
        flops=2 * TOK * FEAT * 8 * NST,
        moved=10 << 20,
        specs=[smem] + [vmem] * 19,
    )(
        place_here, xs, bs, dt4, cum, rate, turned_w, going, last_came, lag, fresh,
        dx_near, db_near, dl_near, dl_far, dl_line, q_near, w_near, w_far, w_line,
    )
    far_keep, far_away = one_step(
        rest_kernel, [shaped(8, FOLD, 128)] * 2, place_here, far_keep, far_came, ("after", rate_row)
    )
    far_came = swap(far_away, 4)

    queried = jnp.concatenate([jnp.sum(w_far, axis=0), jnp.sum(w_line, axis=0)]).reshape(8, HEADS)[:SPANS] * on
    halves = jnp.stack([crossed0, crossed1, crossed2, crossed3, crossed4, jnp.zeros_like(crossed0)])
    halves = jnp.sum(halves.reshape(SPANS, HEADS // 2, SIZE), axis=2)
    keyed = jnp.zeros((SPANS, 2, HEADS // 2), F32)
    keyed = lax.dynamic_update_slice_in_dim(keyed, halves[:, None], core, 1).reshape(SPANS, HEADS)
    inside = jnp.sum(sum_in * queried, axis=0) + jnp.sum(sum_up * keyed[: SPANS - 1], axis=0)
    extra = jnp.concatenate(
        [
            queried,
            keyed,
            (rate_row[0, :HEADS] - inside)[None],
            skip_sum[:1, :HEADS],
            jnp.zeros((2, HEADS), F32),
        ]
    )
    extra = extra.reshape(4, 128)
    far_rows = None
    between = jnp.zeros((HEADS,), F32)
    for step in range(SPANS):
        sent, keep = [extra], []
        if step == 1:
            far_rows = far_keep + far_came
        if 1 <= step <= 3:
            for rows in (far_rows, near_rows) if step <= 2 else (far_rows,):
                split = rows.reshape(rows.shape[0] // 2, 2, rows.shape[1], 128)
                keep.append(lax.dynamic_index_in_dim(split, bits[step], 1, keepdims=False))
                sent.append(lax.dynamic_index_in_dim(split, 1 - bits[step], 1, keepdims=False).reshape(-1, 128))
        came = swap(jnp.concatenate(sent), step)
        at = 4
        added = []
        for rows in keep:
            size = rows.shape[0] * rows.shape[1]
            added.append(rows + came[at : at + size].reshape(rows.shape))
            at += size
        if added:
            far_rows = added[0]
            near_rows = added[1] if len(added) > 1 else near_rows
        told = came[:4].reshape(16, HEADS)
        if step + 1 < SPANS:
            later = jnp.sum(on[step + 1 :] * told[step + 1 : SPANS], axis=0)
            between = between + choose(step, later, jnp.zeros_like(later))
        extra = extra + came[:4]
        between = between + on[step] * extra.reshape(16, HEADS)[SPANS + step]
    total = jnp.concatenate([extra, far_rows[0], near_rows[0]])
    for step in range(2):
        total = total + turn(total, step)
    ends = total[3].reshape(4, HEADS)
    rows, near_rows = total[4 : 4 + FOLD], total[4 + FOLD :]
    packed = rows[ROWS:FOLD]
    grad_level = jnp.concatenate(
        [
            near_rows[:ROWS],
            near_rows[ROWS:],
            rows[:ROWS],
            jnp.concatenate([packed[:, :64], packed[:, 64:]], axis=0),
            jnp.zeros((ROWS, level_weight.shape[1] - 448), F32),
        ],
        axis=1,
    )
    grad_dt = (ddt - rate * between[None])[None]
    return (output[None], grad_inputs[None], grad_b[None], grad_c[None], grad_dt, ends[0], ends[1], grad_level)


def solution(mesh):
    split = P("dp", "ctx", None)
    return jax.shard_map(
        per_device,
        mesh=mesh,
        in_specs=(split, split, split, split, P(), P(), P(), split),
        out_specs=(split, split, split, split, split, P(), P(), P("ctx", None)),
        check_vma=False,
    )
```

```python
import jax
import jax.numpy as jnp
import numpy as np
from jax import lax
from jax.experimental import pallas as pl
from jax.experimental.pallas import tpu as pltpu
from jax.sharding import PartitionSpec as P

F32 = jnp.float32
BF16 = jnp.bfloat16
HIGHEST = lax.Precision.HIGHEST
HEADS = 32
SIZE = 64
TOK = 128
NST = 128
FEAT = HEADS * SIZE
INTRA = 8
SPANS = 6
USED = INTRA + SPANS
CHUNK = 256
CHUNKS = FEAT // CHUNK
PAIRS = FEAT // 128
HALF = PAIRS // 2
BLOCKS = 64
ROWS = FEAT // BLOCKS


def mm(a, b):
    return lax.dot_general(a, b, (((1,), (0,)), ((), ())), preferred_element_type=F32)


def mm_nt(a, b):
    return lax.dot_general(a, b, (((1,), (1,)), ((), ())), preferred_element_type=F32)


def mm_tn(a, b):
    return lax.dot_general(a, b, (((0,), (0,)), ((), ())), preferred_element_type=F32)


def onehot(chunk, quarter, rows=128):
    row = lax.broadcasted_iota(jnp.int32, (rows, CHUNK), 0)
    lane = lax.broadcasted_iota(jnp.int32, (rows, CHUNK), 1)
    if rows > 128:
        row = jnp.where(row >= 128, row - 128, row)
    head = chunk * (CHUNK // SIZE) + jnp.right_shift(lane, 6) + 32 * quarter
    return jnp.where(row == head, 1.0, 0.0).astype(BF16)


def split2(a):
    hi = a.astype(BF16)
    lo = (a - hi.astype(F32)).astype(BF16)
    return jnp.concatenate([hi, lo], axis=1)


def four(a):
    return jnp.concatenate([a, a, a, a], axis=1)


def sums_down():
    row = lax.broadcasted_iota(jnp.int32, (TOK, TOK), 0)
    col = lax.broadcasted_iota(jnp.int32, (TOK, TOK), 1)
    return jnp.where(row >= col, 1.0, 0.0).astype(F32)


def at_chunk(chunk):
    return pl.ds(pl.multiple_of(chunk * CHUNK, CHUNK), CHUNK)


def rows_of(per_head):
    pair = lax.broadcasted_iota(jnp.int32, (PAIRS, HEADS), 0)
    head = lax.broadcasted_iota(jnp.int32, (PAIRS, HEADS), 1)
    picked = jnp.where(jnp.right_shift(head, 1) == pair, per_head, 0.0)
    side = lax.broadcasted_iota(jnp.int32, (HEADS, 128), 0) % 2
    lane = lax.broadcasted_iota(jnp.int32, (HEADS, 128), 1)
    spread = jnp.where(side == jnp.right_shift(lane, 6), 1.0, 0.0).astype(F32)
    return lax.dot_general(
        picked, spread, (((1,), (0,)), ((), ())), precision=HIGHEST, preferred_element_type=F32
    )


def sum_kernel(own_ref, other_ref, row_ref, _first_ref, _second_ref, out_ref, row_out_ref):
    out_ref[...] = own_ref[...] + other_ref[...]
    row_out_ref[...] = row_ref[...]


def state_kernel(x_ref, b_ref, dt_ref, rate_ref, up_ref, u_ref, cum_ref, dt4_ref, row_ref):
    row_ref[...] = rows_of(jnp.exp(-up_ref[...] * rate_ref[...]))
    turned = dt_ref[...]
    dt4 = jnp.concatenate([turned, turned, turned, turned], axis=0).T
    cum = lax.dot_general(
        sums_down(), dt4 * four(rate_ref[...]), (((1,), (0,)), ((), ())),
        precision=HIGHEST, preferred_element_type=F32,
    )
    cum_ref[...] = cum
    dt4_ref[...] = dt4
    held = split2(jnp.exp(cum - cum[TOK - 1 : TOK]) * dt4)
    bmat = b_ref[...]

    @pl.loop(0, CHUNKS, unroll=CHUNKS)
    def _(chunk):
        xs = x_ref[:, at_chunk(chunk)].astype(F32)
        state = mm_tn(bmat, (xs * mm(held, onehot(chunk, 0, 256))).astype(BF16))
        for half in range(2):
            u_ref[2 * chunk + half] = state[:, 128 * half : 128 * half + 128]


def rows_kernel(up_ref, in_ref, there_ref, on_ref, rate_ref, rows_up_ref, rows_own_ref, rows_there_ref, fade_ref):
    rate = rate_ref[...]
    fade_ref[...] = jnp.exp(-in_ref[...] * rate) * on_ref[...]
    for span in range(1, SPANS - 1):
        rows_up_ref[span - 1] = rows_of(jnp.exp(-up_ref[span : span + 1] * rate))
    for span in range(1, SPANS):
        on = on_ref[span : span + 1]
        rows_own_ref[span - 1] = rows_of(jnp.exp(-in_ref[span : span + 1] * rate) * on)
        rows_there_ref[span - 1] = rows_of(jnp.exp(-(in_ref[span : span + 1] + there_ref[...]) * rate) * on)


def cot_kernel(core_ref, x_ref, g_ref, c_ref, cum_ref, w_ref, _after_ref, d0_ref, own_ref, away_ref, lam_ref, sig_ref):
    fade = jnp.exp(-cum_ref[...])
    logit = mm_nt(x_ref[...], w_ref[:512])
    soft = jnp.maximum(logit, 0.0) + jnp.log1p(jnp.exp(-jnp.abs(logit)))
    lam_ref[...] = soft
    sig_ref[...] = 1.0 / (1.0 + jnp.exp(-logit))
    far = jnp.concatenate([split2(soft[:, 256:384] * fade), split2(soft[:, 384:512] * fade)], axis=0)
    cmat = c_ref[...]

    core = core_ref[0]

    def step(local, chunk, d_ref):
        gs = g_ref[:, at_chunk(chunk)].astype(F32)
        parts = [None] * SPANS
        for quarter in range(4):
            wide = mm(far if quarter < 2 else far[:TOK], onehot(chunk, quarter, 256))
            parts[quarter] = (wide[:TOK] * gs).astype(BF16)
            if quarter < 2:
                parts[4 + quarter] = (wide[TOK:] * gs).astype(BF16)
        cots = mm_tn(cmat, jnp.concatenate(parts, axis=1))
        for half in range(2):
            d0_ref[2 * chunk + half] = cots[:, 128 * half : 128 * half + 128]
            for span in range(1, SPANS):
                at = CHUNK * span + 128 * half
                d_ref[span - 1, 2 * local + half] = cots[:, at : at + 128]

    @pl.loop(0, CHUNKS // 2, unroll=CHUNKS // 2)
    def _(local):
        step(local, local + (1 - core) * (CHUNKS // 2), away_ref)

    @pl.loop(0, CHUNKS // 2, unroll=CHUNKS // 2)
    def _(local):
        step(local, local + core * (CHUNKS // 2), own_ref)


def near_kernel(
    place_ref, x_ref, g_ref, b_ref, c_ref, dt_ref, skip_ref, lam_ref, sig_ref, cum_ref, _after_ref,
    y_ref, dx_ref, db_ref, dc_ref, dl_ref, keep_ref, away_ref, q_ref, w_ref, sk_ref,
    kst_ref, dk_ref, da_ref,
):
    bmat = b_ref[...]
    cmat = c_ref[...]
    cum = cum_ref[...]
    fade = jnp.exp(-cum)
    score = mm_nt(cmat, bmat)
    row = lax.broadcasted_iota(jnp.int32, (TOK, TOK), 0)
    col = lax.broadcasted_iota(jnp.int32, (TOK, TOK), 1)
    apart = jnp.bitwise_xor(row, col)

    def mask_of(level):
        if level == 0:
            return row == col
        return (row > col) & (jnp.right_shift(apart, level - 1) == 1)

    for level in range(INTRA):
        kst_ref[level * TOK : (level + 1) * TOK] = jnp.where(mask_of(level), score, 0.0).astype(BF16)
    near = jnp.concatenate(
        [split2(lam_ref[:, :128] * fade), split2(lam_ref[:, 128:256] * fade)], axis=0
    )
    lift = split2(jnp.exp(cum) * dt_ref[...])
    gain = split2(jnp.broadcast_to(four(skip_ref[...]), (8, 128)))
    dk_ref[...] = jnp.zeros_like(dk_ref)
    da_ref[...] = jnp.zeros_like(da_ref)
    q_ref[...] = jnp.zeros_like(q_ref)
    sk_ref[...] = jnp.zeros_like(sk_ref)

    @pl.loop(0, CHUNKS, unroll=CHUNKS)
    def _(chunk):
        cols = at_chunk(chunk)
        xs = x_ref[:, cols].astype(F32)
        gs = g_ref[:, cols].astype(F32)
        spread0 = onehot(chunk, 0, 256)
        lifted = mm(lift, spread0)
        gains = mm(gain, spread0)[0:1]
        xd = (xs * lifted).astype(BF16)
        kst = kst_ref[...]
        mixed = mm(kst, xd)
        out = gains * xs
        parts = [None] * INTRA
        for quarter in range(4):
            wide = mm(near, onehot(chunk, quarter, 256))
            prods = []
            for part in range(2):
                level = 4 * part + quarter
                mult = wide[TOK * part : TOK * part + TOK]
                value = mixed[level * TOK : (level + 1) * TOK]
                out = out + mult * value
                prods.append((gs * value).astype(BF16))
                parts[level] = (mult * gs).astype(BF16)
            da_ref[...] += mm_nt(jnp.concatenate(prods, axis=0), onehot(chunk, quarter))
        y_ref[:, cols] = out
        agst = jnp.concatenate(parts, axis=0)
        dxd = mm_tn(kst, agst)
        dk_ref[...] += mm_nt(agst, xd)
        ones = onehot(chunk, 0)
        q_ref[...] += mm_nt((dxd * xs).astype(BF16), ones)
        dx_ref[:, cols] = dxd * lifted + gains * gs
        skrow = jnp.sum(xs * gs, axis=0, keepdims=True)
        sk_ref[...] += lax.dot_general(
            jnp.broadcast_to(skrow, (8, CHUNK)), ones.astype(F32), (((1,), (1,)), ((), ())),
            precision=HIGHEST, preferred_element_type=F32,
        )

    dscore = jnp.zeros((TOK, TOK), F32)
    for level in range(INTRA):
        dscore = dscore + jnp.where(mask_of(level), dk_ref[level * TOK : (level + 1) * TOK], 0.0)
    dscore = dscore.astype(BF16)
    dc_ref[...] = mm(dscore, bmat)
    db_ref[...] = mm_tn(dscore, cmat)
    dlam = []
    for part in range(2):
        da = da_ref[TOK * part : TOK * part + TOK]
        dlam.append(da * fade)
    w_ref[...] = dlam[0] * lam_ref[:, :128] + dlam[1] * lam_ref[:, 128:256]
    dlogit = (jnp.concatenate(dlam, axis=1) * sig_ref[:, :256]).astype(BF16)
    dl_ref[...] = dlogit
    second = bit_of(place_ref, 0) == 1
    for part in range(FEAT // 128):
        rows = mm_tn(x_ref[:, 128 * part : 128 * part + 128], dlogit)
        for pair in range(64 // ROWS):
            at = part * (64 // ROWS) + pair
            low, high = rows[64 * pair : 64 * pair + ROWS], rows[64 * pair + ROWS : 64 * pair + 64]
            keep, away = jnp.where(second, high, low), jnp.where(second, low, high)
            for quarter in range(4):
                top, left = ROWS // 2 * (quarter % 2), 128 * (quarter // 2)
                keep_ref[quarter, at] = keep[top : top + ROWS // 2, left : left + 128]
                away_ref[quarter, at] = away[top : top + ROWS // 2, left : left + 128]


def spread_level(core_ref, x_ref, g_ref, c_ref, lam, fade_ref, y_ref, out_ref, dcs_ref, da_ref, levels, picked):
    cmat = c_ref[...]
    far = split2(lam * fade_ref[...])
    da_ref[...] = jnp.zeros_like(da_ref)
    core = core_ref[0]

    def step(local, chunk, mine):
        cols = at_chunk(chunk)
        gs = g_ref[:, cols].astype(F32)
        carried = jnp.concatenate([v.astype(BF16) for v in picked(chunk, local, mine)], axis=1)
        mixed = mm(cmat, carried)
        out = y_ref[:, cols]
        parts = []
        for quarter in range(levels):
            ones = onehot(chunk, quarter, 256)
            mult = mm(far, ones)
            value = mixed[:, CHUNK * quarter : CHUNK * quarter + CHUNK]
            out = out + mult * value
            da_ref[...] += mm_nt((gs * value).astype(BF16), ones[:128])
            parts.append((mult * gs).astype(BF16))
        out_ref[:, cols] = out.astype(out_ref.dtype)
        dcs_ref[...] += mm_nt(jnp.concatenate(parts, axis=1), carried)

    @pl.loop(0, CHUNKS // 2, unroll=CHUNKS // 2)
    def _(local):
        step(local, local + core * (CHUNKS // 2), True)

    @pl.loop(0, CHUNKS // 2, unroll=CHUNKS // 2)
    def _(local):
        step(local, local + (1 - core) * (CHUNKS // 2), False)

    return da_ref[...] * fade_ref[...]


def far_kernel(
    core_ref, x_ref, g_ref, c_ref, lam_ref, sig_ref, fade_ref, y_ref, dc_ref,
    first_ref, m1_ref, m2_ref, m3_ref, other_ref, _after_ref,
    out_ref, dcs_ref, dl_ref, w_ref,
    da_ref,
):
    lam = lam_ref[:, 256:384]
    dcs_ref[...] = dc_ref[...]

    def picked(chunk, local, mine):
        values = [first_ref[2 * chunk + half] for half in range(2)]
        for span, ref in enumerate((m1_ref, m2_ref, m3_ref)):
            for half in range(2):
                if mine:
                    values.append(ref[2 * local + half])
                else:
                    values.append(other_ref[span * (PAIRS // 2) + 2 * local + half])
        return values

    dlam = spread_level(
        core_ref, x_ref, g_ref, c_ref, lam, fade_ref, y_ref, out_ref, dcs_ref, da_ref, 4, picked
    )
    w_ref[...] = dlam * lam
    dl_ref[...] = (dlam * sig_ref[:, 256:384]).astype(BF16)


def line_kernel(
    core_ref, x_ref, g_ref, c_ref, lam_ref, sig_ref, fade_ref, y_ref, dc_ref, dl1_ref,
    m4_ref, m5_ref, other_ref, _after_ref,
    out_ref, dcout_ref, dl_ref, keep_ref, away_ref, w_ref,
    da_ref, dcs_ref,
):
    lam = lam_ref[:, 384:512]
    dcs_ref[...] = dc_ref[...]

    def picked(chunk, local, mine):
        values = []
        for span, ref in enumerate((m4_ref, m5_ref)):
            for half in range(2):
                if mine:
                    values.append(ref[2 * local + half])
                else:
                    values.append(other_ref[span * (PAIRS // 2) + 2 * local + half])
        return values

    dlam = spread_level(
        core_ref, x_ref, g_ref, c_ref, lam, fade_ref, y_ref, out_ref, dcs_ref, da_ref, 2, picked
    )
    dcout_ref[...] = dcs_ref[...].astype(BF16)
    w_ref[...] = dlam * lam
    dlogit = (dlam * sig_ref[:, 384:512]).astype(BF16)
    dl_ref[...] = dlogit
    both = jnp.concatenate([dl1_ref[...], dlogit], axis=1)
    lane = lax.broadcasted_iota(jnp.int32, (ROWS // 2, 128), 1)
    second = core_ref[0] == 1
    for part in range(FEAT // 128):
        rows = mm_tn(x_ref[:, 128 * part : 128 * part + 128], both)
        turned = pltpu.roll(rows[:, 128:], 64, 1)

        def packed(top):
            mid = top + ROWS // 2
            return jnp.where(lane < 64, rows[top:mid, 128:], turned[mid : mid + ROWS // 2])

        for pair in range(64 // ROWS):
            at = part * (64 // ROWS) + pair
            low, high = rows[64 * pair : 64 * pair + ROWS, :128], rows[64 * pair + ROWS : 64 * pair + 64, :128]
            keep_ref[at, :ROWS], away_ref[at, :ROWS] = jnp.where(second, high, low), jnp.where(second, low, high)
            low, high = packed(64 * pair), packed(64 * pair + ROWS)
            keep_ref[at, ROWS:], away_ref[at, ROWS:] = jnp.where(second, high, low), jnp.where(second, low, high)


def last_kernel(
    place_ref, x_ref, b_ref, dt_ref, cum_ref, rate_ref, w_ref, mine_ref, came_ref, lag_ref, fresh_ref, dx_ref, db_ref,
    dl0_ref, dl1_ref, dl2_ref, q_ref, w0_ref, w1_ref, w2_ref,
    dxout_ref, dbout_ref, ddt_ref, rate_out_ref,
    dbs_ref, q2_ref,
):
    bmat = b_ref[...]
    cum = cum_ref[...]
    dt4 = dt_ref[...]
    left = jnp.exp(cum - cum[TOK - 1 : TOK])
    held = split2(left * dt4)
    dlogit = jnp.concatenate([dl0_ref[...], dl1_ref[...], dl2_ref[...]], axis=1)
    q2_ref[...] = jnp.zeros_like(q2_ref)
    dbs_ref[...] = db_ref[...]

    core = bit_of(place_ref, 0)

    def step(local, chunk, source):
        cols = at_chunk(chunk)
        xs = x_ref[:, cols].astype(F32)
        spread = mm(held, onehot(chunk, 0, 256))
        du = jnp.concatenate(
            [
                (
                    source[2 * local + half] * lag_ref[2 * chunk + half]
                    + came_ref[PAIRS // 2 + 2 * chunk + half] * fresh_ref[0]
                ).astype(BF16)
                for half in range(2)
            ],
            axis=1,
        )
        dxs = mm(bmat, du)
        q2_ref[...] += mm_nt((dxs * xs).astype(BF16), onehot(chunk, 0))
        dbs_ref[...] += mm_nt((xs * spread).astype(BF16), du)
        dx = dx_ref[:, cols] + dxs * spread + mm(dlogit, w_ref[:512, cols])
        dxout_ref[:, cols] = dx.astype(BF16)

    @pl.loop(0, CHUNKS // 2, unroll=CHUNKS // 2)
    def _(local):
        step(local, local + core * (CHUNKS // 2), mine_ref)

    @pl.loop(0, CHUNKS // 2, unroll=CHUNKS // 2)
    def _(local):
        step(local, local + (1 - core) * (CHUNKS // 2), came_ref)

    dbout_ref[...] = dbs_ref[...].astype(BF16)
    q2 = q2_ref[...]
    q1 = q_ref[...]
    lift = jnp.exp(cum)
    gathered = w0_ref[...] + w1_ref[...] + w2_ref[...]
    queried = gathered + pltpu.roll(gathered, 32, 1)
    queried = queried + pltpu.roll(queried, 64, 1)
    keyed2 = q2 * left * dt4
    dcum = q1 * lift * dt4 + keyed2 - queried
    dlog = lax.dot_general(
        sums_down(), dcum, (((0,), (0,)), ((), ())), precision=HIGHEST, preferred_element_type=F32
    )
    dlog = dlog - jnp.sum(keyed2, axis=0, keepdims=True)
    ddt_ref[...] = (four(rate_ref[...]) * dlog + q1 * lift + q2 * left).T[:HEADS]
    rate_out_ref[...] = jnp.sum(dt4 * dlog, axis=0, keepdims=True)


def bit_of(place_ref, span):
    return jnp.right_shift(place_ref[0], span) % 2


def half_of(rows_ref, index, place_ref):
    return rows_ref[index, pl.ds(pl.multiple_of(bit_of(place_ref, 0) * HALF, HALF), HALF), :]


def up_step(span, place_ref, held_ref, other_ref, rows_ref, lower_ref, next_ref):
    upper = bit_of(place_ref, span) == 1
    rows = half_of(rows_ref, span - 1, place_ref)
    for pair in range(HALF):
        mine, other = held_ref[pair], other_ref[pair]
        lower = jnp.where(upper, other, mine)
        lower_ref[pair] = lower
        next_ref[pair] = lower * rows[pair : pair + 1] + jnp.where(upper, mine, other)


def level_of(span, place_ref, own_ref, came_ref, rows_own_ref, rows_there_ref):
    rows_own = half_of(rows_own_ref, span - 1, place_ref)
    rows_there = half_of(rows_there_ref, span - 1, place_ref)

    def piece(pair):
        return own_ref[0, pair] * rows_own[pair : pair + 1] + came_ref[0, pair] * rows_there[pair : pair + 1]

    return piece


def down_step(span, place_ref, grad, piece, rows_ref, send_ref, keep_ref, crossed_ref=None, lower_ref=None):
    upper = bit_of(place_ref, span) == 1
    rows = half_of(rows_ref, span - 1, place_ref)
    for pair in range(HALF):
        here = grad(pair)
        faded = here * rows[pair : pair + 1]
        send_ref[pair] = jnp.where(upper, faded + piece(pair), here)
        keep_ref[pair] = jnp.where(upper, here, faded)
        if crossed_ref is not None:
            crossed_ref[pair : pair + 1] = jnp.sum(lower_ref[pair] * faded, axis=0, keepdims=True)


def halve(bit, keep_ref, came_ref, keep_out_ref, away_out_ref):
    half = keep_out_ref.shape[0]
    for block in range(half):
        stay, go = bit * half + block, (1 - bit) * half + block
        keep_out_ref[block] = keep_ref[stay] + came_ref[stay]
        away_out_ref[block] = keep_ref[go] + came_ref[go]


def note_kernel(place_ref, c0_ref, c1_ref, c2_ref, c3_ref, c4_ref, far_ref, line_ref, up_ref, in_ref, on_ref, rate_ref, skip_ref, out_ref):
    core = bit_of(place_ref, 0)
    lane = lax.broadcasted_iota(jnp.int32, (128, HEADS), 0)
    side = lax.broadcasted_iota(jnp.int32, (128, HEADS), 1) % 2
    gather = jnp.where(side == jnp.right_shift(lane, 6), 1.0, 0.0).astype(F32)
    pair = lax.broadcasted_iota(jnp.int32, (HALF, HEADS), 0) + HALF * core
    head = lax.broadcasted_iota(jnp.int32, (HALF, HEADS), 1)
    keyed = []
    for ref in (c0_ref, c1_ref, c2_ref, c3_ref, c4_ref):
        sums = lax.dot_general(
            ref[...], gather, (((1,), (0,)), ((), ())), precision=HIGHEST, preferred_element_type=F32
        )
        keyed.append(jnp.sum(jnp.where(jnp.right_shift(head, 1) == pair, sums, 0.0), axis=0, keepdims=True))
    wide = jnp.sum(far_ref[...], axis=0, keepdims=True), jnp.sum(line_ref[...], axis=0, keepdims=True)
    queried = []
    for span in range(SPANS):
        at = 32 * (span % 4)
        queried.append(wide[span // 4][:, at : at + 32] * on_ref[span : span + 1])
    inside = jnp.zeros((1, HEADS), F32)
    for span in range(SPANS):
        inside = inside + in_ref[span : span + 1] * queried[span]
        if span < SPANS - 1:
            inside = inside + up_ref[span : span + 1] * keyed[span]
    none = jnp.zeros((1, HEADS), F32)
    rows = queried + keyed + [none, rate_ref[:, :HEADS] - inside, skip_ref[0:1, :HEADS], none, none]
    for row in range(4):
        out_ref[row : row + 1] = jnp.concatenate(rows[4 * row : 4 * row + 4], axis=1)


def rest_kernel(place_ref, keep_ref, came_ref, _after_ref, keep_out_ref, away_out_ref):
    halve(bit_of(place_ref, 4), keep_ref, came_ref, keep_out_ref, away_out_ref)


def step1_kernel(place_ref, rows_ref, rows_own_ref, rows_there_ref, held_ref, other_ref, own_ref, came_ref, lower_ref, next_ref, send_ref):
    up_step(1, place_ref, held_ref, other_ref, rows_ref, lower_ref, next_ref)
    piece = level_of(5, place_ref, own_ref, came_ref, rows_own_ref, rows_there_ref)
    for pair in range(HALF):
        send_ref[pair] = piece(pair)


def step2_kernel(place_ref, rows_ref, rows_own_ref, rows_there_ref, held_ref, other_ref, own_ref, came_ref, back_ref, near_ref, lower_ref, next_ref, send_ref, keep_ref, near_away_ref):
    near_away_ref[...] = near_ref[...]
    up_step(2, place_ref, held_ref, other_ref, rows_ref, lower_ref, next_ref)
    piece = level_of(4, place_ref, own_ref, came_ref, rows_own_ref, rows_there_ref)
    down_step(4, place_ref, lambda pair: back_ref[pair], piece, rows_ref, send_ref, keep_ref)


def step3_kernel(place_ref, rows_ref, rows_own_ref, rows_there_ref, held_ref, other_ref, own_ref, came_ref, kept_ref, back_ref, near_ref, near_came_ref, level1_ref, level2_ref, lower_ref, next_ref, send_ref, keep_ref, crossed_ref, near_keep_ref, near_away_ref, levels_ref, part_ref):
    halve(place_ref[1] // 2, near_ref, near_came_ref, near_keep_ref, near_away_ref)
    for index, level_ref in enumerate((level1_ref, level2_ref, other_ref)):
        for pair in range(HALF):
            levels_ref[index * HALF + pair] = level_ref[pair]
    up_step(3, place_ref, held_ref, other_ref, rows_ref, lower_ref, next_ref)
    upper = bit_of(place_ref, 4) == 1
    rows = half_of(rows_ref, 3, place_ref)
    for pair in range(HALF):
        part_ref[pair] = jnp.where(upper, next_ref[pair], next_ref[pair] * rows[pair : pair + 1])
    piece = level_of(3, place_ref, own_ref, came_ref, rows_own_ref, rows_there_ref)
    down_step(3, place_ref, lambda pair: kept_ref[pair] + back_ref[pair], piece, rows_ref, send_ref, keep_ref, crossed_ref, lower_ref)


def step4_kernel(place_ref, rows_ref, rows_own_ref, rows_there_ref, held_ref, other_ref, direct_ref, cross_ref, own_ref, came_ref, kept_ref, back_ref, first_ref, lower2_ref, near_ref, near_came_ref, _after_ref, level_ref, both_ref, send_ref, keep_ref, crossed_ref, crossed4_ref, near_keep_ref, near_away_ref):
    halve(place_ref[1] % 2, near_ref, near_came_ref, near_keep_ref, near_away_ref)
    upper = bit_of(place_ref, 4) == 1
    rows = half_of(rows_ref, 3, place_ref)
    for pair in range(HALF):
        mine, other = held_ref[pair], other_ref[pair]
        faded = jnp.where(upper, other, mine) * rows[pair : pair + 1]
        crossed4_ref[pair : pair + 1] = jnp.sum(faded * first_ref[pair], axis=0, keepdims=True)
        whole = direct_ref[pair] + cross_ref[pair]
        level_ref[pair] = whole
        both_ref[pair] = other
        both_ref[HALF + pair] = whole
    piece = level_of(2, place_ref, own_ref, came_ref, rows_own_ref, rows_there_ref)
    down_step(2, place_ref, lambda pair: kept_ref[pair] + back_ref[pair], piece, rows_ref, send_ref, keep_ref, crossed_ref, lower2_ref)


def step5_kernel(place_ref, rows_ref, rows_own_ref, rows_there_ref, own_ref, came_ref, kept_ref, back_ref, lower1_ref, near_ref, near_came_ref, far_ref, send_ref, keep_ref, crossed_ref, near_keep_ref, near_away_ref, far_away_ref):
    halve(bit_of(place_ref, 5), near_ref, near_came_ref, near_keep_ref, near_away_ref)
    far_away_ref[...] = far_ref[...]
    piece = level_of(1, place_ref, own_ref, came_ref, rows_own_ref, rows_there_ref)
    down_step(1, place_ref, lambda pair: kept_ref[pair] + back_ref[pair], piece, rows_ref, send_ref, keep_ref, crossed_ref, lower1_ref)


def step6_kernel(place_ref, row_ref, kept_ref, back_ref, lower0_ref, cot_ref, near_ref, near_came_ref, far_ref, far_came_ref, send_ref, crossed_ref, near_keep_ref, near_away_ref, far_keep_ref, far_away_ref):
    halve(bit_of(place_ref, 4), near_ref, near_came_ref, near_keep_ref, near_away_ref)
    halve(bit_of(place_ref, 5), far_ref, far_came_ref, far_keep_ref, far_away_ref)
    rows = row_ref[pl.ds(pl.multiple_of(bit_of(place_ref, 0) * HALF, HALF), HALF), :]
    upper = bit_of(place_ref, 0) == 1
    for pair in range(HALF):
        grad = kept_ref[pair] + back_ref[pair]
        send_ref[pair] = grad
        crossed_ref[pair : pair + 1] = jnp.sum(lower0_ref[pair] * rows[pair : pair + 1] * grad, axis=0, keepdims=True)
    for pair in range(PAIRS):
        send_ref[HALF + pair] = jnp.where(upper, cot_ref[pair], 0.0)


VMEM_LIMIT = 56 * 1024 * 1024
FOLD = ROWS + ROWS // 2


def call(kernel, outs, scratch=(), flops=0, moved=1 << 20, specs=None):
    extra = {} if specs is None else {"in_specs": specs}
    return pl.pallas_call(
        kernel,
        out_shape=outs,
        scratch_shapes=list(scratch),
        compiler_params=pltpu.CompilerParams(vmem_limit_bytes=VMEM_LIMIT),
        cost_estimate=pl.CostEstimate(flops=flops, bytes_accessed=moved, transcendentals=0),
        **extra,
    )


def one_step(kernel, outs, *operands):
    specs, arrays = [pl.BlockSpec(memory_space=pltpu.SMEM)], [operands[0]]
    for operand in operands[1:]:
        if not isinstance(operand, tuple):
            arrays.append(operand)
            specs.append(pl.BlockSpec(operand.shape, lambda _, rank=operand.ndim: (0,) * rank))
        elif operand[0] == "slab":
            arrays.append(operand[2])
            specs.append(pl.BlockSpec((1,) + operand[2].shape[1:], lambda _, at=operand[1]: (at, 0, 0, 0)))
        else:
            arrays.append(operand[1])
            specs.append(pl.BlockSpec(memory_space=pl.ANY))
    return pl.pallas_call(
        kernel,
        grid=(1,),
        out_shape=tuple(outs),
        in_specs=specs,
        out_specs=tuple(pl.BlockSpec(out.shape, lambda _, rank=len(out.shape): (0,) * rank) for out in outs),
        compiler_params=pltpu.CompilerParams(vmem_limit_bytes=VMEM_LIMIT),
        cost_estimate=pl.CostEstimate(flops=1 << 22, bytes_accessed=4 << 20, transcendentals=0),
    )(*arrays)


def shaped(*dims, dtype=F32):
    return jax.ShapeDtypeStruct(dims, dtype)


def swap(value, bit, only=None, more=0):
    pairs = []
    for source in range(BLOCKS):
        if only is None or (source >> bit) % 2 == only:
            pairs.append((source, source ^ (1 << bit) ^ more))
    return lax.ppermute(value, "ctx", pairs)


def turn(value, bit):
    count = lax.axis_size("dp")
    return lax.ppermute(value, "dp", [(source, source ^ (1 << bit)) for source in range(count)])


def part(value, start, count):
    return lax.dynamic_slice_in_dim(value, start, count, 0)


def per_device(inputs, matrix_b, matrix_c, steps_dt, decay_rate, skip_gain, level_weight, grad_out):
    xs, bs, cs, gs = inputs[0], matrix_b[0], matrix_c[0], grad_out[0]
    turned_dt, turned_w = steps_dt[0].T, level_weight.T
    place = lax.axis_index("ctx")
    core = place % 2
    bits = [jnp.right_shift(place, span) % 2 for span in range(SPANS)]
    rate = decay_rate.reshape(1, HEADS)
    core_here = core.astype(jnp.int32).reshape(1)
    vmem = pl.BlockSpec(memory_space=pltpu.VMEM)
    smem = pl.BlockSpec(memory_space=pltpu.SMEM)
    anywhere = pl.BlockSpec(memory_space=pl.ANY)

    def choose(bit, low, high):
        return jnp.where(bits[bit] == 1, high, low)

    def mine_of(value):
        return part(value, core * HALF, HALF)

    def yours_of(value):
        return part(value, (1 - core) * HALF, HALF)

    own_sum = jnp.sum(turned_dt, axis=1)[None]
    other = swap(own_sum, 0)
    sum_up = [choose(0, other, own_sum)]
    sum_in = [jnp.zeros_like(own_sum), choose(0, jnp.zeros_like(other), other)]
    there = choose(0, own_sum, -other)
    states, cum, dt4, row_first = call(
        state_kernel,
        (shaped(PAIRS, NST, 128), shaped(TOK, 128), shaped(TOK, 128), shaped(PAIRS, 128)),
        flops=2 * TOK * FEAT * 2 * NST,
        moved=2 << 20,
    )(xs, bs, turned_dt, rate, sum_up[0])
    first = swap(states, 0)
    group_sum = own_sum + other
    for span in range(1, SPANS - 1):
        other = swap(group_sum, span)
        sum_up.append(choose(span, other, group_sum))
        sum_in.append(sum_in[-1] + choose(span, jnp.zeros_like(other), other))
        if span in (2, 3):
            beside = (cum, cum) if span == 2 else (lam, first)
            group_sum, row_first = call(
                sum_kernel,
                (shaped(1, HEADS), shaped(PAIRS, 128)),
                specs=[vmem] * 3 + [anywhere] * 2,
                moved=1024,
            )(group_sum, other, row_first, *beside)
        else:
            group_sum = group_sum + other
        if span == 2:
            cot0, own, away, lam, sig = call(
                cot_kernel,
                (
                    shaped(PAIRS, NST, 128),
                    shaped(SPANS - 1, HALF, NST, 128),
                    shaped(SPANS - 1, HALF, NST, 128),
                    shaped(TOK, 512),
                    shaped(TOK, 512),
                ),
                flops=2 * TOK * FEAT * (512 + 10 * NST),
                moved=10 << 20,
                specs=[smem] + [vmem] * 5 + [anywhere],
            )(core_here, xs, gs, cs, cum, turned_w, group_sum)
    on = jnp.stack(bits).astype(F32)[:, None]
    sum_up, sum_in = jnp.concatenate(sum_up), jnp.concatenate(sum_in)
    on_rows = jnp.broadcast_to(on, (SPANS, HEADS))
    rows_up, rows_own, rows_there, fade_in = call(
        rows_kernel,
        (
            shaped(SPANS - 2, PAIRS, 128),
            shaped(SPANS - 1, PAIRS, 128),
            shaped(SPANS - 1, PAIRS, 128),
            shaped(SPANS, HEADS),
        ),
        moved=1024,
    )(sum_up, sum_in, there, on_rows, rate)
    place_here = jnp.stack([place, lax.axis_index("dp")]).astype(jnp.int32)
    rows = (rows_up, rows_own, rows_there)
    slab = shaped(HALF, NST, 128)
    crossed = shaped(HALF, 128)

    mine, yours = mine_of(states), mine_of(first)
    row = mine_of(row_first)[:, None]
    lower0 = choose(0, mine, yours)
    held0 = lower0 * row + choose(0, yours, mine)
    came = swap(away, 0)
    level1 = swap(held0, 1)
    lower1, held1, send = one_step(
        step1_kernel, [slab] * 3, place_here, *rows, held0, level1, ("slab", 4, own), ("slab", 4, came)
    )
    fade_t = jnp.exp(-cum)
    fade_far = fade_t[None] * jnp.concatenate([fade_in, jnp.zeros((2, HEADS), F32)]).reshape(2, 1, 128)
    level2, back4 = swap(held1, 2), swap(send, 5, 1)
    y_near, dx_near, db_near, dc_near, dl_near, near_keep, near_away, q_near, w_near, skip_sum = call(
        near_kernel,
        (
            shaped(TOK, FEAT),
            shaped(TOK, FEAT),
            shaped(TOK, NST),
            shaped(TOK, NST),
            shaped(TOK, 256, dtype=BF16),
            shaped(4, BLOCKS // 2, ROWS // 2, 128),
            shaped(4, BLOCKS // 2, ROWS // 2, 128),
            shaped(TOK, 128),
            shaped(TOK, 128),
            shaped(8, 128),
        ),
        scratch=(
            pltpu.VMEM((INTRA * TOK, TOK), BF16),
            pltpu.VMEM((INTRA * TOK, TOK), F32),
            pltpu.VMEM((2 * TOK, 128), F32),
        ),
        flops=2 * TOK * FEAT * (5 * INTRA * NST),
        moved=12 << 20,
        specs=[smem] + [vmem] * 9 + [anywhere],
    )(place_here, xs, gs, bs, cs, dt4, skip_gain.reshape(1, HEADS), lam, sig, cum, send)
    lower2, held2, send, keep, near_away = one_step(
        step2_kernel, [slab] * 4 + [shaped(4, BLOCKS // 2, ROWS // 2, 128)], place_here, *rows, held1, level2,
        ("slab", 3, own), ("slab", 3, came), back4, near_away,
    )
    level3, back, near_came = swap(held2, 3), swap(send, 4), swap(near_away, 0)
    _, held3, send, keep, crossed3, near_keep, near_away, levels, part3 = one_step(
        step3_kernel,
        [slab] * 4 + [crossed] + [shaped(2, BLOCKS // 2, ROWS // 2, 128)] * 2 + [shaped(3 * HALF, NST, 128), slab],
        place_here, *rows, held2, level3, ("slab", 2, own), ("slab", 2, came), keep, back,
        near_keep, near_came, level1, level2,
    )
    level4, back, near_came = swap(held3, 4), swap(send, 3), turn(near_away, 1)
    direct, cross = swap(part3, 5, 0), swap(part3, 5, 0, 16)
    across_near = swap(levels, 0)
    y_far, dc_far, dl_far, w_far = call(
        far_kernel,
        (shaped(TOK, FEAT), shaped(TOK, NST), shaped(TOK, 128, dtype=BF16), shaped(TOK, 128)),
        scratch=[pltpu.VMEM((TOK, 128), F32)],
        flops=2 * TOK * FEAT * 16 * NST,
        moved=10 << 20,
        specs=[smem] + [vmem] * 13 + [anywhere],
    )(
        core_here, xs, gs, cs, lam, sig, fade_far[0], y_near, dc_near,
        first, level1, level2, level3, across_near, send,
    )
    level5, both, send, keep, crossed2, crossed4, near_keep, near_away = one_step(
        step4_kernel, [slab, shaped(PAIRS, NST, 128)] + [slab] * 2 + [crossed] * 2 + [shaped(1, BLOCKS // 2, ROWS // 2, 128)] * 2,
        place_here, *rows, held3, level4, direct, cross, ("slab", 1, own), ("slab", 1, came), keep, back,
        back4, lower2, near_keep, near_came, ("after", w_far),
    )
    back, across_far, near_came = swap(send, 2), swap(both, 0), turn(near_away, 0)[0]
    output, grad_c, dl_line, far_keep, far_away, w_line = call(
        line_kernel,
        (
            shaped(TOK, FEAT, dtype=BF16),
            shaped(TOK, NST, dtype=BF16),
            shaped(TOK, 128, dtype=BF16),
            shaped(BLOCKS // 2, FOLD, 128),
            shaped(BLOCKS // 2, FOLD, 128),
            shaped(TOK, 128),
        ),
        scratch=[pltpu.VMEM((TOK, 128), F32), pltpu.VMEM((TOK, NST), F32)],
        flops=2 * TOK * FEAT * 10 * NST,
        moved=6 << 20,
        specs=[smem] + [vmem] * 12 + [anywhere],
    )(
        core_here, xs, gs, cs, lam, sig, fade_far[1], y_far, dc_far, dl_far,
        level4, level5, across_far, send,
    )
    send, keep, crossed1, near_keep, near_away, far_away = one_step(
        step5_kernel,
        [slab] * 2 + [crossed] + [shaped(16, ROWS // 2, 128)] * 2 + [shaped(BLOCKS // 2, FOLD, 128)],
        place_here, *rows, ("slab", 0, own), ("slab", 0, came), keep, back, lower1,
        near_keep[0], near_came, far_away,
    )
    back, near_came, far_came = swap(send, 1), swap(near_away, 5), swap(far_away, 0)
    going, crossed0, near_keep, near_away, far_keep, far_away = one_step(
        step6_kernel,
        [shaped(HALF + PAIRS, NST, 128), crossed] + [shaped(8, ROWS // 2, 128)] * 2 + [shaped(16, FOLD, 128)] * 2,
        place_here, row_first, keep, back, lower0, cot0, near_keep, near_came, far_keep, far_came,
    )
    last_came, far_came, near_came = swap(going, 0), swap(far_away, 5), swap(near_away, 4)
    lag = choose(0, row_first, jnp.ones_like(row_first))[:, None]
    fresh = choose(0, jnp.ones((1, 1, 128), F32), jnp.zeros((1, 1, 128), F32))
    grad_inputs, grad_b, ddt, rate_row = call(
        last_kernel,
        (
            shaped(TOK, FEAT, dtype=BF16),
            shaped(TOK, NST, dtype=BF16),
            shaped(HEADS, TOK),
            shaped(1, 128),
        ),
        scratch=[pltpu.VMEM((TOK, NST), F32), pltpu.VMEM((TOK, 128), F32)],
        flops=2 * TOK * FEAT * 8 * NST,
        moved=10 << 20,
        specs=[smem] + [vmem] * 19,
    )(
        place_here, xs, bs, dt4, cum, rate, turned_w, going, last_came, lag, fresh,
        dx_near, db_near, dl_near, dl_far, dl_line, q_near, w_near, w_far, w_line,
    )
    far_keep, far_away = one_step(
        rest_kernel, [shaped(8, FOLD, 128)] * 2, place_here, far_keep, far_came, ("after", rate_row)
    )
    far_came = swap(far_away, 4)

    (extra,) = one_step(
        note_kernel, [shaped(4, 128)], place_here, crossed0, crossed1, crossed2, crossed3, crossed4,
        w_far, w_line, sum_up, sum_in, on_rows, rate_row, skip_sum,
    )
    far_rows = None
    between = jnp.zeros((HEADS,), F32)
    for step in range(SPANS):
        sent, keep = [extra], []
        if step == 1:
            far_rows, near_rows = far_keep + far_came, near_keep + near_came
        if 1 <= step <= 3:
            for rows in (far_rows, near_rows):
                split = rows.reshape(rows.shape[0] // 2, 2, rows.shape[1], 128)
                keep.append(lax.dynamic_index_in_dim(split, bits[step], 1, keepdims=False))
                sent.append(lax.dynamic_index_in_dim(split, 1 - bits[step], 1, keepdims=False).reshape(-1, 128))
        came = swap(jnp.concatenate(sent), step)
        at = 4
        added = []
        for rows in keep:
            size = rows.shape[0] * rows.shape[1]
            added.append(rows + came[at : at + size].reshape(rows.shape))
            at += size
        if added:
            far_rows, near_rows = added
        told = came[:4].reshape(16, HEADS)
        if step + 1 < SPANS:
            later = jnp.sum(on[step + 1 :] * told[step + 1 : SPANS], axis=0)
            between = between + choose(step, later, jnp.zeros_like(later))
        extra = extra + came[:4]
        between = between + on[step] * extra.reshape(16, HEADS)[SPANS + step]
    total, near_rows = jnp.concatenate([extra, far_rows[0]]), near_rows[0]
    at_y = lax.axis_index("dp")
    for step in range(2):
        other = turn(jnp.concatenate([total, near_rows]), step)
        second = (at_y // (step + 1)) % 2 == 1
        other_rows = other[4 + FOLD :]
        near_rows = jnp.where(
            second, jnp.concatenate([other_rows, near_rows]), jnp.concatenate([near_rows, other_rows])
        )
        total = total + other[: 4 + FOLD]
    ends = total[3].reshape(4, HEADS)
    rows = total[4:]
    packed = rows[ROWS:FOLD]
    grad_level = jnp.concatenate(
        [
            near_rows[:ROWS],
            near_rows[ROWS:],
            rows[:ROWS],
            jnp.concatenate([packed[:, :64], packed[:, 64:]], axis=0),
            jnp.zeros((ROWS, level_weight.shape[1] - 448), F32),
        ],
        axis=1,
    )
    grad_dt = (ddt - (decay_rate * between)[:, None]).T[None]
    return (output[None], grad_inputs[None], grad_b[None], grad_c[None], grad_dt, ends[0], ends[1], grad_level)


def solution(mesh):
    split = P("dp", "ctx", None)
    return jax.shard_map(
        per_device,
        mesh=mesh,
        in_specs=(split, split, split, split, P(), P(), P(), split),
        out_specs=(split, split, split, split, split, P(), P(), P("ctx", None)),
        check_vma=False,
    )
```

```python
import jax
import jax.numpy as jnp
import numpy as np
from jax import lax
from jax.experimental import pallas as pl
from jax.experimental.pallas import tpu as pltpu
from jax.sharding import PartitionSpec as P

F32 = jnp.float32
BF16 = jnp.bfloat16
HIGHEST = lax.Precision.HIGHEST
HEADS = 32
SIZE = 64
TOK = 128
NST = 128
FEAT = HEADS * SIZE
INTRA = 8
SPANS = 6
USED = INTRA + SPANS
CHUNK = 256
CHUNKS = FEAT // CHUNK
PAIRS = FEAT // 128
HALF = PAIRS // 2
BLOCKS = 64
ROWS = FEAT // BLOCKS


def mm(a, b):
    return lax.dot_general(a, b, (((1,), (0,)), ((), ())), preferred_element_type=F32)


def mm_nt(a, b):
    return lax.dot_general(a, b, (((1,), (1,)), ((), ())), preferred_element_type=F32)


def mm_tn(a, b):
    return lax.dot_general(a, b, (((0,), (0,)), ((), ())), preferred_element_type=F32)


def onehot(chunk, quarter, rows=128):
    row = lax.broadcasted_iota(jnp.int32, (rows, CHUNK), 0)
    lane = lax.broadcasted_iota(jnp.int32, (rows, CHUNK), 1)
    if rows > 128:
        row = jnp.where(row >= 128, row - 128, row)
    head = chunk * (CHUNK // SIZE) + jnp.right_shift(lane, 6) + 32 * quarter
    return jnp.where(row == head, 1.0, 0.0).astype(BF16)


def split2(a):
    hi = a.astype(BF16)
    lo = (a - hi.astype(F32)).astype(BF16)
    return jnp.concatenate([hi, lo], axis=1)


def four(a):
    return jnp.concatenate([a, a, a, a], axis=1)


def sums_down():
    row = lax.broadcasted_iota(jnp.int32, (TOK, TOK), 0)
    col = lax.broadcasted_iota(jnp.int32, (TOK, TOK), 1)
    return jnp.where(row >= col, 1.0, 0.0).astype(F32)


def at_chunk(chunk):
    return pl.ds(pl.multiple_of(chunk * CHUNK, CHUNK), CHUNK)


def rows_of(per_head):
    pair = lax.broadcasted_iota(jnp.int32, (PAIRS, HEADS), 0)
    head = lax.broadcasted_iota(jnp.int32, (PAIRS, HEADS), 1)
    picked = jnp.where(jnp.right_shift(head, 1) == pair, per_head, 0.0)
    side = lax.broadcasted_iota(jnp.int32, (HEADS, 128), 0) % 2
    lane = lax.broadcasted_iota(jnp.int32, (HEADS, 128), 1)
    spread = jnp.where(side == jnp.right_shift(lane, 6), 1.0, 0.0).astype(F32)
    return lax.dot_general(
        picked, spread, (((1,), (0,)), ((), ())), precision=HIGHEST, preferred_element_type=F32
    )


def sum_kernel(own_ref, other_ref, row_ref, _first_ref, _second_ref, out_ref, row_out_ref):
    out_ref[...] = own_ref[...] + other_ref[...]
    row_out_ref[...] = row_ref[...]


def state_kernel(x_ref, b_ref, dt_ref, rate_ref, up_ref, u_ref, cum_ref, dt4_ref, row_ref):
    row_ref[...] = rows_of(jnp.exp(-up_ref[...] * rate_ref[...]))
    turned = dt_ref[...]
    dt4 = jnp.concatenate([turned, turned, turned, turned], axis=0).T
    cum = lax.dot_general(
        sums_down(), dt4 * four(rate_ref[...]), (((1,), (0,)), ((), ())),
        precision=HIGHEST, preferred_element_type=F32,
    )
    cum_ref[...] = cum
    dt4_ref[...] = dt4
    held = split2(jnp.exp(cum - cum[TOK - 1 : TOK]) * dt4)
    bmat = b_ref[...]

    @pl.loop(0, CHUNKS, unroll=CHUNKS)
    def _(chunk):
        xs = x_ref[:, at_chunk(chunk)].astype(F32)
        state = mm_tn(bmat, (xs * mm(held, onehot(chunk, 0, 256))).astype(BF16))
        for half in range(2):
            u_ref[2 * chunk + half] = state[:, 128 * half : 128 * half + 128]


def rows_kernel(up_ref, in_ref, there_ref, on_ref, rate_ref, rows_up_ref, rows_own_ref, rows_there_ref, fade_ref):
    rate = rate_ref[...]
    fade_ref[...] = jnp.exp(-in_ref[...] * rate) * on_ref[...]
    for span in range(1, SPANS - 1):
        rows_up_ref[span - 1] = rows_of(jnp.exp(-up_ref[span : span + 1] * rate))
    for span in range(1, SPANS):
        on = on_ref[span : span + 1]
        rows_own_ref[span - 1] = rows_of(jnp.exp(-in_ref[span : span + 1] * rate) * on)
        rows_there_ref[span - 1] = rows_of(jnp.exp(-(in_ref[span : span + 1] + there_ref[...]) * rate) * on)


def cot_kernel(core_ref, x_ref, g_ref, c_ref, cum_ref, w_ref, _after_ref, d0_ref, own_ref, away_ref, lam_ref, sig_ref):
    fade = jnp.exp(-cum_ref[...])
    logit = mm_nt(x_ref[...], w_ref[:512])
    soft = jnp.maximum(logit, 0.0) + jnp.log1p(jnp.exp(-jnp.abs(logit)))
    lam_ref[...] = soft
    sig_ref[...] = 1.0 / (1.0 + jnp.exp(-logit))
    far = jnp.concatenate([split2(soft[:, 256:384] * fade), split2(soft[:, 384:512] * fade)], axis=0)
    cmat = c_ref[...]

    core = core_ref[0]

    def step(local, chunk, d_ref):
        gs = g_ref[:, at_chunk(chunk)].astype(F32)
        parts = [None] * SPANS
        for quarter in range(4):
            wide = mm(far if quarter < 2 else far[:TOK], onehot(chunk, quarter, 256))
            parts[quarter] = (wide[:TOK] * gs).astype(BF16)
            if quarter < 2:
                parts[4 + quarter] = (wide[TOK:] * gs).astype(BF16)
        cots = mm_tn(cmat, jnp.concatenate(parts, axis=1))
        for half in range(2):
            d0_ref[2 * chunk + half] = cots[:, 128 * half : 128 * half + 128]
            for span in range(1, SPANS):
                at = CHUNK * span + 128 * half
                d_ref[span - 1, 2 * local + half] = cots[:, at : at + 128]

    @pl.loop(0, CHUNKS // 2, unroll=CHUNKS // 2)
    def _(local):
        step(local, local + (1 - core) * (CHUNKS // 2), away_ref)

    @pl.loop(0, CHUNKS // 2, unroll=CHUNKS // 2)
    def _(local):
        step(local, local + core * (CHUNKS // 2), own_ref)


def near_kernel(
    place_ref, x_ref, g_ref, b_ref, c_ref, dt_ref, skip_ref, lam_ref, sig_ref, cum_ref, _after_ref,
    y_ref, dx_ref, db_ref, dc_ref, dl_ref, keep_ref, away_ref, q_ref, w_ref, sk_ref,
    kst_ref, dk_ref, da_ref,
):
    bmat = b_ref[...]
    cmat = c_ref[...]
    cum = cum_ref[...]
    fade = jnp.exp(-cum)
    score = mm_nt(cmat, bmat)
    row = lax.broadcasted_iota(jnp.int32, (TOK, TOK), 0)
    col = lax.broadcasted_iota(jnp.int32, (TOK, TOK), 1)
    apart = jnp.bitwise_xor(row, col)

    def mask_of(level):
        if level == 0:
            return row == col
        return (row > col) & (jnp.right_shift(apart, level - 1) == 1)

    for level in range(INTRA):
        kst_ref[level * TOK : (level + 1) * TOK] = jnp.where(mask_of(level), score, 0.0).astype(BF16)
    near = jnp.concatenate(
        [split2(lam_ref[:, :128] * fade), split2(lam_ref[:, 128:256] * fade)], axis=0
    )
    lift = split2(jnp.exp(cum) * dt_ref[...])
    gain = split2(jnp.broadcast_to(four(skip_ref[...]), (8, 128)))
    dk_ref[...] = jnp.zeros_like(dk_ref)
    da_ref[...] = jnp.zeros_like(da_ref)
    q_ref[...] = jnp.zeros_like(q_ref)
    sk_ref[...] = jnp.zeros_like(sk_ref)

    @pl.loop(0, CHUNKS, unroll=CHUNKS)
    def _(chunk):
        cols = at_chunk(chunk)
        xs = x_ref[:, cols].astype(F32)
        gs = g_ref[:, cols].astype(F32)
        spread0 = onehot(chunk, 0, 256)
        lifted = mm(lift, spread0)
        gains = mm(gain, spread0)[0:1]
        xd = (xs * lifted).astype(BF16)
        kst = kst_ref[...]
        mixed = mm(kst, xd)
        out = gains * xs
        parts = [None] * INTRA
        for quarter in range(4):
            wide = mm(near, onehot(chunk, quarter, 256))
            prods = []
            for part in range(2):
                level = 4 * part + quarter
                mult = wide[TOK * part : TOK * part + TOK]
                value = mixed[level * TOK : (level + 1) * TOK]
                out = out + mult * value
                prods.append((gs * value).astype(BF16))
                parts[level] = (mult * gs).astype(BF16)
            da_ref[...] += mm_nt(jnp.concatenate(prods, axis=0), onehot(chunk, quarter))
        y_ref[:, cols] = out
        agst = jnp.concatenate(parts, axis=0)
        dxd = mm_tn(kst, agst)
        dk_ref[...] += mm_nt(agst, xd)
        ones = onehot(chunk, 0)
        q_ref[...] += mm_nt((dxd * xs).astype(BF16), ones)
        dx_ref[:, cols] = dxd * lifted + gains * gs
        skrow = jnp.sum(xs * gs, axis=0, keepdims=True)
        sk_ref[...] += lax.dot_general(
            jnp.broadcast_to(skrow, (8, CHUNK)), ones.astype(F32), (((1,), (1,)), ((), ())),
            precision=HIGHEST, preferred_element_type=F32,
        )

    dscore = jnp.zeros((TOK, TOK), F32)
    for level in range(INTRA):
        dscore = dscore + jnp.where(mask_of(level), dk_ref[level * TOK : (level + 1) * TOK], 0.0)
    dscore = dscore.astype(BF16)
    dc_ref[...] = mm(dscore, bmat)
    db_ref[...] = mm_tn(dscore, cmat)
    dlam = []
    for part in range(2):
        da = da_ref[TOK * part : TOK * part + TOK]
        dlam.append(da * fade)
    w_ref[...] = dlam[0] * lam_ref[:, :128] + dlam[1] * lam_ref[:, 128:256]
    dlogit = (jnp.concatenate(dlam, axis=1) * sig_ref[:, :256]).astype(BF16)
    dl_ref[...] = dlogit
    second = bit_of(place_ref, 0) == 1
    for part in range(FEAT // 128):
        rows = mm_tn(x_ref[:, 128 * part : 128 * part + 128], dlogit)
        for pair in range(64 // ROWS):
            at = part * (64 // ROWS) + pair
            low, high = rows[64 * pair : 64 * pair + ROWS], rows[64 * pair + ROWS : 64 * pair + 64]
            keep, away = jnp.where(second, high, low), jnp.where(second, low, high)
            for quarter in range(4):
                top, left = ROWS // 2 * (quarter % 2), 128 * (quarter // 2)
                keep_ref[quarter, at] = keep[top : top + ROWS // 2, left : left + 128]
                away_ref[quarter, at] = away[top : top + ROWS // 2, left : left + 128]


def spread_level(core_ref, x_ref, g_ref, c_ref, lam, fade_ref, y_ref, out_ref, dcs_ref, da_ref, levels, picked):
    cmat = c_ref[...]
    far = split2(lam * fade_ref[...])
    da_ref[...] = jnp.zeros_like(da_ref)
    core = core_ref[0]

    def step(local, chunk, mine):
        cols = at_chunk(chunk)
        gs = g_ref[:, cols].astype(F32)
        carried = jnp.concatenate([v.astype(BF16) for v in picked(chunk, local, mine)], axis=1)
        mixed = mm(cmat, carried)
        out = y_ref[:, cols]
        parts = []
        for quarter in range(levels):
            ones = onehot(chunk, quarter, 256)
            mult = mm(far, ones)
            value = mixed[:, CHUNK * quarter : CHUNK * quarter + CHUNK]
            out = out + mult * value
            da_ref[...] += mm_nt((gs * value).astype(BF16), ones[:128])
            parts.append((mult * gs).astype(BF16))
        out_ref[:, cols] = out.astype(out_ref.dtype)
        dcs_ref[...] += mm_nt(jnp.concatenate(parts, axis=1), carried)

    @pl.loop(0, CHUNKS // 2, unroll=CHUNKS // 2)
    def _(local):
        step(local, local + core * (CHUNKS // 2), True)

    @pl.loop(0, CHUNKS // 2, unroll=CHUNKS // 2)
    def _(local):
        step(local, local + (1 - core) * (CHUNKS // 2), False)

    return da_ref[...] * fade_ref[...]


def far_kernel(
    core_ref, x_ref, g_ref, c_ref, lam_ref, sig_ref, fade_ref, y_ref, dc_ref,
    first_ref, m1_ref, m2_ref, m3_ref, other_ref, _after_ref,
    out_ref, dcs_ref, dl_ref, w_ref,
    da_ref,
):
    lam = lam_ref[:, 256:384]
    dcs_ref[...] = dc_ref[...]

    def picked(chunk, local, mine):
        values = [first_ref[2 * chunk + half] for half in range(2)]
        for span, ref in enumerate((m1_ref, m2_ref, m3_ref)):
            for half in range(2):
                if mine:
                    values.append(ref[2 * local + half])
                else:
                    values.append(other_ref[span * (PAIRS // 2) + 2 * local + half])
        return values

    dlam = spread_level(
        core_ref, x_ref, g_ref, c_ref, lam, fade_ref, y_ref, out_ref, dcs_ref, da_ref, 4, picked
    )
    w_ref[...] = dlam * lam
    dl_ref[...] = (dlam * sig_ref[:, 256:384]).astype(BF16)


def line_kernel(
    core_ref, x_ref, g_ref, c_ref, lam_ref, sig_ref, fade_ref, y_ref, dc_ref, dl1_ref,
    m4_ref, m5_ref, other_ref, _after_ref,
    out_ref, dcout_ref, dl_ref, keep_ref, away_ref, w_ref,
    da_ref, dcs_ref,
):
    lam = lam_ref[:, 384:512]
    dcs_ref[...] = dc_ref[...]

    def picked(chunk, local, mine):
        values = []
        for span, ref in enumerate((m4_ref, m5_ref)):
            for half in range(2):
                if mine:
                    values.append(ref[2 * local + half])
                else:
                    values.append(other_ref[span * (PAIRS // 2) + 2 * local + half])
        return values

    dlam = spread_level(
        core_ref, x_ref, g_ref, c_ref, lam, fade_ref, y_ref, out_ref, dcs_ref, da_ref, 2, picked
    )
    dcout_ref[...] = dcs_ref[...].astype(BF16)
    w_ref[...] = dlam * lam
    dlogit = (dlam * sig_ref[:, 384:512]).astype(BF16)
    dl_ref[...] = dlogit
    both = jnp.concatenate([dl1_ref[...], dlogit], axis=1)
    lane = lax.broadcasted_iota(jnp.int32, (ROWS // 2, 128), 1)
    second = core_ref[0] == 1
    for part in range(FEAT // 128):
        rows = mm_tn(x_ref[:, 128 * part : 128 * part + 128], both)
        turned = pltpu.roll(rows[:, 128:], 64, 1)

        def packed(top):
            mid = top + ROWS // 2
            return jnp.where(lane < 64, rows[top:mid, 128:], turned[mid : mid + ROWS // 2])

        for pair in range(64 // ROWS):
            at = part * (64 // ROWS) + pair
            low, high = rows[64 * pair : 64 * pair + ROWS, :128], rows[64 * pair + ROWS : 64 * pair + 64, :128]
            keep_ref[at, :ROWS], away_ref[at, :ROWS] = jnp.where(second, high, low), jnp.where(second, low, high)
            low, high = packed(64 * pair), packed(64 * pair + ROWS)
            keep_ref[at, ROWS:], away_ref[at, ROWS:] = jnp.where(second, high, low), jnp.where(second, low, high)


def last_kernel(
    place_ref, x_ref, b_ref, dt_ref, cum_ref, rate_ref, w_ref, mine_ref, came_ref, lag_ref, fresh_ref, dx_ref, db_ref,
    dl0_ref, dl1_ref, dl2_ref, q_ref, w0_ref, w1_ref, w2_ref,
    dxout_ref, dbout_ref, ddt_ref, rate_out_ref,
    dbs_ref, q2_ref,
):
    bmat = b_ref[...]
    cum = cum_ref[...]
    dt4 = dt_ref[...]
    left = jnp.exp(cum - cum[TOK - 1 : TOK])
    held = split2(left * dt4)
    dlogit = jnp.concatenate([dl0_ref[...], dl1_ref[...], dl2_ref[...]], axis=1)
    q2_ref[...] = jnp.zeros_like(q2_ref)
    dbs_ref[...] = db_ref[...]

    core = bit_of(place_ref, 0)

    def step(local, chunk, source):
        cols = at_chunk(chunk)
        xs = x_ref[:, cols].astype(F32)
        spread = mm(held, onehot(chunk, 0, 256))
        du = jnp.concatenate(
            [
                (
                    source[2 * local + half] * lag_ref[2 * chunk + half]
                    + came_ref[PAIRS // 2 + 2 * chunk + half] * fresh_ref[0]
                ).astype(BF16)
                for half in range(2)
            ],
            axis=1,
        )
        dxs = mm(bmat, du)
        q2_ref[...] += mm_nt((dxs * xs).astype(BF16), onehot(chunk, 0))
        dbs_ref[...] += mm_nt((xs * spread).astype(BF16), du)
        dx = dx_ref[:, cols] + dxs * spread + mm(dlogit, w_ref[:512, cols])
        dxout_ref[:, cols] = dx.astype(BF16)

    @pl.loop(0, CHUNKS // 2, unroll=CHUNKS // 2)
    def _(local):
        step(local, local + core * (CHUNKS // 2), mine_ref)

    @pl.loop(0, CHUNKS // 2, unroll=CHUNKS // 2)
    def _(local):
        step(local, local + (1 - core) * (CHUNKS // 2), came_ref)

    dbout_ref[...] = dbs_ref[...].astype(BF16)
    q2 = q2_ref[...]
    q1 = q_ref[...]
    lift = jnp.exp(cum)
    gathered = w0_ref[...] + w1_ref[...] + w2_ref[...]
    queried = gathered + pltpu.roll(gathered, 32, 1)
    queried = queried + pltpu.roll(queried, 64, 1)
    keyed2 = q2 * left * dt4
    dcum = q1 * lift * dt4 + keyed2 - queried
    dlog = lax.dot_general(
        sums_down(), dcum, (((0,), (0,)), ((), ())), precision=HIGHEST, preferred_element_type=F32
    )
    dlog = dlog - jnp.sum(keyed2, axis=0, keepdims=True)
    ddt_ref[...] = (four(rate_ref[...]) * dlog + q1 * lift + q2 * left).T[:HEADS]
    rate_out_ref[...] = jnp.sum(dt4 * dlog, axis=0, keepdims=True)


def bit_of(place_ref, span):
    return jnp.right_shift(place_ref[0], span) % 2


def half_of(rows_ref, index, place_ref):
    return rows_ref[index, pl.ds(pl.multiple_of(bit_of(place_ref, 0) * HALF, HALF), HALF), :]


def up_step(span, place_ref, held_ref, other_ref, rows_ref, lower_ref, next_ref):
    upper = bit_of(place_ref, span) == 1
    rows = half_of(rows_ref, span - 1, place_ref)
    for pair in range(HALF):
        mine, other = held_ref[pair], other_ref[pair]
        lower = jnp.where(upper, other, mine)
        lower_ref[pair] = lower
        next_ref[pair] = lower * rows[pair : pair + 1] + jnp.where(upper, mine, other)


def level_of(span, place_ref, own_ref, came_ref, rows_own_ref, rows_there_ref):
    rows_own = half_of(rows_own_ref, span - 1, place_ref)
    rows_there = half_of(rows_there_ref, span - 1, place_ref)

    def piece(pair):
        return own_ref[0, pair] * rows_own[pair : pair + 1] + came_ref[0, pair] * rows_there[pair : pair + 1]

    return piece


def down_step(span, place_ref, grad, piece, rows_ref, send_ref, keep_ref, crossed_ref=None, lower_ref=None):
    upper = bit_of(place_ref, span) == 1
    rows = half_of(rows_ref, span - 1, place_ref)
    for pair in range(HALF):
        here = grad(pair)
        faded = here * rows[pair : pair + 1]
        send_ref[pair] = jnp.where(upper, faded + piece(pair), here)
        keep_ref[pair] = jnp.where(upper, here, faded)
        if crossed_ref is not None:
            crossed_ref[pair : pair + 1] = jnp.sum(lower_ref[pair] * faded, axis=0, keepdims=True)


def halve(bit, keep_ref, came_ref, keep_out_ref, away_out_ref):
    half = keep_out_ref.shape[0]
    for block in range(half):
        stay, go = bit * half + block, (1 - bit) * half + block
        keep_out_ref[block] = keep_ref[stay] + came_ref[stay]
        away_out_ref[block] = keep_ref[go] + came_ref[go]


def note_kernel(place_ref, c0_ref, c1_ref, c2_ref, c3_ref, c4_ref, far_ref, line_ref, up_ref, in_ref, on_ref, rate_ref, skip_ref, out_ref):
    core = bit_of(place_ref, 0)
    lane = lax.broadcasted_iota(jnp.int32, (128, HEADS), 0)
    side = lax.broadcasted_iota(jnp.int32, (128, HEADS), 1) % 2
    gather = jnp.where(side == jnp.right_shift(lane, 6), 1.0, 0.0).astype(F32)
    pair = lax.broadcasted_iota(jnp.int32, (HALF, HEADS), 0) + HALF * core
    head = lax.broadcasted_iota(jnp.int32, (HALF, HEADS), 1)
    keyed = []
    for ref in (c0_ref, c1_ref, c2_ref, c3_ref, c4_ref):
        sums = lax.dot_general(
            ref[...], gather, (((1,), (0,)), ((), ())), precision=HIGHEST, preferred_element_type=F32
        )
        keyed.append(jnp.sum(jnp.where(jnp.right_shift(head, 1) == pair, sums, 0.0), axis=0, keepdims=True))
    wide = jnp.sum(far_ref[...], axis=0, keepdims=True), jnp.sum(line_ref[...], axis=0, keepdims=True)
    queried = []
    for span in range(SPANS):
        at = 32 * (span % 4)
        queried.append(wide[span // 4][:, at : at + 32] * on_ref[span : span + 1])
    inside = jnp.zeros((1, HEADS), F32)
    for span in range(SPANS):
        inside = inside + in_ref[span : span + 1] * queried[span]
        if span < SPANS - 1:
            inside = inside + up_ref[span : span + 1] * keyed[span]
    none = jnp.zeros((1, HEADS), F32)
    rows = queried + keyed + [none, rate_ref[:, :HEADS] - inside, skip_ref[0:1, :HEADS], none, none]
    for row in range(4):
        out_ref[row : row + 1] = jnp.concatenate(rows[4 * row : 4 * row + 4], axis=1)


def between_kernel(place_ref, ddt_ref, on_ref, rate_ref, *refs):
    told, kept, out_ref = refs[:SPANS], refs[SPANS : 2 * SPANS], refs[2 * SPANS]

    def row(ref, index):
        return ref[index // 4 : index // 4 + 1, 32 * (index % 4) : 32 * (index % 4) + 32]

    between = jnp.zeros((1, HEADS), F32)
    for step in range(SPANS):
        first = bit_of(place_ref, step) == 0
        for span in range(step + 1, SPANS):
            between = between + jnp.where(first, on_ref[span : span + 1] * row(told[step], span), 0.0)
        between = between + on_ref[step : step + 1] * row(kept[step], SPANS + step)
    line = lax.broadcasted_iota(jnp.int32, (HEADS, HEADS), 0)
    head = lax.broadcasted_iota(jnp.int32, (HEADS, HEADS), 1)
    column = jnp.sum(jnp.where(line == head, between * rate_ref[...], 0.0), axis=1, keepdims=True)
    out_ref[...] = ddt_ref[...] - column


def rest_kernel(place_ref, keep_ref, came_ref, _after_ref, keep_out_ref, away_out_ref):
    halve(bit_of(place_ref, 4), keep_ref, came_ref, keep_out_ref, away_out_ref)


def step1_kernel(place_ref, rows_ref, rows_own_ref, rows_there_ref, held_ref, other_ref, own_ref, came_ref, lower_ref, next_ref, send_ref):
    up_step(1, place_ref, held_ref, other_ref, rows_ref, lower_ref, next_ref)
    piece = level_of(5, place_ref, own_ref, came_ref, rows_own_ref, rows_there_ref)
    for pair in range(HALF):
        send_ref[pair] = piece(pair)


def step2_kernel(place_ref, rows_ref, rows_own_ref, rows_there_ref, held_ref, other_ref, own_ref, came_ref, back_ref, near_ref, lower_ref, next_ref, send_ref, keep_ref, near_away_ref):
    near_away_ref[...] = near_ref[...]
    up_step(2, place_ref, held_ref, other_ref, rows_ref, lower_ref, next_ref)
    piece = level_of(4, place_ref, own_ref, came_ref, rows_own_ref, rows_there_ref)
    down_step(4, place_ref, lambda pair: back_ref[pair], piece, rows_ref, send_ref, keep_ref)


def step3_kernel(place_ref, rows_ref, rows_own_ref, rows_there_ref, held_ref, other_ref, own_ref, came_ref, kept_ref, back_ref, near_ref, near_came_ref, level1_ref, level2_ref, lower_ref, next_ref, send_ref, keep_ref, crossed_ref, near_keep_ref, near_away_ref, levels_ref, part_ref):
    halve(place_ref[1] // 2, near_ref, near_came_ref, near_keep_ref, near_away_ref)
    for index, level_ref in enumerate((level1_ref, level2_ref, other_ref)):
        for pair in range(HALF):
            levels_ref[index * HALF + pair] = level_ref[pair]
    up_step(3, place_ref, held_ref, other_ref, rows_ref, lower_ref, next_ref)
    upper = bit_of(place_ref, 4) == 1
    rows = half_of(rows_ref, 3, place_ref)
    for pair in range(HALF):
        part_ref[pair] = jnp.where(upper, next_ref[pair], next_ref[pair] * rows[pair : pair + 1])
    piece = level_of(3, place_ref, own_ref, came_ref, rows_own_ref, rows_there_ref)
    down_step(3, place_ref, lambda pair: kept_ref[pair] + back_ref[pair], piece, rows_ref, send_ref, keep_ref, crossed_ref, lower_ref)


def step4_kernel(place_ref, rows_ref, rows_own_ref, rows_there_ref, held_ref, other_ref, direct_ref, cross_ref, own_ref, came_ref, kept_ref, back_ref, first_ref, lower2_ref, near_ref, near_came_ref, _after_ref, level_ref, both_ref, send_ref, keep_ref, crossed_ref, crossed4_ref, near_keep_ref, near_away_ref):
    halve(place_ref[1] % 2, near_ref, near_came_ref, near_keep_ref, near_away_ref)
    upper = bit_of(place_ref, 4) == 1
    rows = half_of(rows_ref, 3, place_ref)
    for pair in range(HALF):
        mine, other = held_ref[pair], other_ref[pair]
        faded = jnp.where(upper, other, mine) * rows[pair : pair + 1]
        crossed4_ref[pair : pair + 1] = jnp.sum(faded * first_ref[pair], axis=0, keepdims=True)
        whole = direct_ref[pair] + cross_ref[pair]
        level_ref[pair] = whole
        both_ref[pair] = other
        both_ref[HALF + pair] = whole
    piece = level_of(2, place_ref, own_ref, came_ref, rows_own_ref, rows_there_ref)
    down_step(2, place_ref, lambda pair: kept_ref[pair] + back_ref[pair], piece, rows_ref, send_ref, keep_ref, crossed_ref, lower2_ref)


def step5_kernel(place_ref, rows_ref, rows_own_ref, rows_there_ref, own_ref, came_ref, kept_ref, back_ref, lower1_ref, near_ref, near_came_ref, far_ref, send_ref, keep_ref, crossed_ref, near_keep_ref, near_away_ref, far_away_ref):
    halve(bit_of(place_ref, 5), near_ref, near_came_ref, near_keep_ref, near_away_ref)
    far_away_ref[...] = far_ref[...]
    piece = level_of(1, place_ref, own_ref, came_ref, rows_own_ref, rows_there_ref)
    down_step(1, place_ref, lambda pair: kept_ref[pair] + back_ref[pair], piece, rows_ref, send_ref, keep_ref, crossed_ref, lower1_ref)


def step6_kernel(place_ref, row_ref, kept_ref, back_ref, lower0_ref, cot_ref, near_ref, near_came_ref, far_ref, far_came_ref, send_ref, crossed_ref, near_out_ref, far_keep_ref, far_away_ref):
    near_out_ref[...] = near_ref[...] + near_came_ref[...]
    halve(bit_of(place_ref, 5), far_ref, far_came_ref, far_keep_ref, far_away_ref)
    rows = row_ref[pl.ds(pl.multiple_of(bit_of(place_ref, 0) * HALF, HALF), HALF), :]
    upper = bit_of(place_ref, 0) == 1
    for pair in range(HALF):
        grad = kept_ref[pair] + back_ref[pair]
        send_ref[pair] = grad
        crossed_ref[pair : pair + 1] = jnp.sum(lower0_ref[pair] * rows[pair : pair + 1] * grad, axis=0, keepdims=True)
    for pair in range(PAIRS):
        send_ref[HALF + pair] = jnp.where(upper, cot_ref[pair], 0.0)


VMEM_LIMIT = 56 * 1024 * 1024
FOLD = ROWS + ROWS // 2


def call(kernel, outs, scratch=(), flops=0, moved=1 << 20, specs=None):
    extra = {} if specs is None else {"in_specs": specs}
    return pl.pallas_call(
        kernel,
        out_shape=outs,
        scratch_shapes=list(scratch),
        compiler_params=pltpu.CompilerParams(vmem_limit_bytes=VMEM_LIMIT),
        cost_estimate=pl.CostEstimate(flops=flops, bytes_accessed=moved, transcendentals=0),
        **extra,
    )


def one_step(kernel, outs, *operands):
    specs, arrays = [pl.BlockSpec(memory_space=pltpu.SMEM)], [operands[0]]
    for operand in operands[1:]:
        if not isinstance(operand, tuple):
            arrays.append(operand)
            specs.append(pl.BlockSpec(operand.shape, lambda _, rank=operand.ndim: (0,) * rank))
        elif operand[0] == "slab":
            arrays.append(operand[2])
            specs.append(pl.BlockSpec((1,) + operand[2].shape[1:], lambda _, at=operand[1]: (at, 0, 0, 0)))
        else:
            arrays.append(operand[1])
            specs.append(pl.BlockSpec(memory_space=pl.ANY))
    return pl.pallas_call(
        kernel,
        grid=(1,),
        out_shape=tuple(outs),
        in_specs=specs,
        out_specs=tuple(pl.BlockSpec(out.shape, lambda _, rank=len(out.shape): (0,) * rank) for out in outs),
        compiler_params=pltpu.CompilerParams(vmem_limit_bytes=VMEM_LIMIT),
        cost_estimate=pl.CostEstimate(flops=1 << 22, bytes_accessed=4 << 20, transcendentals=0),
    )(*arrays)


def shaped(*dims, dtype=F32):
    return jax.ShapeDtypeStruct(dims, dtype)


def swap(value, bit, only=None, more=0):
    pairs = []
    for source in range(BLOCKS):
        if only is None or (source >> bit) % 2 == only:
            pairs.append((source, source ^ (1 << bit) ^ more))
    return lax.ppermute(value, "ctx", pairs)


def turn(value, bit):
    count = lax.axis_size("dp")
    return lax.ppermute(value, "dp", [(source, source ^ (1 << bit)) for source in range(count)])


def part(value, start, count):
    return lax.dynamic_slice_in_dim(value, start, count, 0)


def per_device(inputs, matrix_b, matrix_c, steps_dt, decay_rate, skip_gain, level_weight, grad_out):
    xs, bs, cs, gs = inputs[0], matrix_b[0], matrix_c[0], grad_out[0]
    turned_dt, turned_w = steps_dt[0].T, level_weight.T
    place = lax.axis_index("ctx")
    core = place % 2
    bits = [jnp.right_shift(place, span) % 2 for span in range(SPANS)]
    rate = decay_rate.reshape(1, HEADS)
    core_here = core.astype(jnp.int32).reshape(1)
    vmem = pl.BlockSpec(memory_space=pltpu.VMEM)
    smem = pl.BlockSpec(memory_space=pltpu.SMEM)
    anywhere = pl.BlockSpec(memory_space=pl.ANY)

    def choose(bit, low, high):
        return jnp.where(bits[bit] == 1, high, low)

    def mine_of(value):
        return part(value, core * HALF, HALF)

    def yours_of(value):
        return part(value, (1 - core) * HALF, HALF)

    own_sum = jnp.sum(turned_dt, axis=1)[None]
    other = swap(own_sum, 0)
    sum_up = [choose(0, other, own_sum)]
    sum_in = [jnp.zeros_like(own_sum), choose(0, jnp.zeros_like(other), other)]
    there = choose(0, own_sum, -other)
    states, cum, dt4, row_first = call(
        state_kernel,
        (shaped(PAIRS, NST, 128), shaped(TOK, 128), shaped(TOK, 128), shaped(PAIRS, 128)),
        flops=2 * TOK * FEAT * 2 * NST,
        moved=2 << 20,
    )(xs, bs, turned_dt, rate, sum_up[0])
    first = swap(states, 0)
    group_sum = own_sum + other
    for span in range(1, SPANS - 1):
        other = swap(group_sum, span)
        sum_up.append(choose(span, other, group_sum))
        sum_in.append(sum_in[-1] + choose(span, jnp.zeros_like(other), other))
        if span in (2, 3):
            beside = (cum, cum) if span == 2 else (lam, first)
            group_sum, row_first = call(
                sum_kernel,
                (shaped(1, HEADS), shaped(PAIRS, 128)),
                specs=[vmem] * 3 + [anywhere] * 2,
                moved=1024,
            )(group_sum, other, row_first, *beside)
        else:
            group_sum = group_sum + other
        if span == 2:
            cot0, own, away, lam, sig = call(
                cot_kernel,
                (
                    shaped(PAIRS, NST, 128),
                    shaped(SPANS - 1, HALF, NST, 128),
                    shaped(SPANS - 1, HALF, NST, 128),
                    shaped(TOK, 512),
                    shaped(TOK, 512),
                ),
                flops=2 * TOK * FEAT * (512 + 10 * NST),
                moved=10 << 20,
                specs=[smem] + [vmem] * 5 + [anywhere],
            )(core_here, xs, gs, cs, cum, turned_w, group_sum)
    on = jnp.stack(bits).astype(F32)[:, None]
    sum_up, sum_in = jnp.concatenate(sum_up), jnp.concatenate(sum_in)
    on_rows = jnp.broadcast_to(on, (SPANS, HEADS))
    rows_up, rows_own, rows_there, fade_in = call(
        rows_kernel,
        (
            shaped(SPANS - 2, PAIRS, 128),
            shaped(SPANS - 1, PAIRS, 128),
            shaped(SPANS - 1, PAIRS, 128),
            shaped(SPANS, HEADS),
        ),
        moved=1024,
    )(sum_up, sum_in, there, on_rows, rate)
    place_here = jnp.stack([place, lax.axis_index("dp")]).astype(jnp.int32)
    rows = (rows_up, rows_own, rows_there)
    slab = shaped(HALF, NST, 128)
    crossed = shaped(HALF, 128)

    mine, yours = mine_of(states), mine_of(first)
    row = mine_of(row_first)[:, None]
    lower0 = choose(0, mine, yours)
    held0 = lower0 * row + choose(0, yours, mine)
    came = swap(away, 0)
    level1 = swap(held0, 1)
    lower1, held1, send = one_step(
        step1_kernel, [slab] * 3, place_here, *rows, held0, level1, ("slab", 4, own), ("slab", 4, came)
    )
    fade_t = jnp.exp(-cum)
    fade_far = fade_t[None] * jnp.concatenate([fade_in, jnp.zeros((2, HEADS), F32)]).reshape(2, 1, 128)
    level2, back4 = swap(held1, 2), swap(send, 5, 1)
    y_near, dx_near, db_near, dc_near, dl_near, near_keep, near_away, q_near, w_near, skip_sum = call(
        near_kernel,
        (
            shaped(TOK, FEAT),
            shaped(TOK, FEAT),
            shaped(TOK, NST),
            shaped(TOK, NST),
            shaped(TOK, 256, dtype=BF16),
            shaped(4, BLOCKS // 2, ROWS // 2, 128),
            shaped(4, BLOCKS // 2, ROWS // 2, 128),
            shaped(TOK, 128),
            shaped(TOK, 128),
            shaped(8, 128),
        ),
        scratch=(
            pltpu.VMEM((INTRA * TOK, TOK), BF16),
            pltpu.VMEM((INTRA * TOK, TOK), F32),
            pltpu.VMEM((2 * TOK, 128), F32),
        ),
        flops=2 * TOK * FEAT * (5 * INTRA * NST),
        moved=12 << 20,
        specs=[smem] + [vmem] * 9 + [anywhere],
    )(place_here, xs, gs, bs, cs, dt4, skip_gain.reshape(1, HEADS), lam, sig, cum, send)
    lower2, held2, send, keep, near_away = one_step(
        step2_kernel, [slab] * 4 + [shaped(4, BLOCKS // 2, ROWS // 2, 128)], place_here, *rows, held1, level2,
        ("slab", 3, own), ("slab", 3, came), back4, near_away,
    )
    level3, back, near_came = swap(held2, 3), swap(send, 4), swap(near_away, 0)
    _, held3, send, keep, crossed3, near_keep, near_away, levels, part3 = one_step(
        step3_kernel,
        [slab] * 4 + [crossed] + [shaped(2, BLOCKS // 2, ROWS // 2, 128)] * 2 + [shaped(3 * HALF, NST, 128), slab],
        place_here, *rows, held2, level3, ("slab", 2, own), ("slab", 2, came), keep, back,
        near_keep, near_came, level1, level2,
    )
    level4, back, near_came = swap(held3, 4), swap(send, 3), turn(near_away, 1)
    direct, cross = swap(part3, 5, 0), swap(part3, 5, 0, 16)
    across_near = swap(levels, 0)
    y_far, dc_far, dl_far, w_far = call(
        far_kernel,
        (shaped(TOK, FEAT), shaped(TOK, NST), shaped(TOK, 128, dtype=BF16), shaped(TOK, 128)),
        scratch=[pltpu.VMEM((TOK, 128), F32)],
        flops=2 * TOK * FEAT * 16 * NST,
        moved=10 << 20,
        specs=[smem] + [vmem] * 13 + [anywhere],
    )(
        core_here, xs, gs, cs, lam, sig, fade_far[0], y_near, dc_near,
        first, level1, level2, level3, across_near, send,
    )
    level5, both, send, keep, crossed2, crossed4, near_keep, near_away = one_step(
        step4_kernel, [slab, shaped(PAIRS, NST, 128)] + [slab] * 2 + [crossed] * 2 + [shaped(1, BLOCKS // 2, ROWS // 2, 128)] * 2,
        place_here, *rows, held3, level4, direct, cross, ("slab", 1, own), ("slab", 1, came), keep, back,
        back4, lower2, near_keep, near_came, ("after", w_far),
    )
    back, across_far, near_came = swap(send, 2), swap(both, 0), turn(near_away, 0)[0]
    output, grad_c, dl_line, far_keep, far_away, w_line = call(
        line_kernel,
        (
            shaped(TOK, FEAT, dtype=BF16),
            shaped(TOK, NST, dtype=BF16),
            shaped(TOK, 128, dtype=BF16),
            shaped(BLOCKS // 2, FOLD, 128),
            shaped(BLOCKS // 2, FOLD, 128),
            shaped(TOK, 128),
        ),
        scratch=[pltpu.VMEM((TOK, 128), F32), pltpu.VMEM((TOK, NST), F32)],
        flops=2 * TOK * FEAT * 10 * NST,
        moved=6 << 20,
        specs=[smem] + [vmem] * 12 + [anywhere],
    )(
        core_here, xs, gs, cs, lam, sig, fade_far[1], y_far, dc_far, dl_far,
        level4, level5, across_far, send,
    )
    send, keep, crossed1, near_keep, near_away, far_away = one_step(
        step5_kernel,
        [slab] * 2 + [crossed] + [shaped(16, ROWS // 2, 128)] * 2 + [shaped(BLOCKS // 2, FOLD, 128)],
        place_here, *rows, ("slab", 0, own), ("slab", 0, came), keep, back, lower1,
        near_keep[0], near_came, far_away,
    )
    back, near_came, far_came = swap(send, 1), swap(near_away, 5), swap(far_away, 0)
    going, crossed0, near_rows, far_keep, far_away = one_step(
        step6_kernel,
        [shaped(HALF + PAIRS, NST, 128), crossed, shaped(16, ROWS // 2, 128)] + [shaped(16, FOLD, 128)] * 2,
        place_here, row_first, keep, back, lower0, cot0, near_keep, near_came, far_keep, far_came,
    )
    last_came, far_came = swap(going, 0), swap(far_away, 5)
    lag = choose(0, row_first, jnp.ones_like(row_first))[:, None]
    fresh = choose(0, jnp.ones((1, 1, 128), F32), jnp.zeros((1, 1, 128), F32))
    grad_inputs, grad_b, ddt, rate_row = call(
        last_kernel,
        (
            shaped(TOK, FEAT, dtype=BF16),
            shaped(TOK, NST, dtype=BF16),
            shaped(HEADS, TOK),
            shaped(1, 128),
        ),
        scratch=[pltpu.VMEM((TOK, NST), F32), pltpu.VMEM((TOK, 128), F32)],
        flops=2 * TOK * FEAT * 8 * NST,
        moved=10 << 20,
        specs=[smem] + [vmem] * 19,
    )(
        place_here, xs, bs, dt4, cum, rate, turned_w, going, last_came, lag, fresh,
        dx_near, db_near, dl_near, dl_far, dl_line, q_near, w_near, w_far, w_line,
    )
    far_keep, far_away = one_step(
        rest_kernel, [shaped(8, FOLD, 128)] * 2, place_here, far_keep, far_came, ("after", rate_row)
    )
    far_came = swap(far_away, 4)

    (extra,) = one_step(
        note_kernel, [shaped(4, 128)], place_here, crossed0, crossed1, crossed2, crossed3, crossed4,
        w_far, w_line, sum_up, sum_in, on_rows, rate_row, skip_sum,
    )
    far_rows = None
    told, kept = [], []
    for step in range(SPANS):
        sent, keep = [extra], []
        if step == 1:
            far_rows = far_keep + far_came
        if 1 <= step <= 4:
            for rows in (far_rows, near_rows) if step <= 3 else (near_rows,):
                split = rows.reshape(rows.shape[0] // 2, 2, rows.shape[1], 128)
                keep.append(lax.dynamic_index_in_dim(split, bits[step], 1, keepdims=False))
                sent.append(lax.dynamic_index_in_dim(split, 1 - bits[step], 1, keepdims=False).reshape(-1, 128))
        came = swap(jnp.concatenate(sent), step)
        at = 4
        added = []
        for rows in keep:
            size = rows.shape[0] * rows.shape[1]
            added.append(rows + came[at : at + size].reshape(rows.shape))
            at += size
        if added:
            near_rows = added[-1]
            far_rows = added[0] if step <= 3 else far_rows
        told.append(came[:4])
        extra = extra + came[:4]
        kept.append(extra)
    total, near_rows = jnp.concatenate([extra, far_rows[0]]), near_rows[0]
    at_y = lax.axis_index("dp")
    for step in range(2):
        other = turn(jnp.concatenate([total, near_rows]), step)
        second = (at_y // (step + 1)) % 2 == 1
        other_rows = other[4 + FOLD :]
        near_rows = jnp.where(
            second, jnp.concatenate([other_rows, near_rows]), jnp.concatenate([near_rows, other_rows])
        )
        total = total + other[: 4 + FOLD]
    ends = total[3].reshape(4, HEADS)
    rows = total[4:]
    packed = rows[ROWS:FOLD]
    grad_level = jnp.concatenate(
        [
            near_rows[:ROWS],
            near_rows[ROWS:],
            rows[:ROWS],
            jnp.concatenate([packed[:, :64], packed[:, 64:]], axis=0),
            jnp.zeros((ROWS, level_weight.shape[1] - 448), F32),
        ],
        axis=1,
    )
    (grad_dt,) = one_step(between_kernel, [shaped(HEADS, TOK)], place_here, ddt, on_rows, rate, *told, *kept)
    grad_dt = grad_dt.T[None]
    return (output[None], grad_inputs[None], grad_b[None], grad_c[None], grad_dt, ends[0], ends[1], grad_level)


def solution(mesh):
    split = P("dp", "ctx", None)
    return jax.shard_map(
        per_device,
        mesh=mesh,
        in_specs=(split, split, split, split, P(), P(), P(), split),
        out_specs=(split, split, split, split, split, P(), P(), P("ctx", None)),
        check_vma=False,
    )
```
